256 devices in a mesh: member: 16 (over x, y), tile: 16 (over z, core).
Axes of the slice: x: 4, y: 4, z: 8, core: 2. Of those that a mesh axis runs over, the one named last changes fastest.
Arguments:
- prior_members: bfloat16 [48, 16, 128, 2048], P('member', None, 'tile'), may hold values from -6 to 6
- measured_reading: float32 [16, 16, 256], P('tile', 'member'), may hold values from -6 to 6
- measure_error_spread: float32 [16, 16, 256], P('tile', 'member'), may hold values from 0.01 to 0.1
- measured_cell_index: int32 [16, 16, 256], P('tile', 'member'), may hold values from 0 to 1023
- active_measure_tally: int32 [16, 16], P('tile', 'member'), may hold values from 32 to 256, as said below
Outputs:
- analysis: bfloat16 [48, 16, 128, 2048], P('member', None, 'tile')
The draws below stay inside these ranges and needn't reach their ends.
Inputs may be any that keep to these rules, and one draw needn't show every extreme that they name: `active_measure_tally`: slots from a domain's count on hold values that take no part; in every draw some domain has all 256 slots live.
All inputs are finite; a program needn't handle non-finite values.
Results may differ from the reference program's by a relative error of at most 0.001.
Values may be sent and summed in bfloat16 or wider, within the bound.
No kernel may reach another device: no remote copies, remote signals or barrier semaphores. Data moves between devices by JAX's collectives and lax.ppermute only.
A program may use at most 128 MiB of HBM per device.

```python
import math
import jax
import jax.numpy as jnp
from jax import lax

MEMBER_TOTAL = 48
MODEL_LEVELS = 16
REVISED_LEVELS = 8
OBS_LAYERS = 2
TILE_SPAN_FIRST = 8
TILE_SPAN_SECOND = 128
BLOCK = 4
SLOTS = 256
RADIUS = 8
DOM_X = 16
DOM_Y = 16
MESH_SPAN_FIRST = 128
MESH_SPAN_SECOND = 2048


def draw_active_measure_tally(key, part):
    key = jax.random.fold_in(key, 7)
    first_key, second_key = jax.random.split(key)
    domains = DOM_X * DOM_Y
    counts = jax.random.randint(first_key, (domains,), max(SLOTS // 8, 1), SLOTS + 1)
    chosen = jax.random.randint(second_key, (), 0, domains)
    counts = jnp.where(jnp.arange(domains) == chosen, SLOTS, counts)
    return counts.reshape(DOM_X, DOM_Y).astype(jnp.int32)


def plant(result, own_key, low, largest):
    longest = result.shape.index(max(result.shape))
    spots = []
    for shift in (0, 1):
        where = [jax.random.randint(jax.random.fold_in(own_key, axis), (), 0, length) for axis, length in enumerate(result.shape)]
        where[longest] = (where[longest] + shift) % result.shape[longest]
        spots.append(tuple(where))
    return result.at[spots[0]].set(low).at[spots[1]].set(largest)


def block_scale(key, dims, shards, least, largest):
    gain = 1.0
    for position, blocks in shards:
        draws = jax.random.uniform(jax.random.fold_in(jax.random.fold_in(key, 6), position), (blocks,), jnp.float32, least / len(shards), largest / len(shards))
        gain = gain * jnp.repeat(jnp.exp(draws), dims[position] // blocks).reshape((-1,) + (1,) * (len(dims) - 1 - position))
    return gain


def scatter_about(stream_key, extent, deviation, bound, shards=(), kind=jnp.bfloat16):
    entries = deviation * jax.random.normal(stream_key, extent, jnp.float32)
    if shards:
        entries = entries * block_scale(stream_key, extent, shards, -0.22, 0.18)
    return jnp.clip(entries, -bound, bound).astype(kind)


def setup_inputs(seed: int = 0) -> dict:
    streams_of = jax.random.split(jax.random.key(seed), 6)
    prior_members = scatter_about(streams_of[0], (MEMBER_TOTAL, MODEL_LEVELS, MESH_SPAN_FIRST, MESH_SPAN_SECOND), 1.0, 6.0, ((0, 16), (2, 16)))
    measured_reading = scatter_about(streams_of[1], (DOM_X, DOM_Y, SLOTS), 1.0, 6.0, ((0, 16), (1, 16)), jnp.float32)
    measure_error_spread = jnp.clip(jnp.exp(math.log(0.1) - 2.3025851 * jax.random.uniform(streams_of[2], (DOM_X, DOM_Y, SLOTS), jnp.float32) ** block_scale(streams_of[2], (DOM_X, DOM_Y, SLOTS), ((0, 16), (1, 16)), -0.2, 0.2)), 0.01, 0.1)
    measured_cell_index = plant(jax.random.randint(streams_of[3], (DOM_X, DOM_Y, SLOTS), 0, TILE_SPAN_FIRST * TILE_SPAN_SECOND), jax.random.fold_in(streams_of[3], 1), 0, (TILE_SPAN_FIRST * TILE_SPAN_SECOND) - 1).astype(jnp.int32)
    active_measure_tally = draw_active_measure_tally(jax.random.fold_in(streams_of[5], 71), 0)
    return {"prior_members": prior_members, "measured_reading": measured_reading, "measure_error_spread": measure_error_spread, "measured_cell_index": measured_cell_index, "active_measure_tally": active_measure_tally}


precise = lax.Precision.HIGHEST

def observe(model_levels_stack, cell_ids, values, variances, live_count):
    members = model_levels_stack.shape[0]
    surface = lax.optimization_barrier(jnp.mean(model_levels_stack[:, :OBS_LAYERS].astype(jnp.float32), axis=1)).reshape(members, -1)
    sampled = jnp.take(surface, cell_ids, axis=1)
    obs_mean = lax.optimization_barrier(jnp.mean(sampled, axis=0))
    usable = (jnp.arange(SLOTS, dtype=jnp.int32) < live_count).astype(jnp.float32)
    pos_x = (cell_ids // TILE_SPAN_SECOND).astype(jnp.float32)
    pos_y = (cell_ids % TILE_SPAN_SECOND).astype(jnp.float32)
    return jnp.concatenate([sampled - obs_mean[None], (values - obs_mean)[None], (usable / variances)[None], pos_x[None], pos_y[None]], axis=0)

def analyse(neighbours, model_levels_stack):
    members = model_levels_stack.shape[0]
    rows_x = model_levels_stack.shape[2]
    rows_y = model_levels_stack.shape[3]
    count_x = rows_x // BLOCK
    count_y = rows_y // BLOCK
    radius_sq = float(RADIUS * RADIUS)
    centre_x = jnp.arange(count_x, dtype=jnp.float32) * BLOCK + (BLOCK - 1) / 2.0
    centre_y = jnp.arange(count_y, dtype=jnp.float32) * BLOCK + (BLOCK - 1) / 2.0
    gram_sum = jnp.zeros((count_x * count_y, members * members), jnp.float32)
    drive_sum = jnp.zeros((count_x * count_y, members), jnp.float32)
    for step_x in range(3):
        for step_y in range(3):
            parcel = neighbours[step_x, step_y]
            ens_rows = parcel[:members]
            innovation = parcel[members]
            weight = parcel[members + 1]
            pos_x = parcel[members + 2] + (step_x - 1) * rows_x
            pos_y = parcel[members + 3] + (step_y - 1) * rows_y
            gap_x = pos_x[None, None, :] - centre_x[:, None, None]
            gap_y = pos_y[None, None, :] - centre_y[None, :, None]
            distance = gap_x * gap_x + gap_y * gap_y
            ratio = 1.0 - distance / radius_sq
            tapered = jnp.where(distance < radius_sq, ratio * ratio, 0.0)
            scaled = (tapered * weight[None, None, :]).reshape(count_x * count_y, -1)
            outers = (ens_rows[:, None, :] * ens_rows[None, :, :]).reshape(members * members, -1)
            gram_sum = gram_sum + lax.dot_general(scaled, outers, (((1,), (1,)), ((), ())), precision=precise)
            drive_sum = drive_sum + lax.dot_general(scaled * innovation[None, :], ens_rows, (((1,), (1,)), ((), ())), precision=precise)
    identity = jnp.eye(members, dtype=jnp.float32)
    system = gram_sum.reshape(-1, members, members) + (members - 1.0) * identity[None]
    factor = jnp.linalg.cholesky(system)
    forward = jax.scipy.linalg.solve_triangular(factor, drive_sum[:, :, None], lower=True)
    mean_weight = jax.scipy.linalg.solve_triangular(factor, forward, lower=True, trans=1)[:, :, 0]
    square_root = jax.scipy.linalg.solve_triangular(factor, jnp.broadcast_to(identity, factor.shape), lower=True, trans=1)
    weights = square_root * math.sqrt(members - 1.0) + mean_weight[:, :, None]
    weights = weights.reshape(count_x, count_y, members, members)
    values = model_levels_stack.astype(jnp.float32)
    centre = lax.optimization_barrier(jnp.mean(values, axis=0))
    spread = values - centre[None]
    blocks = spread.reshape(members, model_levels_stack.shape[1], count_x, BLOCK, count_y, BLOCK)
    shifted = jnp.einsum('iuapbq,abij->juapbq', blocks, weights, precision=precise)
    return (centre[None] + shifted.reshape(model_levels_stack.shape)).astype(jnp.bfloat16)

def reference(prior_members, measured_reading, measure_error_spread, measured_cell_index, active_measure_tally):
    domains = DOM_X * DOM_Y

    def slice_fields(number):
        between_tiles = number // DOM_Y
        inside_single_tile = number % DOM_Y
        model_levels_stack = lax.dynamic_slice(prior_members, (jnp.int32(0), jnp.int32(0), (between_tiles * TILE_SPAN_FIRST).astype(jnp.int32), (inside_single_tile * TILE_SPAN_SECOND).astype(jnp.int32)), (MEMBER_TOTAL, REVISED_LEVELS, TILE_SPAN_FIRST, TILE_SPAN_SECOND))
        return (between_tiles, inside_single_tile, model_levels_stack)

    def observe_one(number):
        between_tiles, inside_single_tile, model_levels_stack = slice_fields(number)
        return observe(model_levels_stack, measured_cell_index[between_tiles, inside_single_tile], measured_reading[between_tiles, inside_single_tile], measure_error_spread[between_tiles, inside_single_tile], active_measure_tally[between_tiles, inside_single_tile])
    payload = lax.map(observe_one, jnp.arange(domains, dtype=jnp.int32))
    payload = payload.reshape(DOM_X, DOM_Y, MEMBER_TOTAL + 4, SLOTS)
    padded = jnp.pad(payload, ((1, 1), (1, 1), (0, 0), (0, 0)))

    def analyse_one(number):
        between_tiles, inside_single_tile, model_levels_stack = slice_fields(number)
        neighbours = lax.dynamic_slice(padded, (between_tiles.astype(jnp.int32), inside_single_tile.astype(jnp.int32), jnp.int32(0), jnp.int32(0)), (3, 3, MEMBER_TOTAL + 4, SLOTS))
        return analyse(neighbours, model_levels_stack)
    posterior_members = lax.map(analyse_one, jnp.arange(domains, dtype=jnp.int32))
    posterior_members = posterior_members.reshape(DOM_X, DOM_Y, MEMBER_TOTAL, REVISED_LEVELS, TILE_SPAN_FIRST, TILE_SPAN_SECOND).transpose(2, 3, 0, 4, 1, 5).reshape(MEMBER_TOTAL, REVISED_LEVELS, MESH_SPAN_FIRST, MESH_SPAN_SECOND)
    return jnp.concatenate([posterior_members, prior_members[:, REVISED_LEVELS:]], axis=1)
```

```python
import functools
import math

import jax
import jax.numpy as jnp
import numpy as np
from jax import lax
from jax.experimental import pallas as pl
from jax.experimental.pallas import tpu as pltpu
from jax.sharding import PartitionSpec as P

MEMBERS = 48
UPPER = 8
LANES = 128
SLOTS = 256
RADIUS = 8
BLOCK = 4
CHUNK = 16
GROUPS = LANES // CHUNK
BLOCKS_Y = LANES // BLOCK
ROWS = 64
PACK = 56
DOMS = 16
F32 = jnp.float32
BF16 = jnp.bfloat16


def split3(x):
    hi = x.astype(BF16)
    rest = x - hi.astype(F32)
    mid = rest.astype(BF16)
    low = (rest - mid.astype(F32)).astype(BF16)
    return hi, mid, low


def split2(x):
    hi = x.astype(BF16)
    return hi, (x - hi.astype(F32)).astype(BF16)


def nt(a, b):
    return lax.dot_general(a, b, (((1,), (1,)), ((), ())), preferred_element_type=F32)


def nn(a, b):
    return lax.dot_general(a, b, (((1,), (0,)), ((), ())), preferred_element_type=F32)


def row_spread():
    m = np.zeros((64, 48), np.float32)
    for x in range(8):
        for r in range(6):
            m[x * 8 + r, r * 8 + x] = 1.0
    return m


def row_compact():
    m = np.zeros((ROWS, 80), np.float32)
    for v in range(9):
        for r in range(6):
            m[v * 6 + r, v * 8 + r] = 1.0
    for r in range(6):
        m[54 + r, 72 + r] = 1.0
    return m


def row_sample():
    m = np.zeros((9 * PACK, DOMS * ROWS), np.float32)
    for v in range(9):
        for i in range(MEMBERS):
            for layer in range(2):
                m[v * PACK + i, (i // 3) * ROWS + v * 6 + (i % 3) * 2 + layer] = 0.5
    for s in range(DOMS):
        for r in range(3):
            m[8 * PACK + 48, s * ROWS + 54 + r] = 1.0
            m[8 * PACK + 49, s * ROWS + 57 + r] = 1.0
    return m


OFFSETS = (10, 14, 2, 6)


def taper_rows():
    lane = np.arange(LANES)
    x, y = lane // CHUNK, lane % CHUNK
    t = np.zeros((24, LANES), np.float32)
    for k, o in enumerate(OFFSETS):
        gap_y = np.where(y >= o, y - o, y - o + CHUNK) - 6 - 1.5
        for seg in range(3):
            for p in range(2):
                gap_x = (seg - 1) * 8 + x - (4 * p + 1.5)
                s = gap_x * gap_x + gap_y * gap_y
                t[(k * 3 + seg) * 2 + p] = np.where(s < RADIUS * RADIUS, (1 - s / 64.0) ** 2, 0.0)
    return t


def expand_rows():
    m = np.zeros((128, 512), np.float32)
    for h in range(2):
        for p in range(2):
            for y in range(128):
                m[h * 64 + p * 32 + y // 4, h * 256 + p * 128 + y] = 1.0
    return np.concatenate([m, m], 0)


def pack_kernel(where, tally, x_ref, reading, error, cell, spread, compact, out, own, work):
    me = where[0]
    live = lax.broadcasted_iota(jnp.int32, (1, SLOTS), 1) < tally[0]
    prec = jnp.where(live, 1.0 / error[...], 0.0)
    vals = jnp.where(live, prec * reading[...], 0.0)
    c = cell[...]
    x, y = c // LANES, c % LANES
    group = y // CHUNK
    lane = x * CHUNK + y % CHUNK
    hit = lax.broadcasted_iota(jnp.int32, (8, SLOTS), 0) == group
    spot = (lax.broadcasted_iota(jnp.int32, (LANES, SLOTS), 0) == lane).astype(F32).astype(BF16)
    pv = jnp.concatenate([jnp.where(hit, prec, 0.0), jnp.where(hit, vals, 0.0)], 0)
    a, b, d = split3(pv)
    pv = nt(a, spot) + nt(b, spot) + nt(d, spot)
    own[...] = pv
    sub = lax.broadcasted_iota(jnp.int32, (8, LANES), 0)
    col = lax.broadcasted_iota(jnp.int32, (8, LANES), 1)
    high = (col % CHUNK) >= 8

    def edge(g):
        res = jnp.zeros((8, LANES), F32)
        for n in range(2):
            parts = split3(jnp.broadcast_to(pv[n * 8 + g : n * 8 + g + 1, :], (8, LANES)))
            for k in range(3):
                res = jnp.where(sub == n * 3 + k, parts[k].astype(F32), res)
        return res

    last = jnp.where(high, edge(7), 0.0)
    first = jnp.where(high, 0.0, edge(0))

    flat = x_ref[...].reshape(48, 16 * LANES)
    rows = nn(spread[...], flat)
    for d in range(DOMS):
        v = [rows[8 * k : 8 * k + 8, d * LANES : (d + 1) * LANES] for k in range(8)]
        for step in (4, 2, 1):
            width = step * CHUNK
            low = ((col // width) % 2) == 0
            new = list(v)
            for k in range(8):
                if not k & step:
                    a, b = v[k], v[k + step]
                    new[k] = jnp.where(low, a, pltpu.roll(b, width, 1))
                    new[k + step] = jnp.where(low, pltpu.roll(a, LANES - width, 1), b)
            v = new
        for k in range(8):
            work[d, 8 * k : 8 * k + 8, :] = v[k]
    for d in range(DOMS):
        left = work[(d - 1) % DOMS, 56:64, :]
        right = work[(d + 1) % DOMS, 0:8, :]
        work[d, 64:72, :] = jnp.where(high, left, right)
        work[d, 72:80, :] = jnp.where(
            me == d - 1, last, jnp.where(me == d + 1, first, jnp.zeros_like(first))
        )
    for d in range(DOMS):
        out[d] = nn(compact[...], work[d].astype(BF16)).astype(BF16)


def sample_kernel(r_ref, own, choose, out):
    pv = own[...]
    res = nn(choose[...], r_ref[...].reshape(DOMS * ROWS, LANES))
    for v in range(9):
        s = res[v * PACK : v * PACK + MEMBERS]
        mean = jnp.sum(s, axis=0, keepdims=True) * (1.0 / MEMBERS)
        if v < 8:
            prec, vals = pv[v : v + 1], pv[8 + v : 9 + v]
        else:
            prec, vals = res[v * PACK + 48 : v * PACK + 49], res[v * PACK + 49 : v * PACK + 50]
        out[v, 0:48, :] = s - mean
        sub = lax.broadcasted_iota(jnp.int32, (8, LANES), 0)
        out[v, 48:56, :] = jnp.where(
            sub == 0, prec, jnp.where(sub == 1, vals - prec * mean, 0.0)
        )


def solve_kernel(up, own, down, taper, out, grams, mat, piv, fac):
    segs = (up, own, down)
    lane = lax.broadcasted_iota(jnp.int32, (1, LANES), 1) % CHUNK

    def group(g, carry):
        before = jnp.where(g == 0, 8, g - 1)
        after = jnp.where(g == 7, 8, g + 1)
        for k, o in enumerate(OFFSETS):
            v0, v1 = (before, g) if k < 2 else (g, after)
            mask = lane >= o
            ahi, alo = [], []
            lhi, llo = [], []
            for s in range(3):
                w = jnp.where(mask, segs[s][v0], segs[s][v1])
                a = w[0:48]
                prec, drv = w[48:49], w[49:50]
                h, l = split2(a)
                ahi.append(h)
                alo.append(l)
                t0 = taper[(k * 3 + s) * 2 : (k * 3 + s) * 2 + 1, :]
                t1 = taper[(k * 3 + s) * 2 + 1 : (k * 3 + s) * 2 + 2, :]
                sub = lax.broadcasted_iota(jnp.int32, (16, LANES), 0)
                lhs = jnp.concatenate(
                    [
                        a * (prec * t0),
                        a * (prec * t1),
                        jnp.where(sub == 0, drv * t0, jnp.where(sub == 1, drv * t1, 0.0)),
                    ],
                    0,
                )
                h, l = split2(lhs)
                lhi.append(h)
                llo.append(l)
            left = jnp.concatenate(lhi + lhi + llo, 1)
            right = jnp.concatenate(ahi + alo + ahi, 1)
            res = nt(left, right)
            q = g * 4 + k
            res = jnp.concatenate([res, jnp.zeros((112, LANES - MEMBERS), F32)], 1)
            row0 = pl.multiple_of(q * PACK, 8)
            row1 = pl.multiple_of((q + BLOCKS_Y) * PACK, 8)
            grams[pl.ds(row0, 48), :] = res[0:48]
            grams[pl.ds(row0 + 48, 8), :] = res[96:104]
            grams[pl.ds(row1, 48), :] = res[48:96]
            grams[pl.ds(row1 + 48, 8), :] = pltpu.roll(res[96:104], 7, 0)
        return carry

    lax.fori_loop(0, 8, group, 0)

    for t in range(25):
        a = grams[pl.ds(2 * t, 64, stride=PACK), :]
        b = grams[pl.ds(2 * t + 1, 64, stride=PACK), :] if t < 24 else a
        mat[t] = jnp.concatenate([a, b], 0).T[0:48, :]

    sub = lax.broadcasted_iota(jnp.int32, (8, LANES), 0)
    half = lax.broadcasted_iota(jnp.int32, (8, LANES), 1) // 64
    half0 = half == 0

    def tiles(t):
        return [mat[t, 8 * j : 8 * j + 8, :] for j in range(6)]

    drive = tiles(24)
    scale = []
    for panel in range(6):
        rows = [tiles(4 * panel + n) for n in range(4)]
        for n in range(4):
            diag = jnp.where(sub == 2 * n + half, MEMBERS - 1.0, 0.0)
            rows[n][panel] = rows[n][panel] + diag
        for k in range(8):
            n, h = k // 2, k % 2
            mine = half == h
            row = [jnp.where(mine, x, pltpu.roll(x, 64, 1)) for x in rows[n]]
            inv = 1.0 / jnp.broadcast_to(row[panel][k : k + 1, :], (8, LANES))
            scale.append(jnp.sqrt((MEMBERS - 1.0) * inv[0:1, :]))
            here = sub == k
            f = row[panel] * inv
            for j in range(panel + 1, 6):
                fac[k, 8 * j : 8 * j + 8, :] = row[j] * inv
            row[panel] = jnp.where(here, 1.0, row[panel])
            for j in range(6):
                if j != panel:
                    piv[k, 8 * j : 8 * j + 8, :] = row[j]
            piv[k, 8 * panel : 8 * panel + 8, :] = jnp.where(sub <= k, row[panel], 0.0)
            fd = jnp.broadcast_to(drive[panel][k : k + 1, :], (8, LANES)) * inv
            drive[panel] = jnp.where(here, 0.0, drive[panel])
            drive = [drive[j] - fd * row[j] for j in range(6)]
            for n2 in range(n, 4):
                if n2 == n and h == 1:
                    rows[n][panel] = jnp.where(
                        jnp.logical_and(here, mine), 1.0, rows[n][panel]
                    )
                    continue
                fb = jnp.broadcast_to(f[2 * n2 + 1 : 2 * n2 + 2, :], (8, LANES))
                if n2 == n:
                    fp = jnp.where(half0, 0.0, fb)
                    rows[n][panel] = jnp.where(
                        here, jnp.where(half0, 1.0, 0.0), rows[n][panel]
                    )
                else:
                    fa = jnp.broadcast_to(f[2 * n2 : 2 * n2 + 1, :], (8, LANES))
                    fp = jnp.where(half0, fa, fb)
                    rows[n2][panel] = jnp.where(here, 0.0, rows[n2][panel])
                rows[n2] = [rows[n2][j] - fp * row[j] for j in range(6)]
        for n in range(4):
            for j in range(panel + 1):
                mat[4 * panel + n, 8 * j : 8 * j + 8, :] = rows[n][j]
        for block in range(panel + 1, 6):
            js = list(range(panel + 1)) + list(range(block, 6))
            acc = [
                {
                    j: jnp.zeros((8, LANES), F32)
                    if j == panel
                    else mat[4 * block + n, 8 * j : 8 * j + 8, :]
                    for j in js
                }
                for n in range(4)
            ]
            for k in range(8):
                pr = {j: piv[k, 8 * j : 8 * j + 8, :] for j in js}
                for n in range(4):
                    i = 8 * block + 2 * n
                    fa = jnp.broadcast_to(fac[k, i : i + 1, :], (8, LANES))
                    fb = jnp.broadcast_to(fac[k, i + 1 : i + 2, :], (8, LANES))
                    fp = jnp.where(half0, fa, fb)
                    for j in js:
                        acc[n][j] = acc[n][j] - fp * pr[j]
            for n in range(4):
                for j in js:
                    mat[4 * block + n, 8 * j : 8 * j + 8, :] = acc[n][j]

    for t in range(24):
        panel, n = t // 4, t % 4
        sc = jnp.where(half0, scale[2 * t], scale[2 * t + 1])
        w = []
        for j in range(6):
            x = -drive[j]
            if j <= panel:
                e = mat[t, 8 * j : 8 * j + 8, :]
                if j == panel:
                    e = jnp.where(sub <= 2 * n + half, e, 0.0)
                x = x + sc * e
            w.append(x)
        total = jnp.sum(w[0] + w[1] + w[2] + w[3] + w[4] + w[5], axis=0, keepdims=True)
        fix = (1.0 - total) * (1.0 / MEMBERS)
        for j in range(6):
            out[t, 8 * j : 8 * j + 8, :] = w[j] + fix


def transform_kernel(w_ref, x_ref, expand, out, wide, xs):
    w = w_ref[...].reshape(24 * 48, LANES)
    hi, low = split2(w)
    wide[...] = nn(jnp.concatenate([hi, low], 1), expand[...])

    def widen(i, c):
        for l in range(8):
            xs[i, l] = x_ref[i, l].astype(F32)
        return c

    lax.fori_loop(0, MEMBERS, widen, 0)
    top = lax.broadcasted_iota(jnp.int32, (8, LANES), 0) < 4

    def pair(t, c):
        def step(i, acc):
            acc = list(acc)
            for u in range(4):
                r = t * 48 + i * 4 + u
                line = wide[pl.ds(r, 1), :]
                ws = []
                for h in range(2):
                    a = jnp.broadcast_to(line[:, h * 256 : h * 256 + 128], (8, LANES))
                    b = jnp.broadcast_to(line[:, h * 256 + 128 : h * 256 + 256], (8, LANES))
                    ws.append(jnp.where(top, a, b))
                for l in range(8):
                    x = xs[i * 4 + u, l]
                    acc[l] = acc[l] + x * ws[0]
                    acc[8 + l] = acc[8 + l] + x * ws[1]
            return tuple(acc)

        acc = lax.fori_loop(0, 12, step, tuple(jnp.zeros((8, LANES), F32) for _ in range(16)))
        for h in range(2):
            for l in range(8):
                out[2 * t + h, l] = acc[8 * h + l].astype(BF16)
        return c

    lax.fori_loop(0, 24, pair, 0)


def send_kernel(x_ref, out, sems):
    copies = []
    for d in range(DOMS):
        copies.append(
            pltpu.make_async_copy(
                x_ref.at[:, 0:UPPER, :, pl.ds(d * LANES, LANES)], out.at[d], sems.at[d]
            )
        )
    for c in copies:
        c.start()
    for c in copies:
        c.wait()


def finish_kernel(b_ref, x_ref, out, sems):
    copies = [
        pltpu.make_async_copy(
            x_ref.at[:, UPPER : 2 * UPPER], out.at[:, UPPER : 2 * UPPER], sems.at[DOMS]
        )
    ]
    for d in range(DOMS):
        copies.append(
            pltpu.make_async_copy(
                b_ref.at[d], out.at[:, 0:UPPER, :, pl.ds(d * LANES, LANES)], sems.at[d]
            )
        )
    for c in copies:
        c.start()
    for c in copies:
        c.wait()


VM = pl.BlockSpec(memory_space=pltpu.VMEM)
SM = pl.BlockSpec(memory_space=pltpu.SMEM)
ANY = pl.BlockSpec(memory_space=pl.ANY)
LIMIT = pltpu.CompilerParams(vmem_limit_bytes=48 * 2**20)


def body(prior, reading, error, cell, tally):
    me = lax.axis_index("member").astype(jnp.int32).reshape(1)
    const = lambda a, t: jnp.asarray(a, t)
    packed, own = pl.pallas_call(
        pack_kernel,
        grid=(1,),
        in_specs=[
            SM,
            SM,
            pl.BlockSpec((3, 2, 8, 2048), lambda g: (0, 0, 0, 0)),
            VM,
            VM,
            VM,
            VM,
            VM,
        ],
        out_specs=[VM, VM],
        out_shape=[
            jax.ShapeDtypeStruct((DOMS, ROWS, LANES), BF16),
            jax.ShapeDtypeStruct((16, LANES), F32),
        ],
        scratch_shapes=[pltpu.VMEM((DOMS, 80, LANES), F32)],
        compiler_params=LIMIT,
        name="pack",
    )(
        me,
        tally.reshape(1),
        prior,
        reading.reshape(1, SLOTS),
        error.reshape(1, SLOTS),
        cell.reshape(1, SLOTS),
        const(row_spread(), BF16),
        const(row_compact(), BF16),
    )
    fields = pl.pallas_call(
        send_kernel,
        in_specs=[ANY],
        out_specs=ANY,
        out_shape=jax.ShapeDtypeStruct((DOMS, 3, UPPER, 8, LANES), BF16),
        scratch_shapes=[pltpu.SemaphoreType.DMA((DOMS,))],
        name="send",
    )(prior)
    packed = lax.all_to_all(packed, "member", 0, 0, tiled=True)
    fields = lax.all_to_all(
        fields.reshape(MEMBERS, UPPER, 8, LANES), "member", 0, 0, tiled=True
    )
    sampled = pl.pallas_call(
        sample_kernel,
        in_specs=[VM, VM, VM],
        out_specs=VM,
        out_shape=jax.ShapeDtypeStruct((9, PACK, LANES), F32),
        compiler_params=LIMIT,
        name="sample",
    )(packed, own, const(row_sample(), BF16))
    ends = lax.axis_size("tile") - 1
    up = lax.ppermute(sampled, "tile", [(i, i + 1) for i in range(ends)])
    down = lax.ppermute(sampled, "tile", [(i + 1, i) for i in range(ends)])
    weights = pl.pallas_call(
        solve_kernel,
        in_specs=[VM, VM, VM, VM],
        out_specs=VM,
        out_shape=jax.ShapeDtypeStruct((24, 48, LANES), F32),
        scratch_shapes=[
            pltpu.VMEM((64 * PACK, LANES), F32),
            pltpu.VMEM((25, 48, LANES), F32),
            pltpu.VMEM((8, 48, LANES), F32),
            pltpu.VMEM((8, 48, LANES), F32),
        ],
        compiler_params=LIMIT,
        name="solve",
    )(up, sampled, down, const(taper_rows(), F32))
    result = pl.pallas_call(
        transform_kernel,
        in_specs=[VM, VM, VM],
        out_specs=VM,
        out_shape=jax.ShapeDtypeStruct((MEMBERS, UPPER, 8, LANES), BF16),
        scratch_shapes=[
            pltpu.VMEM((24 * 48, 512), F32),
            pltpu.VMEM((MEMBERS, UPPER, 8, LANES), F32),
        ],
        compiler_params=LIMIT,
        name="transform",
    )(weights, fields, const(expand_rows(), BF16))
    result = lax.all_to_all(result, "member", 0, 0, tiled=True)
    return pl.pallas_call(
        finish_kernel,
        in_specs=[ANY, ANY],
        out_specs=ANY,
        out_shape=jax.ShapeDtypeStruct(prior.shape, BF16),
        scratch_shapes=[pltpu.SemaphoreType.DMA((DOMS + 1,))],
        name="finish",
    )(result.reshape(DOMS, 3, UPPER, 8, LANES), prior)


def solution(mesh):
    return jax.shard_map(
        body,
        mesh=mesh,
        in_specs=(
            P("member", None, "tile", None),
            P("tile", "member", None),
            P("tile", "member", None),
            P("tile", "member", None),
            P("tile", "member"),
        ),
        out_specs=P("member", None, "tile", None),
        check_vma=False,
    )
```

```python
import functools
import math

import jax
import jax.numpy as jnp
import numpy as np
from jax import lax
from jax.experimental import pallas as pl
from jax.experimental.pallas import tpu as pltpu
from jax.sharding import PartitionSpec as P

MEMBERS = 48
UPPER = 8
LANES = 128
SLOTS = 256
RADIUS = 8
BLOCK = 4
CHUNK = 16
GROUPS = LANES // CHUNK
BLOCKS_Y = LANES // BLOCK
ROWS = 64
PACK = 56
DOMS = 16
F32 = jnp.float32
BF16 = jnp.bfloat16


def split3(x):
    hi = x.astype(BF16)
    rest = x - hi.astype(F32)
    mid = rest.astype(BF16)
    low = (rest - mid.astype(F32)).astype(BF16)
    return hi, mid, low


def split2(x):
    hi = x.astype(BF16)
    return hi, (x - hi.astype(F32)).astype(BF16)


def nt(a, b):
    return lax.dot_general(a, b, (((1,), (1,)), ((), ())), preferred_element_type=F32)


def nn(a, b):
    return lax.dot_general(a, b, (((1,), (0,)), ((), ())), preferred_element_type=F32)


def row_spread():
    m = np.zeros((64, 48), np.float32)
    for x in range(8):
        for r in range(6):
            m[x * 8 + r, r * 8 + x] = 1.0
    return m


def row_compact():
    m = np.zeros((ROWS, 80), np.float32)
    for v in range(9):
        for r in range(6):
            m[v * 6 + r, v * 8 + r] = 1.0
    for r in range(6):
        m[54 + r, 72 + r] = 1.0
    return m


def row_sample():
    m = np.zeros((9 * PACK, DOMS * ROWS), np.float32)
    for v in range(9):
        for i in range(MEMBERS):
            for layer in range(2):
                m[v * PACK + i, (i // 3) * ROWS + v * 6 + (i % 3) * 2 + layer] = 0.5
    for s in range(DOMS):
        for r in range(3):
            m[8 * PACK + 48, s * ROWS + 54 + r] = 1.0
            m[8 * PACK + 49, s * ROWS + 57 + r] = 1.0
    return m


OFFSETS = (10, 14, 2, 6)


def taper_rows():
    lane = np.arange(LANES)
    x, y = lane // CHUNK, lane % CHUNK
    t = np.zeros((24, LANES), np.float32)
    for k, o in enumerate(OFFSETS):
        gap_y = np.where(y >= o, y - o, y - o + CHUNK) - 6 - 1.5
        for seg in range(3):
            for p in range(2):
                gap_x = (seg - 1) * 8 + x - (4 * p + 1.5)
                s = gap_x * gap_x + gap_y * gap_y
                t[(k * 3 + seg) * 2 + p] = np.where(s < RADIUS * RADIUS, (1 - s / 64.0) ** 2, 0.0)
    return t


def expand_rows():
    m = np.zeros((128, 512), np.float32)
    for h in range(2):
        for p in range(2):
            for y in range(128):
                m[h * 64 + p * 32 + y // 4, h * 256 + p * 128 + y] = 1.0
    return np.concatenate([m, m], 0)


def pack_kernel(where, tally, x_ref, reading, error, cell, spread, compact, out, own, work):
    me = where[0]
    live = lax.broadcasted_iota(jnp.int32, (1, SLOTS), 1) < tally[0]
    prec = jnp.where(live, 1.0 / error[...], 0.0)
    vals = jnp.where(live, prec * reading[...], 0.0)
    c = cell[...]
    x, y = c // LANES, c % LANES
    group = y // CHUNK
    lane = x * CHUNK + y % CHUNK
    hit = lax.broadcasted_iota(jnp.int32, (8, SLOTS), 0) == group
    spot = (lax.broadcasted_iota(jnp.int32, (LANES, SLOTS), 0) == lane).astype(F32).astype(BF16)
    pv = jnp.concatenate([jnp.where(hit, prec, 0.0), jnp.where(hit, vals, 0.0)], 0)
    a, b, d = split3(pv)
    pv = nt(a, spot) + nt(b, spot) + nt(d, spot)
    own[...] = pv
    sub = lax.broadcasted_iota(jnp.int32, (8, LANES), 0)
    col = lax.broadcasted_iota(jnp.int32, (8, LANES), 1)
    high = (col % CHUNK) >= 8

    def edge(g):
        res = jnp.zeros((8, LANES), F32)
        for n in range(2):
            parts = split3(jnp.broadcast_to(pv[n * 8 + g : n * 8 + g + 1, :], (8, LANES)))
            for k in range(3):
                res = jnp.where(sub == n * 3 + k, parts[k].astype(F32), res)
        return res

    last = jnp.where(high, edge(7), 0.0)
    first = jnp.where(high, 0.0, edge(0))

    flat = x_ref[...].reshape(48, 16 * LANES)
    rows = nn(spread[...], flat)
    for d in range(DOMS):
        v = [rows[8 * k : 8 * k + 8, d * LANES : (d + 1) * LANES] for k in range(8)]
        for step in (4, 2, 1):
            width = step * CHUNK
            low = ((col // width) % 2) == 0
            new = list(v)
            for k in range(8):
                if not k & step:
                    a, b = v[k], v[k + step]
                    new[k] = jnp.where(low, a, pltpu.roll(b, width, 1))
                    new[k + step] = jnp.where(low, pltpu.roll(a, LANES - width, 1), b)
            v = new
        for k in range(8):
            work[d, 8 * k : 8 * k + 8, :] = v[k]
    for d in range(DOMS):
        left = work[(d - 1) % DOMS, 56:64, :]
        right = work[(d + 1) % DOMS, 0:8, :]
        work[d, 64:72, :] = jnp.where(high, left, right)
        work[d, 72:80, :] = jnp.where(
            me == d - 1, last, jnp.where(me == d + 1, first, jnp.zeros_like(first))
        )
    for d in range(DOMS):
        out[d] = nn(compact[...], work[d].astype(BF16)).astype(BF16)


def sample_kernel(r_ref, own, choose, out):
    pv = own[...]
    res = nn(choose[...], r_ref[...].reshape(DOMS * ROWS, LANES))
    for v in range(9):
        s = res[v * PACK : v * PACK + MEMBERS]
        mean = jnp.sum(s, axis=0, keepdims=True) * (1.0 / MEMBERS)
        if v < 8:
            prec, vals = pv[v : v + 1], pv[8 + v : 9 + v]
        else:
            prec, vals = res[v * PACK + 48 : v * PACK + 49], res[v * PACK + 49 : v * PACK + 50]
        out[v, 0:48, :] = s - mean
        sub = lax.broadcasted_iota(jnp.int32, (8, LANES), 0)
        out[v, 48:56, :] = jnp.where(
            sub == 0, prec, jnp.where(sub == 1, vals - prec * mean, 0.0)
        )


def solve_kernel(up, own, down, taper, out, grams, mat, piv, fac):
    segs = (up, own, down)
    lane = lax.broadcasted_iota(jnp.int32, (1, LANES), 1) % CHUNK

    def group(g, carry):
        before = jnp.where(g == 0, 8, g - 1)
        after = jnp.where(g == 7, 8, g + 1)
        for k, o in enumerate(OFFSETS):
            v0, v1 = (before, g) if k < 2 else (g, after)
            mask = lane >= o
            ahi, alo = [], []
            lhi, llo = [], []
            for s in range(3):
                w = jnp.where(mask, segs[s][v0], segs[s][v1])
                a = w[0:48]
                prec, drv = w[48:49], w[49:50]
                h, l = split2(a)
                ahi.append(h)
                alo.append(l)
                t0 = taper[(k * 3 + s) * 2 : (k * 3 + s) * 2 + 1, :]
                t1 = taper[(k * 3 + s) * 2 + 1 : (k * 3 + s) * 2 + 2, :]
                sub = lax.broadcasted_iota(jnp.int32, (16, LANES), 0)
                lhs = jnp.concatenate(
                    [
                        a * (prec * t0),
                        a * (prec * t1),
                        jnp.where(sub == 0, drv * t0, jnp.where(sub == 1, drv * t1, 0.0)),
                    ],
                    0,
                )
                h, l = split2(lhs)
                lhi.append(h)
                llo.append(l)
            left = jnp.concatenate(lhi + lhi + llo, 1)
            right = jnp.concatenate(ahi + alo + ahi, 1)
            res = nt(left, right)
            q = g * 4 + k
            res = jnp.concatenate([res, jnp.zeros((112, LANES - MEMBERS), F32)], 1)
            row0 = pl.multiple_of(q * PACK, 8)
            row1 = pl.multiple_of((q + BLOCKS_Y) * PACK, 8)
            grams[pl.ds(row0, 48), :] = res[0:48]
            grams[pl.ds(row0 + 48, 8), :] = res[96:104]
            grams[pl.ds(row1, 48), :] = res[48:96]
            grams[pl.ds(row1 + 48, 8), :] = pltpu.roll(res[96:104], 7, 0)
        return carry

    lax.fori_loop(0, 8, group, 0)

    for t in range(25):
        a = grams[pl.ds(2 * t, 64, stride=PACK), :]
        b = grams[pl.ds(2 * t + 1, 64, stride=PACK), :] if t < 24 else a
        mat[t] = jnp.concatenate([a, b], 0).T[0:48, :]

    sub = lax.broadcasted_iota(jnp.int32, (8, LANES), 0)
    half = lax.broadcasted_iota(jnp.int32, (8, LANES), 1) // 64
    half0 = half == 0

    def tiles(t):
        return [mat[t, 8 * j : 8 * j + 8, :] for j in range(6)]

    drive = tiles(24)
    scale = []
    for panel in range(6):
        rows = [tiles(4 * panel + n) for n in range(4)]
        for n in range(4):
            diag = jnp.where(sub == 2 * n + half, MEMBERS - 1.0, 0.0)
            rows[n][panel] = rows[n][panel] + diag
        for k in range(8):
            n, h = k // 2, k % 2
            mine = half == h
            row = [jnp.where(mine, x, pltpu.roll(x, 64, 1)) for x in rows[n]]
            inv = 1.0 / jnp.broadcast_to(row[panel][k : k + 1, :], (8, LANES))
            scale.append(jnp.sqrt((MEMBERS - 1.0) * inv[0:1, :]))
            here = sub == k
            f = row[panel] * inv
            for j in range(panel + 1, 6):
                fac[k, 8 * j : 8 * j + 8, :] = row[j] * inv
            row[panel] = jnp.where(here, 1.0, row[panel])
            for j in range(6):
                if j != panel:
                    piv[k, 8 * j : 8 * j + 8, :] = row[j]
            piv[k, 8 * panel : 8 * panel + 8, :] = jnp.where(sub <= k, row[panel], 0.0)
            fd = jnp.broadcast_to(drive[panel][k : k + 1, :], (8, LANES)) * inv
            drive[panel] = jnp.where(here, 0.0, drive[panel])
            drive = [drive[j] - fd * row[j] for j in range(6)]
            for n2 in range(n, 4):
                if n2 == n and h == 1:
                    rows[n][panel] = jnp.where(
                        jnp.logical_and(here, mine), 1.0, rows[n][panel]
                    )
                    continue
                fb = jnp.broadcast_to(f[2 * n2 + 1 : 2 * n2 + 2, :], (8, LANES))
                if n2 == n:
                    fp = jnp.where(half0, 0.0, fb)
                    rows[n][panel] = jnp.where(
                        here, jnp.where(half0, 1.0, 0.0), rows[n][panel]
                    )
                else:
                    fa = jnp.broadcast_to(f[2 * n2 : 2 * n2 + 1, :], (8, LANES))
                    fp = jnp.where(half0, fa, fb)
                    rows[n2][panel] = jnp.where(here, 0.0, rows[n2][panel])
                rows[n2] = [rows[n2][j] - fp * row[j] for j in range(6)]
        for n in range(4):
            for j in range(panel + 1):
                mat[4 * panel + n, 8 * j : 8 * j + 8, :] = rows[n][j]
        for block in range(panel + 1, 6):
            js = list(range(panel + 1)) + list(range(block, 6))
            acc = [
                {
                    j: jnp.zeros((8, LANES), F32)
                    if j == panel
                    else mat[4 * block + n, 8 * j : 8 * j + 8, :]
                    for j in js
                }
                for n in range(4)
            ]
            for k in range(8):
                pr = {j: piv[k, 8 * j : 8 * j + 8, :] for j in js}
                for n in range(4):
                    i = 8 * block + 2 * n
                    fa = jnp.broadcast_to(fac[k, i : i + 1, :], (8, LANES))
                    fb = jnp.broadcast_to(fac[k, i + 1 : i + 2, :], (8, LANES))
                    fp = jnp.where(half0, fa, fb)
                    for j in js:
                        acc[n][j] = acc[n][j] - fp * pr[j]
            for n in range(4):
                for j in js:
                    mat[4 * block + n, 8 * j : 8 * j + 8, :] = acc[n][j]

    for t in range(24):
        panel, n = t // 4, t % 4
        sc = jnp.where(half0, scale[2 * t], scale[2 * t + 1])
        w = []
        for j in range(6):
            x = -drive[j]
            if j <= panel:
                e = mat[t, 8 * j : 8 * j + 8, :]
                if j == panel:
                    e = jnp.where(sub <= 2 * n + half, e, 0.0)
                x = x + sc * e
            w.append(x)
        total = jnp.sum(w[0] + w[1] + w[2] + w[3] + w[4] + w[5], axis=0, keepdims=True)
        fix = (1.0 - total) * (1.0 / MEMBERS)
        for j in range(6):
            out[t, 8 * j : 8 * j + 8, :] = w[j] + fix


def transform_kernel(w_ref, x_ref, expand, out, wide, xs):
    w = w_ref[...].reshape(24 * 48, LANES)
    hi, low = split2(w)
    wide[...] = nn(jnp.concatenate([hi, low], 1), expand[...])

    def widen(i, c):
        for l in range(8):
            xs[i, l] = x_ref[i, l].astype(F32)
        return c

    lax.fori_loop(0, MEMBERS, widen, 0)
    top = lax.broadcasted_iota(jnp.int32, (8, LANES), 0) < 4

    def pair(t, c):
        def step(i, acc):
            acc = list(acc)
            for u in range(4):
                r = t * 48 + i * 4 + u
                line = wide[pl.ds(r, 1), :]
                ws = []
                for h in range(2):
                    a = jnp.broadcast_to(line[:, h * 256 : h * 256 + 128], (8, LANES))
                    b = jnp.broadcast_to(line[:, h * 256 + 128 : h * 256 + 256], (8, LANES))
                    ws.append(jnp.where(top, a, b))
                for l in range(8):
                    x = xs[i * 4 + u, l]
                    acc[l] = acc[l] + x * ws[0]
                    acc[8 + l] = acc[8 + l] + x * ws[1]
            return tuple(acc)

        acc = lax.fori_loop(0, 12, step, tuple(jnp.zeros((8, LANES), F32) for _ in range(16)))
        for h in range(2):
            for l in range(8):
                out[2 * t + h, l] = acc[8 * h + l].astype(BF16)
        return c

    lax.fori_loop(0, 24, pair, 0)


def send_kernel(x_ref, out):
    for d in range(DOMS):
        for m in range(3):
            out[d, m] = x_ref[m, :, :, d * LANES : (d + 1) * LANES]


def lower_kernel(x_ref, out):
    out[...] = x_ref[...]


def finish_kernel(b_ref, partial, out, work, sems):
    del partial
    copies = []
    for m in range(3):
        for d in range(DOMS):
            work[m, :, :, d * LANES : (d + 1) * LANES] = b_ref[d, m]
        copy = pltpu.make_async_copy(work.at[m], out.at[m, 0:UPPER], sems.at[m])
        copy.start()
        copies.append(copy)
    for copy in copies:
        copy.wait()


VM = pl.BlockSpec(memory_space=pltpu.VMEM)
SM = pl.BlockSpec(memory_space=pltpu.SMEM)
ANY = pl.BlockSpec(memory_space=pl.ANY)
FULL = pltpu.CompilerParams(vmem_limit_bytes=62000000)
LIMIT = pltpu.CompilerParams(vmem_limit_bytes=48 * 2**20)


def body(prior, reading, error, cell, tally):
    me = lax.axis_index("member").astype(jnp.int32).reshape(1)
    const = lambda a, t: jnp.asarray(a, t)
    whole = lambda *shape: pl.BlockSpec(shape, lambda g: (0,) * len(shape))
    packed, own = pl.pallas_call(
        pack_kernel,
        grid=(1,),
        in_specs=[
            SM,
            SM,
            whole(3, 2, 8, 2048),
            whole(1, SLOTS),
            whole(1, SLOTS),
            whole(1, SLOTS),
            whole(64, 48),
            whole(ROWS, 80),
        ],
        out_specs=[VM, VM],
        out_shape=[
            jax.ShapeDtypeStruct((DOMS, ROWS, LANES), BF16),
            jax.ShapeDtypeStruct((16, LANES), F32),
        ],
        scratch_shapes=[pltpu.VMEM((DOMS, 80, LANES), F32)],
        compiler_params=FULL,
        name="pack",
    )(
        me,
        tally.reshape(1),
        prior,
        reading.reshape(1, SLOTS),
        error.reshape(1, SLOTS),
        cell.reshape(1, SLOTS),
        const(row_spread(), BF16),
        const(row_compact(), BF16),
    )
    fields = pl.pallas_call(
        send_kernel,
        grid=(1,),
        in_specs=[whole(3, UPPER, 8, 2048)],
        out_specs=VM,
        out_shape=jax.ShapeDtypeStruct((DOMS, 3, UPPER, 8, LANES), BF16),
        compiler_params=FULL,
        name="send",
    )(prior)
    lower = pl.BlockSpec((1, UPPER, 8, 2048), lambda g: (g, 1, 0, 0))
    partial = pl.pallas_call(
        lower_kernel,
        grid=(3,),
        in_specs=[lower],
        out_specs=lower,
        out_shape=jax.ShapeDtypeStruct(prior.shape, BF16),
        compiler_params=FULL,
        name="lower",
    )(prior)
    packed = lax.all_to_all(packed, "member", 0, 0, tiled=True)
    fields = lax.all_to_all(
        fields.reshape(MEMBERS, UPPER, 8, LANES), "member", 0, 0, tiled=True
    )
    sampled = pl.pallas_call(
        sample_kernel,
        in_specs=[VM, VM, VM],
        out_specs=VM,
        out_shape=jax.ShapeDtypeStruct((9, PACK, LANES), F32),
        compiler_params=LIMIT,
        name="sample",
    )(packed, own, const(row_sample(), BF16))
    ends = lax.axis_size("tile") - 1
    up = lax.ppermute(sampled, "tile", [(i, i + 1) for i in range(ends)])
    down = lax.ppermute(sampled, "tile", [(i + 1, i) for i in range(ends)])
    weights = pl.pallas_call(
        solve_kernel,
        in_specs=[VM, VM, VM, VM],
        out_specs=VM,
        out_shape=jax.ShapeDtypeStruct((24, 48, LANES), F32),
        scratch_shapes=[
            pltpu.VMEM((64 * PACK, LANES), F32),
            pltpu.VMEM((25, 48, LANES), F32),
            pltpu.VMEM((8, 48, LANES), F32),
            pltpu.VMEM((8, 48, LANES), F32),
        ],
        compiler_params=LIMIT,
        name="solve",
    )(up, sampled, down, const(taper_rows(), F32))
    result = pl.pallas_call(
        transform_kernel,
        in_specs=[VM, VM, VM],
        out_specs=VM,
        out_shape=jax.ShapeDtypeStruct((MEMBERS, UPPER, 8, LANES), BF16),
        scratch_shapes=[
            pltpu.VMEM((24 * 48, 512), F32),
            pltpu.VMEM((MEMBERS, UPPER, 8, LANES), F32),
        ],
        compiler_params=LIMIT,
        name="transform",
    )(weights, fields, const(expand_rows(), BF16))
    result = lax.all_to_all(result, "member", 0, 0, tiled=True)
    return pl.pallas_call(
        finish_kernel,
        in_specs=[VM, ANY],
        out_specs=ANY,
        out_shape=jax.ShapeDtypeStruct(prior.shape, BF16),
        scratch_shapes=[
            pltpu.VMEM((3, UPPER, 8, 2048), BF16),
            pltpu.SemaphoreType.DMA((3,)),
        ],
        input_output_aliases={1: 0},
        compiler_params=LIMIT,
        name="finish",
    )(result.reshape(DOMS, 3, UPPER, 8, LANES), partial)


def solution(mesh):
    return jax.shard_map(
        body,
        mesh=mesh,
        in_specs=(
            P("member", None, "tile", None),
            P("tile", "member", None),
            P("tile", "member", None),
            P("tile", "member", None),
            P("tile", "member"),
        ),
        out_specs=P("member", None, "tile", None),
        check_vma=False,
    )
```

```python
import functools
import math

import jax
import jax.numpy as jnp
import numpy as np
from jax import lax
from jax.experimental import pallas as pl
from jax.experimental.pallas import tpu as pltpu
from jax.sharding import PartitionSpec as P

MEMBERS = 48
UPPER = 8
LANES = 128
SLOTS = 256
RADIUS = 8
BLOCK = 4
CHUNK = 16
GROUPS = LANES // CHUNK
BLOCKS_Y = LANES // BLOCK
ROWS = 64
PACK = 56
DOMS = 16
F32 = jnp.float32
BF16 = jnp.bfloat16


def split3(x):
    hi = x.astype(BF16)
    rest = x - hi.astype(F32)
    mid = rest.astype(BF16)
    low = (rest - mid.astype(F32)).astype(BF16)
    return hi, mid, low


def split2(x):
    hi = x.astype(BF16)
    return hi, (x - hi.astype(F32)).astype(BF16)


def nt(a, b):
    return lax.dot_general(a, b, (((1,), (1,)), ((), ())), preferred_element_type=F32)


def nn(a, b):
    return lax.dot_general(a, b, (((1,), (0,)), ((), ())), preferred_element_type=F32)


def row_spread():
    m = np.zeros((64, 48), np.float32)
    for x in range(8):
        for r in range(6):
            m[x * 8 + r, r * 8 + x] = 1.0
    return m


def row_compact():
    m = np.zeros((ROWS, 80), np.float32)
    for v in range(9):
        for r in range(6):
            m[v * 6 + r, v * 8 + r] = 1.0
    for r in range(6):
        m[54 + r, 72 + r] = 1.0
    return m


def row_sample():
    m = np.zeros((9 * PACK, DOMS * ROWS), np.float32)
    for v in range(9):
        for i in range(MEMBERS):
            for layer in range(2):
                m[v * PACK + i, (i // 3) * ROWS + v * 6 + (i % 3) * 2 + layer] = 0.5
    for s in range(DOMS):
        for r in range(3):
            m[8 * PACK + 48, s * ROWS + 54 + r] = 1.0
            m[8 * PACK + 49, s * ROWS + 57 + r] = 1.0
    return m


OFFSETS = (10, 14, 2, 6)


def taper_rows():
    lane = np.arange(LANES)
    x, y = lane // CHUNK, lane % CHUNK
    t = np.zeros((24, LANES), np.float32)
    for k, o in enumerate(OFFSETS):
        gap_y = np.where(y >= o, y - o, y - o + CHUNK) - 6 - 1.5
        for seg in range(3):
            for p in range(2):
                gap_x = (seg - 1) * 8 + x - (4 * p + 1.5)
                s = gap_x * gap_x + gap_y * gap_y
                t[(k * 3 + seg) * 2 + p] = np.where(s < RADIUS * RADIUS, (1 - s / 64.0) ** 2, 0.0)
    return t


def expand_rows():
    m = np.zeros((128, 512), np.float32)
    for h in range(2):
        for p in range(2):
            for y in range(128):
                m[p * 64 + h * 32 + y // 4, h * 256 + p * 128 + y] = 1.0
    return np.concatenate([m, m], 0)


def pack_kernel(where, tally, x_ref, reading, error, cell, spread, compact, out, own, work):
    me = where[0]
    live = lax.broadcasted_iota(jnp.int32, (1, SLOTS), 1) < tally[0]
    prec = jnp.where(live, 1.0 / error[...], 0.0)
    vals = jnp.where(live, prec * reading[...], 0.0)
    c = cell[...]
    x, y = c // LANES, c % LANES
    group = y // CHUNK
    lane = x * CHUNK + y % CHUNK
    hit = lax.broadcasted_iota(jnp.int32, (8, SLOTS), 0) == group
    spot = (lax.broadcasted_iota(jnp.int32, (LANES, SLOTS), 0) == lane).astype(F32).astype(BF16)
    pv = jnp.concatenate([jnp.where(hit, prec, 0.0), jnp.where(hit, vals, 0.0)], 0)
    a, b, d = split3(pv)
    pv = nt(a, spot) + nt(b, spot) + nt(d, spot)
    own[...] = pv
    sub = lax.broadcasted_iota(jnp.int32, (8, LANES), 0)
    col = lax.broadcasted_iota(jnp.int32, (8, LANES), 1)
    high = (col % CHUNK) >= 8

    def edge(g):
        res = jnp.zeros((8, LANES), F32)
        for n in range(2):
            parts = split3(jnp.broadcast_to(pv[n * 8 + g : n * 8 + g + 1, :], (8, LANES)))
            for k in range(3):
                res = jnp.where(sub == n * 3 + k, parts[k].astype(F32), res)
        return res

    last = jnp.where(high, edge(7), 0.0)
    first = jnp.where(high, 0.0, edge(0))

    flat = x_ref[...].reshape(48, 16 * LANES)
    rows = nn(spread[...], flat)
    for d in range(DOMS):
        v = [rows[8 * k : 8 * k + 8, d * LANES : (d + 1) * LANES] for k in range(8)]
        for step in (4, 2, 1):
            width = step * CHUNK
            low = ((col // width) % 2) == 0
            new = list(v)
            for k in range(8):
                if not k & step:
                    a, b = v[k], v[k + step]
                    new[k] = jnp.where(low, a, pltpu.roll(b, width, 1))
                    new[k + step] = jnp.where(low, pltpu.roll(a, LANES - width, 1), b)
            v = new
        for k in range(8):
            work[d, 8 * k : 8 * k + 8, :] = v[k]
    for d in range(DOMS):
        left = work[(d - 1) % DOMS, 56:64, :]
        right = work[(d + 1) % DOMS, 0:8, :]
        work[d, 64:72, :] = jnp.where(high, left, right)
        work[d, 72:80, :] = jnp.where(
            me == d - 1, last, jnp.where(me == d + 1, first, jnp.zeros_like(first))
        )
    for d in range(DOMS):
        out[d] = nn(compact[...], work[d].astype(BF16)).astype(BF16)


def sample_kernel(r_ref, own, choose, out):
    pv = own[...]
    res = nn(choose[...], r_ref[...].reshape(DOMS * ROWS, LANES))
    for v in range(9):
        s = res[v * PACK : v * PACK + MEMBERS]
        mean = jnp.sum(s, axis=0, keepdims=True) * (1.0 / MEMBERS)
        if v < 8:
            prec, vals = pv[v : v + 1], pv[8 + v : 9 + v]
        else:
            prec, vals = res[v * PACK + 48 : v * PACK + 49], res[v * PACK + 49 : v * PACK + 50]
        out[v, 0:48, :] = s - mean
        sub = lax.broadcasted_iota(jnp.int32, (8, LANES), 0)
        out[v, 48:56, :] = jnp.where(
            sub == 0, prec, jnp.where(sub == 1, vals - prec * mean, 0.0)
        )


def solve_kernel(up, own, down, taper, out, grams, mat, piv, fac):
    segs = (up, own, down)
    lane = lax.broadcasted_iota(jnp.int32, (1, LANES), 1) % CHUNK
    first = lax.broadcasted_iota(jnp.int32, (16, LANES), 0) == 0
    for g in range(GROUPS):
        for k, o in enumerate(OFFSETS):
            v0 = g - 1 if k < 2 else g
            v1 = v0 + 1
            v0, v1 = (8 if v in (-1, 8) else v for v in (v0, v1))
            mask = lane >= o
            shi, slo, whi, wlo = [], [], [], []
            for s in range(3):
                w = jnp.where(mask, segs[s][v0], segs[s][v1])
                a = w[0:48]
                prec, drv = w[48:49], w[49:50]
                row = (k * 3 + s) * 2
                stream = jnp.concatenate([a * prec, jnp.where(first, drv, 0.0)], 0)
                h, l = split2(stream)
                shi.append(h)
                slo.append(l)
                h, l = split2(
                    jnp.concatenate([a * taper[row : row + 1, :], a * taper[row + 1 : row + 2, :]], 0)
                )
                whi.append(h)
                wlo.append(l)
            stream = jnp.concatenate(
                [jnp.concatenate(shi + shi, 1), jnp.concatenate(slo + slo, 1)], 0
            )
            res = nt(stream, jnp.concatenate(whi + wlo, 1))
            res = res[0:56] + res[64:120]
            res = jnp.concatenate([res, jnp.zeros((56, LANES - 2 * MEMBERS), F32)], 1)
            q = g * 4 + k
            grams[q * PACK : (q + 1) * PACK, :] = res

    sub = lax.broadcasted_iota(jnp.int32, (8, LANES), 0)
    half = (lax.broadcasted_iota(jnp.int32, (8, LANES), 1) // 32) % 2
    half0 = half == 0
    low = lax.broadcasted_iota(jnp.int32, (48, LANES), 1) < 64

    def columns(js):
        t = jnp.concatenate([grams[pl.ds(j, 32, stride=PACK), :] for j in js], 0).T
        return t[0:48], t[48:96]

    for j in range(12):
        t0, t1 = columns(range(4 * j, 4 * j + 4))
        mat[2 * j] = jnp.where(low, t0, pltpu.roll(t1, 64, 1))
        mat[2 * j + 1] = jnp.where(low, pltpu.roll(t0, 64, 1), t1)
    t0, t1 = columns([48] * 4)
    drive = jnp.where(low, t0, t1)
    drive = [drive[8 * j : 8 * j + 8] for j in range(6)]

    def bcast(x, k):
        return jnp.broadcast_to(x[k : k + 1, :], (8, LANES))

    def both(x, h):
        return jnp.where(half == h, x, pltpu.roll(x, 32 if h == 0 else 96, 1))

    scale = []
    for panel in range(6):
        buf = panel % 2
        others = [j for j in range(6) if j != panel]
        rows = [
            [mat[4 * panel + n, 8 * j : 8 * j + 8, :] for j in range(6)] for n in range(4)
        ]
        d = [both(rows[r // 2][panel], r % 2) for r in range(8)]
        d = [jnp.where(sub == r, d[r] + (MEMBERS - 1.0), d[r]) for r in range(8)]
        invs, fds = [], []
        for k in range(8):
            inv = 1.0 / bcast(d[k], k)
            invs.append(inv)
            scale.append(jnp.sqrt((MEMBERS - 1.0) * inv[0:1, :]))
            here = sub == k
            row = jnp.where(here, 1.0, d[k])
            for r in range(k + 1, 8):
                d[r] = jnp.where(here, 0.0, d[r]) - (bcast(d[k], r) * inv) * row
            fd = bcast(drive[panel], k) * inv
            fds.append(fd)
            drive[panel] = jnp.where(here, 0.0, drive[panel]) - fd * row
            d[k] = jnp.where(sub <= k, row, 0.0)
            piv[buf, k, 8 * panel : 8 * panel + 8, :] = d[k]
        for n in range(4):
            mat[4 * panel + n, 8 * panel : 8 * panel + 8, :] = jnp.where(
                half0, d[2 * n], d[2 * n + 1]
            )
        eb = [[bcast(d[r], c) for c in range(r)] for r in range(8)]
        for j in others:
            x = [both(rows[r // 2][j], r % 2) for r in range(8)]
            y = []
            for r in range(8):
                t = x[r]
                for c in range(r):
                    t = t + eb[r][c] * x[c]
                y.append(t)
                piv[buf, r, 8 * j : 8 * j + 8, :] = t
                if j > panel:
                    fac[buf, r, 8 * j : 8 * j + 8, :] = t * invs[r]
                drive[j] = drive[j] - fds[r] * t
            if j < panel:
                for n in range(4):
                    mat[4 * panel + n, 8 * j : 8 * j + 8, :] = jnp.where(
                        half0, y[2 * n], y[2 * n + 1]
                    )
        for block in range(panel + 1, 6):
            js = list(range(panel + 1)) + list(range(block, 6))
            acc = [
                {
                    j: jnp.zeros((8, LANES), F32)
                    if j == panel
                    else mat[4 * block + n, 8 * j : 8 * j + 8, :]
                    for j in js
                }
                for n in range(4)
            ]
            for k in range(8):
                pr = {j: piv[buf, k, 8 * j : 8 * j + 8, :] for j in js}
                for n in range(4):
                    i = 8 * block + 2 * n
                    fa = jnp.broadcast_to(fac[buf, k, i : i + 1, :], (8, LANES))
                    fb = jnp.broadcast_to(fac[buf, k, i + 1 : i + 2, :], (8, LANES))
                    fp = jnp.where(half0, fa, fb)
                    for j in js:
                        acc[n][j] = acc[n][j] - fp * pr[j]
            for n in range(4):
                for j in js:
                    mat[4 * block + n, 8 * j : 8 * j + 8, :] = acc[n][j]

    for t in range(24):
        panel = t // 4
        sc = jnp.where(half0, scale[2 * t], scale[2 * t + 1])
        w = []
        for j in range(6):
            x = -drive[j]
            if j <= panel:
                x = x + sc * mat[t, 8 * j : 8 * j + 8, :]
            w.append(x)
        total = jnp.sum(w[0] + w[1] + w[2] + w[3] + w[4] + w[5], axis=0, keepdims=True)
        fix = (1.0 - total) * (1.0 / MEMBERS)
        for j in range(6):
            out[t, 8 * j : 8 * j + 8, :] = w[j] + fix


def transform_kernel(w_ref, x_ref, expand, out, wide, xs):
    w = w_ref[...].reshape(24 * 48, LANES)
    hi, low = split2(w)
    wide[...] = nn(jnp.concatenate([hi, low], 1), expand[...])

    def widen(i, c):
        for l in range(8):
            xs[i, l] = x_ref[i, l].astype(F32)
        return c

    lax.fori_loop(0, MEMBERS, widen, 0)
    top = lax.broadcasted_iota(jnp.int32, (8, LANES), 0) < 4

    def pair(t, c):
        def step(i, acc):
            acc = list(acc)
            for u in range(16):
                r = t * 48 + i * 16 + u
                line = wide[pl.ds(r, 1), :]
                ws = []
                for h in range(2):
                    a = jnp.broadcast_to(line[:, h * 256 : h * 256 + 128], (8, LANES))
                    b = jnp.broadcast_to(line[:, h * 256 + 128 : h * 256 + 256], (8, LANES))
                    ws.append(jnp.where(top, a, b))
                for l in range(8):
                    x = xs[i * 16 + u, l]
                    acc[l] = acc[l] + x * ws[0]
                    acc[8 + l] = acc[8 + l] + x * ws[1]
            return tuple(acc)

        acc = lax.fori_loop(0, 3, step, tuple(jnp.zeros((8, LANES), F32) for _ in range(16)))
        for h in range(2):
            for l in range(8):
                out[2 * t + h, l] = acc[8 * h + l].astype(BF16)
        return c

    lax.fori_loop(0, 24, pair, 0)


def send_kernel(x_ref, out):
    for d in range(DOMS):
        for m in range(3):
            out[d, m] = x_ref[m, :, :, d * LANES : (d + 1) * LANES]


def lower_kernel(x_ref, out):
    out[...] = x_ref[...]


def finish_kernel(b_ref, partial, out, work, sems):
    del partial
    copies = []
    for m in range(3):
        for d in range(DOMS):
            work[m, :, :, d * LANES : (d + 1) * LANES] = b_ref[d, m]
        copy = pltpu.make_async_copy(work.at[m], out.at[m, 0:UPPER], sems.at[m])
        copy.start()
        copies.append(copy)
    for copy in copies:
        copy.wait()


VM = pl.BlockSpec(memory_space=pltpu.VMEM)
SM = pl.BlockSpec(memory_space=pltpu.SMEM)
ANY = pl.BlockSpec(memory_space=pl.ANY)
FULL = pltpu.CompilerParams(vmem_limit_bytes=62000000)
LIMIT = pltpu.CompilerParams(vmem_limit_bytes=48 * 2**20)


def body(prior, reading, error, cell, tally):
    me = lax.axis_index("member").astype(jnp.int32).reshape(1)
    const = lambda a, t: jnp.asarray(a, t)
    whole = lambda *shape: pl.BlockSpec(shape, lambda g: (0,) * len(shape))
    packed, own = pl.pallas_call(
        pack_kernel,
        grid=(1,),
        in_specs=[
            SM,
            SM,
            whole(3, 2, 8, 2048),
            whole(1, SLOTS),
            whole(1, SLOTS),
            whole(1, SLOTS),
            whole(64, 48),
            whole(ROWS, 80),
        ],
        out_specs=[VM, VM],
        out_shape=[
            jax.ShapeDtypeStruct((DOMS, ROWS, LANES), BF16),
            jax.ShapeDtypeStruct((16, LANES), F32),
        ],
        scratch_shapes=[pltpu.VMEM((DOMS, 80, LANES), F32)],
        compiler_params=FULL,
        name="pack",
    )(
        me,
        tally.reshape(1),
        prior,
        reading.reshape(1, SLOTS),
        error.reshape(1, SLOTS),
        cell.reshape(1, SLOTS),
        const(row_spread(), BF16),
        const(row_compact(), BF16),
    )
    fields = pl.pallas_call(
        send_kernel,
        grid=(1,),
        in_specs=[whole(3, UPPER, 8, 2048)],
        out_specs=VM,
        out_shape=jax.ShapeDtypeStruct((DOMS, 3, UPPER, 8, LANES), BF16),
        compiler_params=FULL,
        name="send",
    )(prior)
    lower = pl.BlockSpec((1, UPPER, 8, 2048), lambda g: (g, 1, 0, 0))
    partial = pl.pallas_call(
        lower_kernel,
        grid=(3,),
        in_specs=[lower],
        out_specs=lower,
        out_shape=jax.ShapeDtypeStruct(prior.shape, BF16),
        compiler_params=FULL,
        name="lower",
    )(prior)
    packed = lax.all_to_all(packed, "member", 0, 0, tiled=True)
    fields = lax.all_to_all(
        fields.reshape(MEMBERS, UPPER, 8, LANES), "member", 0, 0, tiled=True
    )
    sampled = pl.pallas_call(
        sample_kernel,
        in_specs=[VM, VM, VM],
        out_specs=VM,
        out_shape=jax.ShapeDtypeStruct((9, PACK, LANES), F32),
        compiler_params=LIMIT,
        name="sample",
    )(packed, own, const(row_sample(), BF16))
    ends = lax.axis_size("tile") - 1
    up = lax.ppermute(sampled, "tile", [(i, i + 1) for i in range(ends)])
    down = lax.ppermute(sampled, "tile", [(i + 1, i) for i in range(ends)])
    weights = pl.pallas_call(
        solve_kernel,
        in_specs=[VM, VM, VM, VM],
        out_specs=VM,
        out_shape=jax.ShapeDtypeStruct((24, 48, LANES), F32),
        scratch_shapes=[
            pltpu.VMEM((BLOCKS_Y * PACK, LANES), F32),
            pltpu.VMEM((24, 48, LANES), F32),
            pltpu.VMEM((2, 8, 48, LANES), F32),
            pltpu.VMEM((2, 8, 48, LANES), F32),
        ],
        compiler_params=LIMIT,
        name="solve",
    )(up, sampled, down, const(taper_rows(), F32))
    result = pl.pallas_call(
        transform_kernel,
        in_specs=[VM, VM, VM],
        out_specs=VM,
        out_shape=jax.ShapeDtypeStruct((MEMBERS, UPPER, 8, LANES), BF16),
        scratch_shapes=[
            pltpu.VMEM((24 * 48, 512), F32),
            pltpu.VMEM((MEMBERS, UPPER, 8, LANES), F32),
        ],
        compiler_params=LIMIT,
        name="transform",
    )(weights, fields, const(expand_rows(), BF16))
    result = lax.all_to_all(result, "member", 0, 0, tiled=True)
    return pl.pallas_call(
        finish_kernel,
        in_specs=[VM, ANY],
        out_specs=ANY,
        out_shape=jax.ShapeDtypeStruct(prior.shape, BF16),
        scratch_shapes=[
            pltpu.VMEM((3, UPPER, 8, 2048), BF16),
            pltpu.SemaphoreType.DMA((3,)),
        ],
        input_output_aliases={1: 0},
        compiler_params=LIMIT,
        name="finish",
    )(result.reshape(DOMS, 3, UPPER, 8, LANES), partial)


def solution(mesh):
    return jax.shard_map(
        body,
        mesh=mesh,
        in_specs=(
            P("member", None, "tile", None),
            P("tile", "member", None),
            P("tile", "member", None),
            P("tile", "member", None),
            P("tile", "member"),
        ),
        out_specs=P("member", None, "tile", None),
        check_vma=False,
    )
```

```python
import functools
import math

import jax
import jax.numpy as jnp
import numpy as np
from jax import lax
from jax.experimental import pallas as pl
from jax.experimental.pallas import tpu as pltpu
from jax.sharding import PartitionSpec as P

MEMBERS = 48
UPPER = 8
LANES = 128
SLOTS = 256
RADIUS = 8
BLOCK = 4
CHUNK = 16
GROUPS = LANES // CHUNK
BLOCKS_Y = LANES // BLOCK
ROWS = 64
PACK = 56
DOMS = 16
F32 = jnp.float32
BF16 = jnp.bfloat16


def split3(x):
    hi = x.astype(BF16)
    rest = x - hi.astype(F32)
    mid = rest.astype(BF16)
    low = (rest - mid.astype(F32)).astype(BF16)
    return hi, mid, low


def split2(x):
    hi = x.astype(BF16)
    return hi, (x - hi.astype(F32)).astype(BF16)


def nt(a, b):
    return lax.dot_general(a, b, (((1,), (1,)), ((), ())), preferred_element_type=F32)


def nn(a, b):
    return lax.dot_general(a, b, (((1,), (0,)), ((), ())), preferred_element_type=F32)


def row_spread():
    m = np.zeros((64, 48), np.float32)
    for x in range(8):
        for r in range(6):
            m[x * 8 + r, r * 8 + x] = 1.0
    return m


def row_compact():
    m = np.zeros((ROWS, 80), np.float32)
    for v in range(9):
        for r in range(6):
            m[v * 6 + r, v * 8 + r] = 1.0
    for r in range(6):
        m[54 + r, 72 + r] = 1.0
    return m


def row_sample():
    m = np.zeros((9 * PACK, DOMS * ROWS), np.float32)
    for v in range(9):
        for i in range(MEMBERS):
            for layer in range(2):
                m[v * PACK + i, (i // 3) * ROWS + v * 6 + (i % 3) * 2 + layer] = 0.5
    for s in range(DOMS):
        for r in range(3):
            m[8 * PACK + 48, s * ROWS + 54 + r] = 1.0
            m[8 * PACK + 49, s * ROWS + 57 + r] = 1.0
    return m


OFFSETS = (10, 14, 2, 6)


def taper_rows():
    lane = np.arange(LANES)
    x, y = lane // CHUNK, lane % CHUNK
    t = np.zeros((24, LANES), np.float32)
    for k, o in enumerate(OFFSETS):
        gap_y = np.where(y >= o, y - o, y - o + CHUNK) - 6 - 1.5
        for seg in range(3):
            for p in range(2):
                gap_x = (seg - 1) * 8 + x - (4 * p + 1.5)
                s = gap_x * gap_x + gap_y * gap_y
                t[(k * 3 + seg) * 2 + p] = np.where(s < RADIUS * RADIUS, (1 - s / 64.0) ** 2, 0.0)
    return t


def expand_rows():
    m = np.zeros((128, 512), np.float32)
    for h in range(2):
        for p in range(2):
            for y in range(128):
                m[p * 64 + h * 32 + y // 4, h * 256 + p * 128 + y] = 1.0
    return np.concatenate([m, m], 0)


def pack_kernel(where, tally, x_ref, reading, error, cell, spread, compact, out, own, work):
    me = where[0]
    live = lax.broadcasted_iota(jnp.int32, (1, SLOTS), 1) < tally[0]
    prec = jnp.where(live, 1.0 / error[...], 0.0)
    vals = jnp.where(live, prec * reading[...], 0.0)
    c = cell[...]
    x, y = c // LANES, c % LANES
    group = y // CHUNK
    lane = x * CHUNK + y % CHUNK
    hit = lax.broadcasted_iota(jnp.int32, (8, SLOTS), 0) == group
    spot = (lax.broadcasted_iota(jnp.int32, (LANES, SLOTS), 0) == lane).astype(F32).astype(BF16)
    pv = jnp.concatenate([jnp.where(hit, prec, 0.0), jnp.where(hit, vals, 0.0)], 0)
    a, b, d = split3(pv)
    pv = nt(a, spot) + nt(b, spot) + nt(d, spot)
    own[...] = pv
    sub = lax.broadcasted_iota(jnp.int32, (8, LANES), 0)
    col = lax.broadcasted_iota(jnp.int32, (8, LANES), 1)
    high = (col % CHUNK) >= 8

    def edge(g):
        res = jnp.zeros((8, LANES), F32)
        for n in range(2):
            parts = split3(jnp.broadcast_to(pv[n * 8 + g : n * 8 + g + 1, :], (8, LANES)))
            for k in range(3):
                res = jnp.where(sub == n * 3 + k, parts[k].astype(F32), res)
        return res

    last = jnp.where(high, edge(7), 0.0)
    first = jnp.where(high, 0.0, edge(0))

    flat = x_ref[...].reshape(48, 16 * LANES)
    rows = nn(spread[...], flat)
    for d in range(DOMS):
        v = [rows[8 * k : 8 * k + 8, d * LANES : (d + 1) * LANES] for k in range(8)]
        for step in (4, 2, 1):
            width = step * CHUNK
            low = ((col // width) % 2) == 0
            new = list(v)
            for k in range(8):
                if not k & step:
                    a, b = v[k], v[k + step]
                    new[k] = jnp.where(low, a, pltpu.roll(b, width, 1))
                    new[k + step] = jnp.where(low, pltpu.roll(a, LANES - width, 1), b)
            v = new
        for k in range(8):
            work[d, 8 * k : 8 * k + 8, :] = v[k]
    for d in range(DOMS):
        left = work[(d - 1) % DOMS, 56:64, :]
        right = work[(d + 1) % DOMS, 0:8, :]
        work[d, 64:72, :] = jnp.where(high, left, right)
        work[d, 72:80, :] = jnp.where(
            me == d - 1, last, jnp.where(me == d + 1, first, jnp.zeros_like(first))
        )
    for d in range(DOMS):
        out[d] = nn(compact[...], work[d].astype(BF16)).astype(BF16)


def sample_kernel(r_ref, own, choose, out):
    pv = own[...]
    res = nn(choose[...], r_ref[...].reshape(DOMS * ROWS, LANES))
    for v in range(9):
        s = res[v * PACK : v * PACK + MEMBERS]
        mean = jnp.sum(s, axis=0, keepdims=True) * (1.0 / MEMBERS)
        if v < 8:
            prec, vals = pv[v : v + 1], pv[8 + v : 9 + v]
        else:
            prec, vals = res[v * PACK + 48 : v * PACK + 49], res[v * PACK + 49 : v * PACK + 50]
        out[v, 0:48, :] = s - mean
        sub = lax.broadcasted_iota(jnp.int32, (8, LANES), 0)
        out[v, 48:56, :] = jnp.where(
            sub == 0, prec, jnp.where(sub == 1, vals - prec * mean, 0.0)
        )


def solve_kernel(up, own, down, taper, out, grams, mat, piv, fac):
    segs = (up, own, down)
    lane = lax.broadcasted_iota(jnp.int32, (1, LANES), 1) % CHUNK
    first = lax.broadcasted_iota(jnp.int32, (16, LANES), 0) == 0
    for g in range(GROUPS):
        for k, o in enumerate(OFFSETS):
            v0 = g - 1 if k < 2 else g
            v1 = v0 + 1
            v0, v1 = (8 if v in (-1, 8) else v for v in (v0, v1))
            mask = lane >= o
            shi, slo, whi, wlo = [], [], [], []
            for s in range(3):
                w = jnp.where(mask, segs[s][v0], segs[s][v1])
                a = w[0:48]
                prec, drv = w[48:49], w[49:50]
                row = (k * 3 + s) * 2
                stream = jnp.concatenate([a * prec, jnp.where(first, drv, 0.0)], 0)
                h, l = split2(stream)
                shi.append(h)
                slo.append(l)
                h, l = split2(
                    jnp.concatenate([a * taper[row : row + 1, :], a * taper[row + 1 : row + 2, :]], 0)
                )
                whi.append(h)
                wlo.append(l)
            stream = jnp.concatenate(
                [jnp.concatenate(shi + shi, 1), jnp.concatenate(slo + slo, 1)], 0
            )
            res = nt(stream, jnp.concatenate(whi + wlo, 1))
            res = res[0:56] + res[64:120]
            res = jnp.concatenate([res, jnp.zeros((56, LANES - 2 * MEMBERS), F32)], 1)
            q = g * 4 + k
            grams[q * PACK : (q + 1) * PACK, :] = res

    sub = lax.broadcasted_iota(jnp.int32, (8, LANES), 0)
    half = (lax.broadcasted_iota(jnp.int32, (8, LANES), 1) // 32) % 2
    half0 = half == 0
    low = lax.broadcasted_iota(jnp.int32, (48, LANES), 1) < 64

    def columns(js):
        t = jnp.concatenate([grams[pl.ds(j, 32, stride=PACK), :] for j in js], 0).T
        return t[0:48], t[48:96]

    for j in range(12):
        t0, t1 = columns(range(4 * j, 4 * j + 4))
        mat[2 * j] = jnp.where(low, t0, pltpu.roll(t1, 64, 1))
        mat[2 * j + 1] = jnp.where(low, pltpu.roll(t0, 64, 1), t1)
    t0, t1 = columns([48] * 4)
    drive = jnp.where(low, t0, t1)
    drive = [drive[8 * j : 8 * j + 8] for j in range(6)]

    def bcast(x, k):
        return jnp.broadcast_to(x[k : k + 1, :], (8, LANES))

    def both(x, h):
        return jnp.where(half == h, x, pltpu.roll(x, 32 if h == 0 else 96, 1))

    scale = []
    for panel in range(6):
        buf = panel % 2
        others = [j for j in range(6) if j != panel]
        rows = [
            [mat[4 * panel + n, 8 * j : 8 * j + 8, :] for j in range(6)] for n in range(4)
        ]
        d = [both(rows[r // 2][panel], r % 2) for r in range(8)]
        d = [jnp.where(sub == r, d[r] + (MEMBERS - 1.0), d[r]) for r in range(8)]
        invs, fds = [], []
        for k in range(8):
            inv = 1.0 / bcast(d[k], k)
            invs.append(inv)
            scale.append(jnp.sqrt((MEMBERS - 1.0) * inv[0:1, :]))
            here = sub == k
            row = jnp.where(here, 1.0, d[k])
            for r in range(k + 1, 8):
                d[r] = jnp.where(here, 0.0, d[r]) - (bcast(d[k], r) * inv) * row
            fd = bcast(drive[panel], k) * inv
            fds.append(fd)
            drive[panel] = jnp.where(here, 0.0, drive[panel]) - fd * row
            d[k] = jnp.where(sub <= k, row, 0.0)
            piv[buf, k, 8 * panel : 8 * panel + 8, :] = d[k]
        for n in range(4):
            mat[4 * panel + n, 8 * panel : 8 * panel + 8, :] = jnp.where(
                half0, d[2 * n], d[2 * n + 1]
            )
        eb = [[bcast(d[r], c) for c in range(r)] for r in range(8)]
        for j in others:
            x = [both(rows[r // 2][j], r % 2) for r in range(8)]
            y = []
            for r in range(8):
                t = x[r]
                for c in range(r):
                    t = t + eb[r][c] * x[c]
                y.append(t)
                piv[buf, r, 8 * j : 8 * j + 8, :] = t
                if j > panel:
                    fac[buf, r, 8 * j : 8 * j + 8, :] = t * invs[r]
                drive[j] = drive[j] - fds[r] * t
            if j < panel:
                for n in range(4):
                    mat[4 * panel + n, 8 * j : 8 * j + 8, :] = jnp.where(
                        half0, y[2 * n], y[2 * n + 1]
                    )
        for block in range(panel + 1, 6):
            js = list(range(panel + 1)) + list(range(block, 6))
            acc = [
                {
                    j: jnp.zeros((8, LANES), F32)
                    if j == panel
                    else mat[4 * block + n, 8 * j : 8 * j + 8, :]
                    for j in js
                }
                for n in range(4)
            ]
            for k in range(8):
                pr = {j: piv[buf, k, 8 * j : 8 * j + 8, :] for j in js}
                for n in range(4):
                    i = 8 * block + 2 * n
                    fa = jnp.broadcast_to(fac[buf, k, i : i + 1, :], (8, LANES))
                    fb = jnp.broadcast_to(fac[buf, k, i + 1 : i + 2, :], (8, LANES))
                    fp = jnp.where(half0, fa, fb)
                    for j in js:
                        acc[n][j] = acc[n][j] - fp * pr[j]
            for n in range(4):
                for j in js:
                    mat[4 * block + n, 8 * j : 8 * j + 8, :] = acc[n][j]

    for t in range(24):
        panel = t // 4
        sc = jnp.where(half0, scale[2 * t], scale[2 * t + 1])
        w = []
        for j in range(6):
            x = -drive[j]
            if j <= panel:
                x = x + sc * mat[t, 8 * j : 8 * j + 8, :]
            w.append(x)
        total = jnp.sum(w[0] + w[1] + w[2] + w[3] + w[4] + w[5], axis=0, keepdims=True)
        fix = (1.0 - total) * (1.0 / MEMBERS)
        for j in range(6):
            out[t, 8 * j : 8 * j + 8, :] = w[j] + fix


def transform_kernel(w_ref, x_ref, expand, out, wide, xs):
    w = w_ref[...].reshape(24 * 48, LANES)
    hi, low = split2(w)
    wide[...] = nn(jnp.concatenate([hi, low], 1), expand[...])

    for i in range(MEMBERS):
        for l in range(8):
            xs[i, l] = x_ref[i, l].astype(F32)
    top = lax.broadcasted_iota(jnp.int32, (8, LANES), 0) < 4

    def pair(t, c):
        def step(i, acc):
            acc = list(acc)
            for u in range(16):
                r = t * 48 + i * 16 + u
                line = wide[pl.ds(r, 1), :]
                ws = []
                for h in range(2):
                    a = jnp.broadcast_to(line[:, h * 256 : h * 256 + 128], (8, LANES))
                    b = jnp.broadcast_to(line[:, h * 256 + 128 : h * 256 + 256], (8, LANES))
                    ws.append(jnp.where(top, a, b))
                for l in range(8):
                    x = xs[i * 16 + u, l]
                    acc[l] = acc[l] + x * ws[0]
                    acc[8 + l] = acc[8 + l] + x * ws[1]
            return tuple(acc)

        acc = lax.fori_loop(0, 3, step, tuple(jnp.zeros((8, LANES), F32) for _ in range(16)))
        for h in range(2):
            for l in range(8):
                out[2 * t + h, l] = acc[8 * h + l].astype(BF16)
        return c

    lax.fori_loop(0, 24, pair, 0)


def send_kernel(x_ref, out, lower):
    for d in range(DOMS):
        out[d, 0] = x_ref[0, 0:UPPER, :, d * LANES : (d + 1) * LANES]
    lower[...] = x_ref[:, UPPER : 2 * UPPER]


def finish_kernel(b_ref, partial, out, work, sems):
    del partial
    copies = []
    for m in range(3):
        for d in range(DOMS):
            work[m, :, :, d * LANES : (d + 1) * LANES] = b_ref[d, m]
        copy = pltpu.make_async_copy(work.at[m], out.at[m, 0:UPPER], sems.at[m])
        copy.start()
        copies.append(copy)
    for copy in copies:
        copy.wait()


VM = pl.BlockSpec(memory_space=pltpu.VMEM)
SM = pl.BlockSpec(memory_space=pltpu.SMEM)
ANY = pl.BlockSpec(memory_space=pl.ANY)
FULL = pltpu.CompilerParams(vmem_limit_bytes=62000000)
LIMIT = pltpu.CompilerParams(vmem_limit_bytes=48 * 2**20)


def body(prior, reading, error, cell, tally):
    me = lax.axis_index("member").astype(jnp.int32).reshape(1)
    const = lambda a, t: jnp.asarray(a, t)
    whole = lambda *shape: pl.BlockSpec(shape, lambda g: (0,) * len(shape))
    packed, own = pl.pallas_call(
        pack_kernel,
        grid=(1,),
        in_specs=[
            SM,
            SM,
            whole(3, 2, 8, 2048),
            whole(1, SLOTS),
            whole(1, SLOTS),
            whole(1, SLOTS),
            whole(64, 48),
            whole(ROWS, 80),
        ],
        out_specs=[VM, VM],
        out_shape=[
            jax.ShapeDtypeStruct((DOMS, ROWS, LANES), BF16),
            jax.ShapeDtypeStruct((16, LANES), F32),
        ],
        scratch_shapes=[pltpu.VMEM((DOMS, 80, LANES), F32)],
        compiler_params=FULL,
        name="pack",
    )(
        me,
        tally.reshape(1),
        prior,
        reading.reshape(1, SLOTS),
        error.reshape(1, SLOTS),
        cell.reshape(1, SLOTS),
        const(row_spread(), BF16),
        const(row_compact(), BF16),
    )
    fields, partial = pl.pallas_call(
        send_kernel,
        grid=(3,),
        in_specs=[pl.BlockSpec((1, 2 * UPPER, 8, 2048), lambda g: (g, 0, 0, 0))],
        out_specs=[
            pl.BlockSpec((DOMS, 1, UPPER, 8, LANES), lambda g: (0, g, 0, 0, 0)),
            pl.BlockSpec((1, UPPER, 8, 2048), lambda g: (g, 1, 0, 0)),
        ],
        out_shape=[
            jax.ShapeDtypeStruct((DOMS, 3, UPPER, 8, LANES), BF16),
            jax.ShapeDtypeStruct(prior.shape, BF16),
        ],
        compiler_params=FULL,
        name="send",
    )(prior)
    packed = lax.all_to_all(packed, "member", 0, 0, tiled=True)
    fields = lax.all_to_all(
        fields.reshape(MEMBERS, UPPER, 8, LANES), "member", 0, 0, tiled=True
    )
    sampled = pl.pallas_call(
        sample_kernel,
        in_specs=[VM, VM, VM],
        out_specs=VM,
        out_shape=jax.ShapeDtypeStruct((9, PACK, LANES), F32),
        compiler_params=LIMIT,
        name="sample",
    )(packed, own, const(row_sample(), BF16))
    ends = lax.axis_size("tile") - 1
    up = lax.ppermute(sampled, "tile", [(i, i + 1) for i in range(ends)])
    down = lax.ppermute(sampled, "tile", [(i + 1, i) for i in range(ends)])
    weights = pl.pallas_call(
        solve_kernel,
        in_specs=[VM, VM, VM, VM],
        out_specs=VM,
        out_shape=jax.ShapeDtypeStruct((24, 48, LANES), F32),
        scratch_shapes=[
            pltpu.VMEM((BLOCKS_Y * PACK, LANES), F32),
            pltpu.VMEM((24, 48, LANES), F32),
            pltpu.VMEM((2, 8, 48, LANES), F32),
            pltpu.VMEM((2, 8, 48, LANES), F32),
        ],
        compiler_params=LIMIT,
        name="solve",
    )(up, sampled, down, const(taper_rows(), F32))
    result = pl.pallas_call(
        transform_kernel,
        in_specs=[VM, VM, VM],
        out_specs=VM,
        out_shape=jax.ShapeDtypeStruct((MEMBERS, UPPER, 8, LANES), BF16),
        scratch_shapes=[
            pltpu.VMEM((24 * 48, 512), F32),
            pltpu.VMEM((MEMBERS, UPPER, 8, LANES), F32),
        ],
        compiler_params=LIMIT,
        name="transform",
    )(weights, fields, const(expand_rows(), BF16))
    result = lax.all_to_all(result, "member", 0, 0, tiled=True)
    return pl.pallas_call(
        finish_kernel,
        in_specs=[VM, ANY],
        out_specs=ANY,
        out_shape=jax.ShapeDtypeStruct(prior.shape, BF16),
        scratch_shapes=[
            pltpu.VMEM((3, UPPER, 8, 2048), BF16),
            pltpu.SemaphoreType.DMA((3,)),
        ],
        input_output_aliases={1: 0},
        compiler_params=LIMIT,
        name="finish",
    )(result.reshape(DOMS, 3, UPPER, 8, LANES), partial)


def solution(mesh):
    return jax.shard_map(
        body,
        mesh=mesh,
        in_specs=(
            P("member", None, "tile", None),
            P("tile", "member", None),
            P("tile", "member", None),
            P("tile", "member", None),
            P("tile", "member"),
        ),
        out_specs=P("member", None, "tile", None),
        check_vma=False,
    )
```

```python
import functools
import math

import jax
import jax.numpy as jnp
import numpy as np
from jax import lax
from jax.experimental import pallas as pl
from jax.experimental.pallas import tpu as pltpu
from jax.sharding import PartitionSpec as P

MEMBERS = 48
UPPER = 8
LANES = 128
SLOTS = 256
RADIUS = 8
BLOCK = 4
CHUNK = 16
GROUPS = LANES // CHUNK
BLOCKS_Y = LANES // BLOCK
ROWS = 64
PACK = 56
DOMS = 16
F32 = jnp.float32
BF16 = jnp.bfloat16


def split3(x):
    hi = x.astype(BF16)
    rest = x - hi.astype(F32)
    mid = rest.astype(BF16)
    low = (rest - mid.astype(F32)).astype(BF16)
    return hi, mid, low


def split2(x):
    hi = x.astype(BF16)
    return hi, (x - hi.astype(F32)).astype(BF16)


def nt(a, b):
    return lax.dot_general(a, b, (((1,), (1,)), ((), ())), preferred_element_type=F32)


def nn(a, b):
    return lax.dot_general(a, b, (((1,), (0,)), ((), ())), preferred_element_type=F32)


def row_spread():
    m = np.zeros((64, 48), np.float32)
    for x in range(8):
        for r in range(6):
            m[x * 8 + r, r * 8 + x] = 1.0
    return m


def row_compact():
    m = np.zeros((ROWS, 80), np.float32)
    for v in range(9):
        for r in range(6):
            m[v * 6 + r, v * 8 + r] = 1.0
    for r in range(6):
        m[54 + r, 72 + r] = 1.0
    return m


def row_sample():
    m = np.zeros((9 * PACK, DOMS * ROWS), np.float32)
    for v in range(9):
        for i in range(MEMBERS):
            for layer in range(2):
                m[v * PACK + i, (i // 3) * ROWS + v * 6 + (i % 3) * 2 + layer] = 0.5
    for s in range(DOMS):
        for r in range(3):
            m[8 * PACK + 48, s * ROWS + 54 + r] = 1.0
            m[8 * PACK + 49, s * ROWS + 57 + r] = 1.0
    return m


OFFSETS = (10, 14, 2, 6)
MEAN_ROW = 672
FIX_ROW = 720
WEIGHT_ROWS = 744


def first_row(t):
    panel = t // 4
    return 16 * panel * (panel + 1) + (t % 4) * 8 * (panel + 1)


def taper_rows():
    lane = np.arange(LANES)
    x, y = lane // CHUNK, lane % CHUNK
    t = np.zeros((24, LANES), np.float32)
    for k, o in enumerate(OFFSETS):
        gap_y = np.where(y >= o, y - o, y - o + CHUNK) - 6 - 1.5
        for seg in range(3):
            for p in range(2):
                gap_x = (seg - 1) * 8 + x - (4 * p + 1.5)
                s = gap_x * gap_x + gap_y * gap_y
                t[(k * 3 + seg) * 2 + p] = np.where(s < RADIUS * RADIUS, (1 - s / 64.0) ** 2, 0.0)
    return t


def expand_rows():
    m = np.zeros((128, 512), np.float32)
    for h in range(2):
        for p in range(2):
            for y in range(128):
                m[p * 64 + h * 32 + y // 4, h * 256 + p * 128 + y] = 1.0
    return np.concatenate([m, m], 0)


def pack_kernel(where, tally, x_ref, reading, error, cell, spread, compact, out, own, work):
    me = where[0]
    live = lax.broadcasted_iota(jnp.int32, (1, SLOTS), 1) < tally[0]
    prec = jnp.where(live, 1.0 / error[...], 0.0)
    vals = jnp.where(live, prec * reading[...], 0.0)
    c = cell[...]
    x, y = c // LANES, c % LANES
    group = y // CHUNK
    lane = x * CHUNK + y % CHUNK
    hit = lax.broadcasted_iota(jnp.int32, (8, SLOTS), 0) == group
    spot = (lax.broadcasted_iota(jnp.int32, (LANES, SLOTS), 0) == lane).astype(F32).astype(BF16)
    pv = jnp.concatenate([jnp.where(hit, prec, 0.0), jnp.where(hit, vals, 0.0)], 0)
    a, b, d = split3(pv)
    pv = nt(a, spot) + nt(b, spot) + nt(d, spot)
    own[...] = pv
    sub = lax.broadcasted_iota(jnp.int32, (8, LANES), 0)
    col = lax.broadcasted_iota(jnp.int32, (8, LANES), 1)
    high = (col % CHUNK) >= 8

    def edge(g):
        res = jnp.zeros((8, LANES), F32)
        for n in range(2):
            parts = split3(jnp.broadcast_to(pv[n * 8 + g : n * 8 + g + 1, :], (8, LANES)))
            for k in range(3):
                res = jnp.where(sub == n * 3 + k, parts[k].astype(F32), res)
        return res

    last = jnp.where(high, edge(7), 0.0)
    first = jnp.where(high, 0.0, edge(0))

    flat = x_ref[...].reshape(48, 16 * LANES)
    rows = nn(spread[...], flat)
    for d in range(DOMS):
        v = [rows[8 * k : 8 * k + 8, d * LANES : (d + 1) * LANES] for k in range(8)]
        for step in (4, 2, 1):
            width = step * CHUNK
            low = ((col // width) % 2) == 0
            new = list(v)
            for k in range(8):
                if not k & step:
                    a, b = v[k], v[k + step]
                    new[k] = jnp.where(low, a, pltpu.roll(b, width, 1))
                    new[k + step] = jnp.where(low, pltpu.roll(a, LANES - width, 1), b)
            v = new
        for k in range(8):
            work[d, 8 * k : 8 * k + 8, :] = v[k]
    for d in range(DOMS):
        left = work[(d - 1) % DOMS, 56:64, :]
        right = work[(d + 1) % DOMS, 0:8, :]
        work[d, 64:72, :] = jnp.where(high, left, right)
        work[d, 72:80, :] = jnp.where(
            me == d - 1, last, jnp.where(me == d + 1, first, jnp.zeros_like(first))
        )
    for d in range(DOMS):
        out[d] = nn(compact[...], work[d].astype(BF16)).astype(BF16)


def sample_kernel(r_ref, own, choose, out):
    pv = own[...]
    res = nn(choose[...], r_ref[...].reshape(DOMS * ROWS, LANES))
    for v in range(9):
        s = res[v * PACK : v * PACK + MEMBERS]
        mean = jnp.sum(s, axis=0, keepdims=True) * (1.0 / MEMBERS)
        if v < 8:
            prec, vals = pv[v : v + 1], pv[8 + v : 9 + v]
        else:
            prec, vals = res[v * PACK + 48 : v * PACK + 49], res[v * PACK + 49 : v * PACK + 50]
        out[v, 0:48, :] = s - mean
        sub = lax.broadcasted_iota(jnp.int32, (8, LANES), 0)
        out[v, 48:56, :] = jnp.where(
            sub == 0, prec, jnp.where(sub == 1, vals - prec * mean, 0.0)
        )


def solve_kernel(up, own, down, taper, out, grams, mat, piv, fac):
    segs = (up, own, down)
    lane = lax.broadcasted_iota(jnp.int32, (1, LANES), 1) % CHUNK
    first = lax.broadcasted_iota(jnp.int32, (16, LANES), 0) == 0
    for g in range(GROUPS):
        for k, o in enumerate(OFFSETS):
            v0 = g - 1 if k < 2 else g
            v1 = v0 + 1
            v0, v1 = (8 if v in (-1, 8) else v for v in (v0, v1))
            mask = lane >= o
            shi, slo, whi, wlo = [], [], [], []
            for s in range(3):
                w = jnp.where(mask, segs[s][v0], segs[s][v1])
                a = w[0:48]
                prec, drv = w[48:49], w[49:50]
                row = (k * 3 + s) * 2
                stream = jnp.concatenate([a * prec, jnp.where(first, drv, 0.0)], 0)
                h, l = split2(stream)
                shi.append(h)
                slo.append(l)
                h, l = split2(
                    jnp.concatenate([a * taper[row : row + 1, :], a * taper[row + 1 : row + 2, :]], 0)
                )
                whi.append(h)
                wlo.append(l)
            stream = jnp.concatenate(
                [jnp.concatenate(shi + shi, 1), jnp.concatenate(slo + slo, 1)], 0
            )
            res = nt(stream, jnp.concatenate(whi + wlo, 1))
            res = res[0:56] + res[64:120]
            res = jnp.concatenate([res, jnp.zeros((56, LANES - 2 * MEMBERS), F32)], 1)
            q = g * 4 + k
            grams[q * PACK : (q + 1) * PACK, :] = res

    sub = lax.broadcasted_iota(jnp.int32, (8, LANES), 0)
    half = (lax.broadcasted_iota(jnp.int32, (8, LANES), 1) // 32) % 2
    half0 = half == 0
    low = lax.broadcasted_iota(jnp.int32, (48, LANES), 1) < 64

    def columns(js):
        t = jnp.concatenate([grams[pl.ds(j, 32, stride=PACK), :] for j in js], 0).T
        return t[0:48], t[48:96]

    for j in range(12):
        t0, t1 = columns(range(4 * j, 4 * j + 4))
        mat[2 * j] = jnp.where(low, t0, pltpu.roll(t1, 64, 1))
        mat[2 * j + 1] = jnp.where(low, pltpu.roll(t0, 64, 1), t1)
    t0, t1 = columns([48] * 4)
    drive = jnp.where(low, t0, t1)
    drive = [drive[8 * j : 8 * j + 8] for j in range(6)]

    def bcast(x, k):
        return jnp.broadcast_to(x[k : k + 1, :], (8, LANES))

    def both(x, h):
        return jnp.where(half == h, x, pltpu.roll(x, 32 if h == 0 else 96, 1))

    scale = []
    for panel in range(6):
        buf = panel % 2
        others = [j for j in range(6) if j != panel]
        rows = [
            [mat[4 * panel + n, 8 * j : 8 * j + 8, :] for j in range(6)] for n in range(4)
        ]
        d = [both(rows[r // 2][panel], r % 2) for r in range(8)]
        d = [jnp.where(sub == r, d[r] + (MEMBERS - 1.0), d[r]) for r in range(8)]
        invs, fds = [], []
        for k in range(8):
            inv = 1.0 / bcast(d[k], k)
            invs.append(inv)
            scale.append(jnp.sqrt((MEMBERS - 1.0) * inv[0:1, :]))
            here = sub == k
            row = jnp.where(here, 1.0, d[k])
            for r in range(k + 1, 8):
                d[r] = jnp.where(here, 0.0, d[r]) - (bcast(d[k], r) * inv) * row
            fd = bcast(drive[panel], k) * inv
            fds.append(fd)
            drive[panel] = jnp.where(here, 0.0, drive[panel]) - fd * row
            d[k] = jnp.where(sub <= k, row, 0.0)
            piv[buf, k, 8 * panel : 8 * panel + 8, :] = d[k]
        for n in range(4):
            mat[4 * panel + n, 8 * panel : 8 * panel + 8, :] = jnp.where(
                half0, d[2 * n], d[2 * n + 1]
            )
        eb = [[bcast(d[r], c) for c in range(r)] for r in range(8)]
        for j in others:
            x = [both(rows[r // 2][j], r % 2) for r in range(8)]
            y = []
            for r in range(8):
                t = x[r]
                for c in range(r):
                    t = t + eb[r][c] * x[c]
                y.append(t)
                piv[buf, r, 8 * j : 8 * j + 8, :] = t
                if j > panel:
                    fac[buf, r, 8 * j : 8 * j + 8, :] = t * invs[r]
                drive[j] = drive[j] - fds[r] * t
            if j < panel:
                for n in range(4):
                    mat[4 * panel + n, 8 * j : 8 * j + 8, :] = jnp.where(
                        half0, y[2 * n], y[2 * n + 1]
                    )
        for block in range(panel + 1, 6):
            js = list(range(panel + 1)) + list(range(block, 6))
            acc = [
                {
                    j: jnp.zeros((8, LANES), F32)
                    if j == panel
                    else mat[4 * block + n, 8 * j : 8 * j + 8, :]
                    for j in js
                }
                for n in range(4)
            ]
            for k in range(8):
                pr = {j: piv[buf, k, 8 * j : 8 * j + 8, :] for j in js}
                for n in range(4):
                    i = 8 * block + 2 * n
                    fa = jnp.broadcast_to(fac[buf, k, i : i + 1, :], (8, LANES))
                    fb = jnp.broadcast_to(fac[buf, k, i + 1 : i + 2, :], (8, LANES))
                    fp = jnp.where(half0, fa, fb)
                    for j in js:
                        acc[n][j] = acc[n][j] - fp * pr[j]
            for n in range(4):
                for j in js:
                    mat[4 * block + n, 8 * j : 8 * j + 8, :] = acc[n][j]

    mean = [-x for x in drive]
    mean_total = mean[0] + mean[1] + mean[2] + mean[3] + mean[4] + mean[5]
    for j in range(6):
        out[MEAN_ROW + 8 * j : MEAN_ROW + 8 * j + 8, :] = mean[j]
    for t in range(24):
        panel = t // 4
        base = first_row(t)
        sc = jnp.where(half0, scale[2 * t], scale[2 * t + 1])
        total = mean_total
        for j in range(panel + 1):
            x = sc * mat[t, 8 * j : 8 * j + 8, :]
            out[base + 8 * j : base + 8 * j + 8, :] = x
            total = total + x
        total = jnp.sum(total, axis=0, keepdims=True)
        out[FIX_ROW + t : FIX_ROW + t + 1, :] = (1.0 - total) * (1.0 / MEMBERS)


def transform_kernel(w_ref, x_ref, expand, out, wide, xs, base):
    hi, low = split2(w_ref[...])
    wide[...] = nn(jnp.concatenate([hi, low], 1), expand[...])
    for i in range(MEMBERS):
        for l in range(8):
            xs[i, l] = x_ref[i, l].astype(F32)
    top = lax.broadcasted_iota(jnp.int32, (8, LANES), 0) < 4

    def weights(r, halves):
        line = wide[pl.ds(r, 1), :]
        res = []
        for h in range(halves):
            a = jnp.broadcast_to(line[:, h * 256 : h * 256 + 128], (8, LANES))
            b = jnp.broadcast_to(line[:, h * 256 + 128 : h * 256 + 256], (8, LANES))
            res.append(jnp.where(top, a, b))
        return res

    def common(i, acc):
        acc = list(acc)
        for u in range(16):
            w = weights(MEAN_ROW + i * 16 + u, 1)[0]
            for l in range(8):
                x = xs[i * 16 + u, l]
                acc[l] = acc[l] + x * w
                acc[8 + l] = acc[8 + l] + x
        return tuple(acc)

    zeros = tuple(jnp.zeros((8, LANES), F32) for _ in range(16))
    acc = lax.fori_loop(0, 3, common, zeros)
    for l in range(8):
        base[l] = acc[l]
        base[8 + l] = acc[8 + l]

    for panel, step in enumerate((8, 16, 24, 16, 20, 24)):
        count = 8 * (panel + 1)

        def pair(n, c, panel=panel, step=step, count=count):
            t = 4 * panel + n
            row = first_row(4 * panel) + n * count
            fix = weights(FIX_ROW + t, 2)

            def some(i, acc):
                acc = list(acc)
                for u in range(step):
                    w = weights(row + i * step + u, 2)
                    for l in range(8):
                        x = xs[i * step + u, l]
                        acc[l] = acc[l] + x * w[0]
                        acc[8 + l] = acc[8 + l] + x * w[1]
                return tuple(acc)

            acc = tuple(base[l] + base[8 + l] * fix[h] for h in range(2) for l in range(8))
            acc = lax.fori_loop(0, count // step, some, acc)
            for h in range(2):
                for l in range(8):
                    out[2 * t + h, l] = acc[8 * h + l].astype(BF16)
            return c

        lax.fori_loop(0, 4, pair, 0)


def send_kernel(x_ref, out, lower):
    for d in range(DOMS):
        out[d, 0] = x_ref[0, 0:UPPER, :, d * LANES : (d + 1) * LANES]
    lower[...] = x_ref[:, UPPER : 2 * UPPER]


def finish_kernel(b_ref, partial, out, work, sems):
    del partial
    copies = []
    for m in range(3):
        for d in range(DOMS):
            work[m, :, :, d * LANES : (d + 1) * LANES] = b_ref[d, m]
        copy = pltpu.make_async_copy(work.at[m], out.at[m, 0:UPPER], sems.at[m])
        copy.start()
        copies.append(copy)
    for copy in copies:
        copy.wait()


VM = pl.BlockSpec(memory_space=pltpu.VMEM)
SM = pl.BlockSpec(memory_space=pltpu.SMEM)
ANY = pl.BlockSpec(memory_space=pl.ANY)
FULL = pltpu.CompilerParams(vmem_limit_bytes=62000000)
LIMIT = pltpu.CompilerParams(vmem_limit_bytes=48 * 2**20)


def body(prior, reading, error, cell, tally):
    me = lax.axis_index("member").astype(jnp.int32).reshape(1)
    const = lambda a, t: jnp.asarray(a, t)
    whole = lambda *shape: pl.BlockSpec(shape, lambda g: (0,) * len(shape))
    packed, own = pl.pallas_call(
        pack_kernel,
        grid=(1,),
        in_specs=[
            SM,
            SM,
            whole(3, 2, 8, 2048),
            whole(1, SLOTS),
            whole(1, SLOTS),
            whole(1, SLOTS),
            whole(64, 48),
            whole(ROWS, 80),
        ],
        out_specs=[VM, VM],
        out_shape=[
            jax.ShapeDtypeStruct((DOMS, ROWS, LANES), BF16),
            jax.ShapeDtypeStruct((16, LANES), F32),
        ],
        scratch_shapes=[pltpu.VMEM((DOMS, 80, LANES), F32)],
        compiler_params=FULL,
        name="pack",
    )(
        me,
        tally.reshape(1),
        prior,
        reading.reshape(1, SLOTS),
        error.reshape(1, SLOTS),
        cell.reshape(1, SLOTS),
        const(row_spread(), BF16),
        const(row_compact(), BF16),
    )
    fields, partial = pl.pallas_call(
        send_kernel,
        grid=(3,),
        in_specs=[pl.BlockSpec((1, 2 * UPPER, 8, 2048), lambda g: (g, 0, 0, 0))],
        out_specs=[
            pl.BlockSpec((DOMS, 1, UPPER, 8, LANES), lambda g: (0, g, 0, 0, 0)),
            pl.BlockSpec((1, UPPER, 8, 2048), lambda g: (g, 1, 0, 0)),
        ],
        out_shape=[
            jax.ShapeDtypeStruct((DOMS, 3, UPPER, 8, LANES), BF16),
            jax.ShapeDtypeStruct(prior.shape, BF16),
        ],
        compiler_params=FULL,
        name="send",
    )(prior)
    packed = lax.all_to_all(packed, "member", 0, 0, tiled=True)
    fields = lax.all_to_all(
        fields.reshape(MEMBERS, UPPER, 8, LANES), "member", 0, 0, tiled=True
    )
    sampled = pl.pallas_call(
        sample_kernel,
        in_specs=[VM, VM, VM],
        out_specs=VM,
        out_shape=jax.ShapeDtypeStruct((9, PACK, LANES), F32),
        compiler_params=LIMIT,
        name="sample",
    )(packed, own, const(row_sample(), BF16))
    ends = lax.axis_size("tile") - 1
    up = lax.ppermute(sampled, "tile", [(i, i + 1) for i in range(ends)])
    down = lax.ppermute(sampled, "tile", [(i + 1, i) for i in range(ends)])
    weights = pl.pallas_call(
        solve_kernel,
        in_specs=[VM, VM, VM, VM],
        out_specs=VM,
        out_shape=jax.ShapeDtypeStruct((WEIGHT_ROWS, LANES), F32),
        scratch_shapes=[
            pltpu.VMEM((BLOCKS_Y * PACK, LANES), F32),
            pltpu.VMEM((24, 48, LANES), F32),
            pltpu.VMEM((2, 8, 48, LANES), F32),
            pltpu.VMEM((2, 8, 48, LANES), F32),
        ],
        compiler_params=LIMIT,
        name="solve",
    )(up, sampled, down, const(taper_rows(), F32))
    result = pl.pallas_call(
        transform_kernel,
        in_specs=[VM, VM, VM],
        out_specs=VM,
        out_shape=jax.ShapeDtypeStruct((MEMBERS, UPPER, 8, LANES), BF16),
        scratch_shapes=[
            pltpu.VMEM((WEIGHT_ROWS, 512), F32),
            pltpu.VMEM((MEMBERS, UPPER, 8, LANES), F32),
            pltpu.VMEM((16, 8, LANES), F32),
        ],
        compiler_params=LIMIT,
        name="transform",
    )(weights, fields, const(expand_rows(), BF16))
    result = lax.all_to_all(result, "member", 0, 0, tiled=True)
    return pl.pallas_call(
        finish_kernel,
        in_specs=[VM, ANY],
        out_specs=ANY,
        out_shape=jax.ShapeDtypeStruct(prior.shape, BF16),
        scratch_shapes=[
            pltpu.VMEM((3, UPPER, 8, 2048), BF16),
            pltpu.SemaphoreType.DMA((3,)),
        ],
        input_output_aliases={1: 0},
        compiler_params=LIMIT,
        name="finish",
    )(result.reshape(DOMS, 3, UPPER, 8, LANES), partial)


def solution(mesh):
    return jax.shard_map(
        body,
        mesh=mesh,
        in_specs=(
            P("member", None, "tile", None),
            P("tile", "member", None),
            P("tile", "member", None),
            P("tile", "member", None),
            P("tile", "member"),
        ),
        out_specs=P("member", None, "tile", None),
        check_vma=False,
    )
```

```python
import functools
import math

import jax
import jax.numpy as jnp
import numpy as np
from jax import lax
from jax.experimental import pallas as pl
from jax.experimental.pallas import tpu as pltpu
from jax.sharding import PartitionSpec as P

MEMBERS = 48
UPPER = 8
LANES = 128
SLOTS = 256
RADIUS = 8
BLOCK = 4
CHUNK = 16
GROUPS = LANES // CHUNK
BLOCKS_Y = LANES // BLOCK
ROWS = 64
PACK = 56
DOMS = 16
F32 = jnp.float32
BF16 = jnp.bfloat16


def split3(x):
    hi = x.astype(BF16)
    rest = x - hi.astype(F32)
    mid = rest.astype(BF16)
    low = (rest - mid.astype(F32)).astype(BF16)
    return hi, mid, low


def split2(x):
    hi = x.astype(BF16)
    return hi, (x - hi.astype(F32)).astype(BF16)


def nt(a, b):
    return lax.dot_general(a, b, (((1,), (1,)), ((), ())), preferred_element_type=F32)


def nn(a, b):
    return lax.dot_general(a, b, (((1,), (0,)), ((), ())), preferred_element_type=F32)


def row_spread():
    m = np.zeros((64, 48), np.float32)
    for x in range(8):
        for r in range(6):
            m[x * 8 + r, r * 8 + x] = 1.0
    return m


def row_compact():
    m = np.zeros((ROWS, 80), np.float32)
    for v in range(9):
        for r in range(6):
            m[v * 6 + r, v * 8 + r] = 1.0
    for r in range(6):
        m[54 + r, 72 + r] = 1.0
    return m


def row_sample():
    m = np.zeros((9 * PACK, DOMS * ROWS), np.float32)
    for v in range(9):
        for i in range(MEMBERS):
            for layer in range(2):
                m[v * PACK + i, (i // 3) * ROWS + v * 6 + (i % 3) * 2 + layer] = 0.5
    for s in range(DOMS):
        for r in range(3):
            m[8 * PACK + 48, s * ROWS + 54 + r] = 1.0
            m[8 * PACK + 49, s * ROWS + 57 + r] = 1.0
    return m


OFFSETS = (10, 14, 2, 6)
MEAN_ROW = 672
FIX_ROW = 720
WEIGHT_ROWS = 744


def first_row(t):
    panel = t // 4
    return 16 * panel * (panel + 1) + (t % 4) * 8 * (panel + 1)


def taper_rows():
    lane = np.arange(LANES)
    x, y = lane // CHUNK, lane % CHUNK
    t = np.zeros((24, LANES), np.float32)
    for k, o in enumerate(OFFSETS):
        gap_y = np.where(y >= o, y - o, y - o + CHUNK) - 6 - 1.5
        for seg in range(3):
            for p in range(2):
                gap_x = (seg - 1) * 8 + x - (4 * p + 1.5)
                s = gap_x * gap_x + gap_y * gap_y
                t[(k * 3 + seg) * 2 + p] = np.where(s < RADIUS * RADIUS, (1 - s / 64.0) ** 2, 0.0)
    return t


def taper_table():
    base = taper_rows().reshape(4, 3, 2, LANES)
    table = np.zeros((4, 4, 3, 2, LANES), np.float32)
    for odd in range(2):
        for edge in range(2):
            t = table[2 * odd + edge]
            t[:, 0] = base[:, 0 if odd else 2]
            t[:, 1] = base[:, 1]
            t[:, 2] = 0.0 if edge else base[:, 2 if odd else 0]
    return table.reshape(96, LANES)


def expand_rows():
    m = np.zeros((128, 512), np.float32)
    for h in range(2):
        for p in range(2):
            for y in range(128):
                m[p * 64 + h * 32 + y // 4, h * 256 + p * 128 + y] = 1.0
    return np.concatenate([m, m], 0)


def pack_kernel(where, tally, x_ref, reading, error, cell, spread, compact, out, own, work):
    me = where[0]
    live = lax.broadcasted_iota(jnp.int32, (1, SLOTS), 1) < tally[0]
    prec = jnp.where(live, 1.0 / error[...], 0.0)
    vals = jnp.where(live, prec * reading[...], 0.0)
    c = cell[...]
    x, y = c // LANES, c % LANES
    group = y // CHUNK
    lane = x * CHUNK + y % CHUNK
    hit = lax.broadcasted_iota(jnp.int32, (8, SLOTS), 0) == group
    spot = (lax.broadcasted_iota(jnp.int32, (LANES, SLOTS), 0) == lane).astype(F32).astype(BF16)
    pv = jnp.concatenate([jnp.where(hit, prec, 0.0), jnp.where(hit, vals, 0.0)], 0)
    a, b, d = split3(pv)
    pv = nt(a, spot) + nt(b, spot) + nt(d, spot)
    own[...] = pv
    sub = lax.broadcasted_iota(jnp.int32, (8, LANES), 0)
    col = lax.broadcasted_iota(jnp.int32, (8, LANES), 1)
    high = (col % CHUNK) >= 8

    def edge(g):
        res = jnp.zeros((8, LANES), F32)
        for n in range(2):
            parts = split3(jnp.broadcast_to(pv[n * 8 + g : n * 8 + g + 1, :], (8, LANES)))
            for k in range(3):
                res = jnp.where(sub == n * 3 + k, parts[k].astype(F32), res)
        return res

    last = jnp.where(high, edge(7), 0.0)
    first = jnp.where(high, 0.0, edge(0))

    flat = x_ref[...].reshape(48, 16 * LANES)
    rows = nn(spread[...], flat)
    for d in range(DOMS):
        v = [rows[8 * k : 8 * k + 8, d * LANES : (d + 1) * LANES] for k in range(8)]
        for step in (4, 2, 1):
            width = step * CHUNK
            low = ((col // width) % 2) == 0
            new = list(v)
            for k in range(8):
                if not k & step:
                    a, b = v[k], v[k + step]
                    new[k] = jnp.where(low, a, pltpu.roll(b, width, 1))
                    new[k + step] = jnp.where(low, pltpu.roll(a, LANES - width, 1), b)
            v = new
        for k in range(8):
            work[d, 8 * k : 8 * k + 8, :] = v[k]
    for d in range(DOMS):
        left = work[(d - 1) % DOMS, 56:64, :]
        right = work[(d + 1) % DOMS, 0:8, :]
        work[d, 64:72, :] = jnp.where(high, left, right)
        work[d, 72:80, :] = jnp.where(
            me == d - 1, last, jnp.where(me == d + 1, first, jnp.zeros_like(first))
        )
    for d in range(DOMS):
        out[d] = nn(compact[...], work[d].astype(BF16)).astype(BF16)


def sample_kernel(r_ref, own, choose, out):
    pv = own[...]
    res = nn(choose[...], r_ref[...].reshape(DOMS * ROWS, LANES))
    for v in range(9):
        s = res[v * PACK : v * PACK + MEMBERS]
        mean = jnp.sum(s, axis=0, keepdims=True) * (1.0 / MEMBERS)
        if v < 8:
            prec, vals = pv[v : v + 1], pv[8 + v : 9 + v]
        else:
            prec, vals = res[v * PACK + 48 : v * PACK + 49], res[v * PACK + 49 : v * PACK + 50]
        out[v, 0:48, :] = s - mean
        sub = lax.broadcasted_iota(jnp.int32, (8, LANES), 0)
        out[v, 48:56, :] = jnp.where(
            sub == 0, prec, jnp.where(sub == 1, vals - prec * mean, 0.0)
        )


def gram_products(segs, taper):
    lane = lax.broadcasted_iota(jnp.int32, (1, LANES), 1) % CHUNK
    first = lax.broadcasted_iota(jnp.int32, (16, LANES), 0) == 0
    for g in range(GROUPS):
        for k, o in enumerate(OFFSETS):
            v0 = g - 1 if k < 2 else g
            v1 = v0 + 1
            v0, v1 = (8 if v in (-1, 8) else v for v in (v0, v1))
            mask = lane >= o
            shi, slo, whi, wlo = [], [], [], []
            for s, ref in segs:
                w = jnp.where(mask, ref[v0], ref[v1])
                a = w[0:48]
                prec, drv = w[48:49], w[49:50]
                row = (k * 3 + s) * 2
                stream = jnp.concatenate([a * prec, jnp.where(first, drv, 0.0)], 0)
                h, l = split2(stream)
                shi.append(h)
                slo.append(l)
                h, l = split2(
                    jnp.concatenate([a * taper[row : row + 1], a * taper[row + 1 : row + 2]], 0)
                )
                whi.append(h)
                wlo.append(l)
            stream = jnp.concatenate(
                [jnp.concatenate(shi + shi, 1), jnp.concatenate(slo + slo, 1)], 0
            )
            res = nt(stream, jnp.concatenate(whi + wlo, 1))
            res = res[0:56] + res[64:120]
            res = jnp.concatenate([res, jnp.zeros((56, LANES - 2 * MEMBERS), F32)], 1)
            yield g * 4 + k, res


def pick_taper(tile, taper):
    place = tile[0]
    edge = jnp.logical_or(place == 0, place == 15).astype(jnp.int32)
    variant = 2 * (place % 2) + edge
    return taper[pl.ds(pl.multiple_of(variant * 24, 8), 24), :]


def near_kernel(tile, own, pair, taper, out):
    for q, res in gram_products([(0, pair), (1, own)], pick_taper(tile, taper)):
        out[q * PACK : (q + 1) * PACK, :] = res


def solve_kernel(tile, following, partial, taper, out, grams, mat, piv, fac):
    for q, res in gram_products([(2, following)], pick_taper(tile, taper)):
        grams[q * PACK : (q + 1) * PACK, :] = partial[q * PACK : (q + 1) * PACK, :] + res

    sub = lax.broadcasted_iota(jnp.int32, (8, LANES), 0)
    half = (lax.broadcasted_iota(jnp.int32, (8, LANES), 1) // 32) % 2
    half0 = half == 0
    low = lax.broadcasted_iota(jnp.int32, (48, LANES), 1) < 64

    def columns(js):
        t = jnp.concatenate([grams[pl.ds(j, 32, stride=PACK), :] for j in js], 0).T
        return t[0:48], t[48:96]

    for j in range(12):
        t0, t1 = columns(range(4 * j, 4 * j + 4))
        mat[2 * j] = jnp.where(low, t0, pltpu.roll(t1, 64, 1))
        mat[2 * j + 1] = jnp.where(low, pltpu.roll(t0, 64, 1), t1)
    t0, t1 = columns([48] * 4)
    drive = jnp.where(low, t0, t1)
    drive = [drive[8 * j : 8 * j + 8] for j in range(6)]

    def bcast(x, k):
        return jnp.broadcast_to(x[k : k + 1, :], (8, LANES))

    def both(x, h):
        return jnp.where(half == h, x, pltpu.roll(x, 32 if h == 0 else 96, 1))

    scale = []
    for panel in range(6):
        buf = panel % 2
        others = [j for j in range(6) if j != panel]
        rows = [
            [mat[4 * panel + n, 8 * j : 8 * j + 8, :] for j in range(6)] for n in range(4)
        ]
        d = [both(rows[r // 2][panel], r % 2) for r in range(8)]
        d = [jnp.where(sub == r, d[r] + (MEMBERS - 1.0), d[r]) for r in range(8)]
        invs, fds = [], []
        for k in range(8):
            inv = 1.0 / bcast(d[k], k)
            invs.append(inv)
            scale.append(jnp.sqrt((MEMBERS - 1.0) * inv[0:1, :]))
            here = sub == k
            row = jnp.where(here, 1.0, d[k])
            for r in range(k + 1, 8):
                d[r] = jnp.where(here, 0.0, d[r]) - (bcast(d[k], r) * inv) * row
            fd = bcast(drive[panel], k) * inv
            fds.append(fd)
            drive[panel] = jnp.where(here, 0.0, drive[panel]) - fd * row
            d[k] = jnp.where(sub <= k, row, 0.0)
            piv[buf, k, 8 * panel : 8 * panel + 8, :] = d[k]
        for n in range(4):
            mat[4 * panel + n, 8 * panel : 8 * panel + 8, :] = jnp.where(
                half0, d[2 * n], d[2 * n + 1]
            )
        eb = [[bcast(d[r], c) for c in range(r)] for r in range(8)]
        for j in others:
            x = [both(rows[r // 2][j], r % 2) for r in range(8)]
            y = []
            for r in range(8):
                t = x[r]
                for c in range(r):
                    t = t + eb[r][c] * x[c]
                y.append(t)
                piv[buf, r, 8 * j : 8 * j + 8, :] = t
                if j > panel:
                    fac[buf, r, 8 * j : 8 * j + 8, :] = t * invs[r]
                drive[j] = drive[j] - fds[r] * t
            if j < panel:
                for n in range(4):
                    mat[4 * panel + n, 8 * j : 8 * j + 8, :] = jnp.where(
                        half0, y[2 * n], y[2 * n + 1]
                    )
        for block in range(panel + 1, 6):
            js = list(range(panel + 1)) + list(range(block, 6))
            acc = [
                {
                    j: jnp.zeros((8, LANES), F32)
                    if j == panel
                    else mat[4 * block + n, 8 * j : 8 * j + 8, :]
                    for j in js
                }
                for n in range(4)
            ]
            for k in range(8):
                pr = {j: piv[buf, k, 8 * j : 8 * j + 8, :] for j in js}
                for n in range(4):
                    i = 8 * block + 2 * n
                    fa = jnp.broadcast_to(fac[buf, k, i : i + 1, :], (8, LANES))
                    fb = jnp.broadcast_to(fac[buf, k, i + 1 : i + 2, :], (8, LANES))
                    fp = jnp.where(half0, fa, fb)
                    for j in js:
                        acc[n][j] = acc[n][j] - fp * pr[j]
            for n in range(4):
                for j in js:
                    mat[4 * block + n, 8 * j : 8 * j + 8, :] = acc[n][j]

    mean = [-x for x in drive]
    mean_total = mean[0] + mean[1] + mean[2] + mean[3] + mean[4] + mean[5]
    for j in range(6):
        out[MEAN_ROW + 8 * j : MEAN_ROW + 8 * j + 8, :] = mean[j]
    for t in range(24):
        panel = t // 4
        base = first_row(t)
        sc = jnp.where(half0, scale[2 * t], scale[2 * t + 1])
        total = mean_total
        for j in range(panel + 1):
            x = sc * mat[t, 8 * j : 8 * j + 8, :]
            out[base + 8 * j : base + 8 * j + 8, :] = x
            total = total + x
        total = jnp.sum(total, axis=0, keepdims=True)
        out[FIX_ROW + t : FIX_ROW + t + 1, :] = (1.0 - total) * (1.0 / MEMBERS)


def transform_kernel(w_ref, x_ref, expand, out, wide, xs, base):
    hi, low = split2(w_ref[...])
    wide[...] = nn(jnp.concatenate([hi, low], 1), expand[...])
    for i in range(MEMBERS):
        for l in range(8):
            xs[i, l] = x_ref[i, l].astype(F32)
    top = lax.broadcasted_iota(jnp.int32, (8, LANES), 0) < 4

    def weights(r, halves):
        line = wide[pl.ds(r, 1), :]
        res = []
        for h in range(halves):
            a = jnp.broadcast_to(line[:, h * 256 : h * 256 + 128], (8, LANES))
            b = jnp.broadcast_to(line[:, h * 256 + 128 : h * 256 + 256], (8, LANES))
            res.append(jnp.where(top, a, b))
        return res

    def common(i, acc):
        acc = list(acc)
        for u in range(16):
            w = weights(MEAN_ROW + i * 16 + u, 1)[0]
            for l in range(8):
                x = xs[i * 16 + u, l]
                acc[l] = acc[l] + x * w
                acc[8 + l] = acc[8 + l] + x
        return tuple(acc)

    zeros = tuple(jnp.zeros((8, LANES), F32) for _ in range(16))
    acc = lax.fori_loop(0, 3, common, zeros)
    for l in range(8):
        base[l] = acc[l]
        base[8 + l] = acc[8 + l]

    for panel, step in enumerate((8, 16, 24, 16, 20, 24)):
        count = 8 * (panel + 1)

        def pair(n, c, panel=panel, step=step, count=count):
            t = 4 * panel + n
            row = first_row(4 * panel) + n * count
            fix = weights(FIX_ROW + t, 2)

            def some(i, acc):
                acc = list(acc)
                for u in range(step):
                    w = weights(row + i * step + u, 2)
                    for l in range(8):
                        x = xs[i * step + u, l]
                        acc[l] = acc[l] + x * w[0]
                        acc[8 + l] = acc[8 + l] + x * w[1]
                return tuple(acc)

            acc = tuple(base[l] + base[8 + l] * fix[h] for h in range(2) for l in range(8))
            acc = lax.fori_loop(0, count // step, some, acc)
            for h in range(2):
                for l in range(8):
                    out[2 * t + h, l] = acc[8 * h + l].astype(BF16)
            return c

        lax.fori_loop(0, 4, pair, 0)


def send_kernel(x_ref, out, lower):
    for d in range(DOMS):
        out[d, 0] = x_ref[0, 0:UPPER, :, d * LANES : (d + 1) * LANES]
    lower[...] = x_ref[:, UPPER : 2 * UPPER]


def finish_kernel(b_ref, partial, out, work, sems):
    del partial
    copies = []
    for m in range(3):
        for d in range(DOMS):
            work[m, :, :, d * LANES : (d + 1) * LANES] = b_ref[d, m]
        copy = pltpu.make_async_copy(work.at[m], out.at[m, 0:UPPER], sems.at[m])
        copy.start()
        copies.append(copy)
    for copy in copies:
        copy.wait()


VM = pl.BlockSpec(memory_space=pltpu.VMEM)
SM = pl.BlockSpec(memory_space=pltpu.SMEM)
ANY = pl.BlockSpec(memory_space=pl.ANY)
FULL = pltpu.CompilerParams(vmem_limit_bytes=62000000)
LIMIT = pltpu.CompilerParams(vmem_limit_bytes=48 * 2**20)


def body(prior, reading, error, cell, tally):
    me = lax.axis_index("member").astype(jnp.int32).reshape(1)
    tile = lax.axis_index("tile").astype(jnp.int32).reshape(1)
    const = lambda a, t: jnp.asarray(a, t)
    whole = lambda *shape: pl.BlockSpec(shape, lambda g: (0,) * len(shape))
    packed, own = pl.pallas_call(
        pack_kernel,
        grid=(1,),
        in_specs=[
            SM,
            SM,
            whole(3, 2, 8, 2048),
            whole(1, SLOTS),
            whole(1, SLOTS),
            whole(1, SLOTS),
            whole(64, 48),
            whole(ROWS, 80),
        ],
        out_specs=[VM, VM],
        out_shape=[
            jax.ShapeDtypeStruct((DOMS, ROWS, LANES), BF16),
            jax.ShapeDtypeStruct((16, LANES), F32),
        ],
        scratch_shapes=[pltpu.VMEM((DOMS, 80, LANES), F32)],
        compiler_params=FULL,
        name="pack",
    )(
        me,
        tally.reshape(1),
        prior,
        reading.reshape(1, SLOTS),
        error.reshape(1, SLOTS),
        cell.reshape(1, SLOTS),
        const(row_spread(), BF16),
        const(row_compact(), BF16),
    )
    fields, partial = pl.pallas_call(
        send_kernel,
        grid=(3,),
        in_specs=[pl.BlockSpec((1, 2 * UPPER, 8, 2048), lambda g: (g, 0, 0, 0))],
        out_specs=[
            pl.BlockSpec((DOMS, 1, UPPER, 8, LANES), lambda g: (0, g, 0, 0, 0)),
            pl.BlockSpec((1, UPPER, 8, 2048), lambda g: (g, 1, 0, 0)),
        ],
        out_shape=[
            jax.ShapeDtypeStruct((DOMS, 3, UPPER, 8, LANES), BF16),
            jax.ShapeDtypeStruct(prior.shape, BF16),
        ],
        compiler_params=FULL,
        name="send",
    )(prior)
    packed = lax.all_to_all(packed, "member", 0, 0, tiled=True)
    fields = lax.all_to_all(
        fields.reshape(MEMBERS, UPPER, 8, LANES), "member", 0, 0, tiled=True
    )
    sampled = pl.pallas_call(
        sample_kernel,
        in_specs=[VM, VM, VM],
        out_specs=VM,
        out_shape=jax.ShapeDtypeStruct((9, PACK, LANES), F32),
        compiler_params=LIMIT,
        name="sample",
    )(packed, own, const(row_sample(), BF16))
    tiles = lax.axis_size("tile")
    pair = lax.ppermute(sampled, "tile", [(i, i ^ 1) for i in range(tiles)])
    following = lax.ppermute(
        sampled, "tile", [(i, (i + 1 if i % 2 else i - 1) % tiles) for i in range(tiles)]
    )
    table = const(taper_table(), F32)
    partial_gram = pl.pallas_call(
        near_kernel,
        in_specs=[SM, VM, VM, VM],
        out_specs=VM,
        out_shape=jax.ShapeDtypeStruct((BLOCKS_Y * PACK, LANES), F32),
        compiler_params=LIMIT,
        cost_estimate=pl.CostEstimate(flops=10**9, bytes_accessed=3 * 10**6, transcendentals=0),
        name="near_gram",
    )(tile, sampled, pair, table)
    weights = pl.pallas_call(
        solve_kernel,
        in_specs=[SM, VM, VM, VM],
        out_specs=VM,
        out_shape=jax.ShapeDtypeStruct((WEIGHT_ROWS, LANES), F32),
        scratch_shapes=[
            pltpu.VMEM((BLOCKS_Y * PACK, LANES), F32),
            pltpu.VMEM((24, 48, LANES), F32),
            pltpu.VMEM((2, 8, 48, LANES), F32),
            pltpu.VMEM((2, 8, 48, LANES), F32),
        ],
        compiler_params=LIMIT,
        name="solve",
    )(tile, following, partial_gram, table)
    result = pl.pallas_call(
        transform_kernel,
        in_specs=[VM, VM, VM],
        out_specs=VM,
        out_shape=jax.ShapeDtypeStruct((MEMBERS, UPPER, 8, LANES), BF16),
        scratch_shapes=[
            pltpu.VMEM((WEIGHT_ROWS, 512), F32),
            pltpu.VMEM((MEMBERS, UPPER, 8, LANES), F32),
            pltpu.VMEM((16, 8, LANES), F32),
        ],
        compiler_params=LIMIT,
        name="transform",
    )(weights, fields, const(expand_rows(), BF16))
    result = lax.all_to_all(result, "member", 0, 0, tiled=True)
    return pl.pallas_call(
        finish_kernel,
        in_specs=[VM, ANY],
        out_specs=ANY,
        out_shape=jax.ShapeDtypeStruct(prior.shape, BF16),
        scratch_shapes=[
            pltpu.VMEM((3, UPPER, 8, 2048), BF16),
            pltpu.SemaphoreType.DMA((3,)),
        ],
        input_output_aliases={1: 0},
        compiler_params=LIMIT,
        name="finish",
    )(result.reshape(DOMS, 3, UPPER, 8, LANES), partial)


def solution(mesh):
    return jax.shard_map(
        body,
        mesh=mesh,
        in_specs=(
            P("member", None, "tile", None),
            P("tile", "member", None),
            P("tile", "member", None),
            P("tile", "member", None),
            P("tile", "member"),
        ),
        out_specs=P("member", None, "tile", None),
        check_vma=False,
    )
```

```python
import functools
import math

import jax
import jax.numpy as jnp
import numpy as np
from jax import lax
from jax.experimental import pallas as pl
from jax.experimental.pallas import tpu as pltpu
from jax.sharding import PartitionSpec as P

MEMBERS = 48
UPPER = 8
LANES = 128
SLOTS = 256
RADIUS = 8
BLOCK = 4
CHUNK = 16
GROUPS = LANES // CHUNK
BLOCKS_Y = LANES // BLOCK
ROWS = 64
PACK = 56
DOMS = 16
F32 = jnp.float32
BF16 = jnp.bfloat16


def split3(x):
    hi = x.astype(BF16)
    rest = x - hi.astype(F32)
    mid = rest.astype(BF16)
    low = (rest - mid.astype(F32)).astype(BF16)
    return hi, mid, low


def split2(x):
    hi = x.astype(BF16)
    return hi, (x - hi.astype(F32)).astype(BF16)


def nt(a, b):
    return lax.dot_general(a, b, (((1,), (1,)), ((), ())), preferred_element_type=F32)


def nn(a, b):
    return lax.dot_general(a, b, (((1,), (0,)), ((), ())), preferred_element_type=F32)


def row_spread():
    m = np.zeros((64, 48), np.float32)
    for x in range(8):
        for r in range(6):
            m[x * 8 + r, r * 8 + x] = 1.0
    return m


def row_compact():
    m = np.zeros((ROWS, 80), np.float32)
    for v in range(9):
        for r in range(6):
            m[v * 6 + r, v * 8 + r] = 1.0
    for r in range(6):
        m[54 + r, 72 + r] = 1.0
    return m


def row_sample():
    m = np.zeros((9 * PACK, DOMS * ROWS), np.float32)
    for v in range(9):
        for i in range(MEMBERS):
            for layer in range(2):
                m[v * PACK + i, (i // 3) * ROWS + v * 6 + (i % 3) * 2 + layer] = 0.5
    for s in range(DOMS):
        for r in range(3):
            m[8 * PACK + 48, s * ROWS + 54 + r] = 1.0
            m[8 * PACK + 49, s * ROWS + 57 + r] = 1.0
    return m


OFFSETS = (10, 14, 2, 6)
MEAN_ROW = 672
FIX_ROW = 720
WEIGHT_ROWS = 744


def first_row(t):
    panel = t // 4
    return 16 * panel * (panel + 1) + (t % 4) * 8 * (panel + 1)


def taper_rows():
    lane = np.arange(LANES)
    x, y = lane // CHUNK, lane % CHUNK
    t = np.zeros((24, LANES), np.float32)
    for k, o in enumerate(OFFSETS):
        gap_y = np.where(y >= o, y - o, y - o + CHUNK) - 6 - 1.5
        for seg in range(3):
            for p in range(2):
                gap_x = (seg - 1) * 8 + x - (4 * p + 1.5)
                s = gap_x * gap_x + gap_y * gap_y
                t[(k * 3 + seg) * 2 + p] = np.where(s < RADIUS * RADIUS, (1 - s / 64.0) ** 2, 0.0)
    return t


def taper_table():
    base = taper_rows().reshape(4, 3, 2, LANES)
    table = np.zeros((4, 4, 3, 2, LANES), np.float32)
    for odd in range(2):
        for edge in range(2):
            t = table[2 * odd + edge]
            t[:, 0] = base[:, 0 if odd else 2]
            t[:, 1] = base[:, 1]
            t[:, 2] = 0.0 if edge else base[:, 2 if odd else 0]
    return table.reshape(96, LANES)


def expand_rows():
    m = np.zeros((128, 512), np.float32)
    for h in range(2):
        for p in range(2):
            for y in range(128):
                m[p * 64 + h * 32 + y // 4, h * 256 + p * 128 + y] = 1.0
    return np.concatenate([m, m], 0)


def pack_kernel(where, tally, x_ref, reading, error, cell, spread, compact, out, own, work):
    me = where[0]
    live = lax.broadcasted_iota(jnp.int32, (1, SLOTS), 1) < tally[0]
    prec = jnp.where(live, 1.0 / error[...], 0.0)
    vals = jnp.where(live, prec * reading[...], 0.0)
    c = cell[...]
    x, y = c // LANES, c % LANES
    group = y // CHUNK
    lane = x * CHUNK + y % CHUNK
    hit = lax.broadcasted_iota(jnp.int32, (8, SLOTS), 0) == group
    spot = (lax.broadcasted_iota(jnp.int32, (LANES, SLOTS), 0) == lane).astype(F32).astype(BF16)
    pv = jnp.concatenate([jnp.where(hit, prec, 0.0), jnp.where(hit, vals, 0.0)], 0)
    a, b, d = split3(pv)
    pv = nt(a, spot) + nt(b, spot) + nt(d, spot)
    own[...] = pv
    sub = lax.broadcasted_iota(jnp.int32, (8, LANES), 0)
    col = lax.broadcasted_iota(jnp.int32, (8, LANES), 1)
    high = (col % CHUNK) >= 8

    def edge(g):
        res = jnp.zeros((8, LANES), F32)
        for n in range(2):
            parts = split3(jnp.broadcast_to(pv[n * 8 + g : n * 8 + g + 1, :], (8, LANES)))
            for k in range(3):
                res = jnp.where(sub == n * 3 + k, parts[k].astype(F32), res)
        return res

    last = jnp.where(high, edge(7), 0.0)
    first = jnp.where(high, 0.0, edge(0))

    flat = x_ref[...].reshape(48, 16 * LANES)
    rows = nn(spread[...], flat)
    for d in range(DOMS):
        v = [rows[8 * k : 8 * k + 8, d * LANES : (d + 1) * LANES] for k in range(8)]
        for step in (4, 2, 1):
            width = step * CHUNK
            low = ((col // width) % 2) == 0
            new = list(v)
            for k in range(8):
                if not k & step:
                    a, b = v[k], v[k + step]
                    new[k] = jnp.where(low, a, pltpu.roll(b, width, 1))
                    new[k + step] = jnp.where(low, pltpu.roll(a, LANES - width, 1), b)
            v = new
        for k in range(8):
            work[d, 8 * k : 8 * k + 8, :] = v[k]
    for d in range(DOMS):
        left = work[(d - 1) % DOMS, 56:64, :]
        right = work[(d + 1) % DOMS, 0:8, :]
        work[d, 64:72, :] = jnp.where(high, left, right)
        work[d, 72:80, :] = jnp.where(
            me == d - 1, last, jnp.where(me == d + 1, first, jnp.zeros_like(first))
        )
    for d in range(DOMS):
        out[d] = nn(compact[...], work[d].astype(BF16)).astype(BF16)


def sample_kernel(r_ref, own, choose, out):
    pv = own[...]
    res = nn(choose[...], r_ref[...].reshape(DOMS * ROWS, LANES))
    for v in range(9):
        s = res[v * PACK : v * PACK + MEMBERS]
        mean = jnp.sum(s, axis=0, keepdims=True) * (1.0 / MEMBERS)
        if v < 8:
            prec, vals = pv[v : v + 1], pv[8 + v : 9 + v]
        else:
            prec, vals = res[v * PACK + 48 : v * PACK + 49], res[v * PACK + 49 : v * PACK + 50]
        out[v, 0:48, :] = s - mean
        sub = lax.broadcasted_iota(jnp.int32, (8, LANES), 0)
        out[v, 48:56, :] = jnp.where(
            sub == 0, prec, jnp.where(sub == 1, vals - prec * mean, 0.0)
        )


def gram_products(segs, taper):
    lane = lax.broadcasted_iota(jnp.int32, (1, LANES), 1) % CHUNK
    first = lax.broadcasted_iota(jnp.int32, (16, LANES), 0) == 0
    for g in range(GROUPS):
        for k, o in enumerate(OFFSETS):
            v0 = g - 1 if k < 2 else g
            v1 = v0 + 1
            v0, v1 = (8 if v in (-1, 8) else v for v in (v0, v1))
            mask = lane >= o
            shi, slo, whi, wlo = [], [], [], []
            for s, ref in segs:
                w = jnp.where(mask, ref[v0], ref[v1])
                a = w[0:48]
                prec, drv = w[48:49], w[49:50]
                row = (k * 3 + s) * 2
                stream = jnp.concatenate([a * prec, jnp.where(first, drv, 0.0)], 0)
                h, l = split2(stream)
                shi.append(h)
                slo.append(l)
                h, l = split2(
                    jnp.concatenate([a * taper[row : row + 1], a * taper[row + 1 : row + 2]], 0)
                )
                whi.append(h)
                wlo.append(l)
            stream = jnp.concatenate(
                [jnp.concatenate(shi + shi, 1), jnp.concatenate(slo + slo, 1)], 0
            )
            res = nt(stream, jnp.concatenate(whi + wlo, 1))
            res = res[0:56] + res[64:120]
            res = jnp.concatenate([res, jnp.zeros((56, LANES - 2 * MEMBERS), F32)], 1)
            yield g * 4 + k, res


def pick_taper(tile, taper):
    place = tile[0]
    edge = jnp.logical_or(place == 0, place == 15).astype(jnp.int32)
    variant = 2 * (place % 2) + edge
    return taper[pl.ds(pl.multiple_of(variant * 24, 8), 24), :]


def near_kernel(tile, own, pair, taper, out):
    for q, res in gram_products([(0, pair), (1, own)], pick_taper(tile, taper)):
        out[q * PACK : (q + 1) * PACK, :] = res


def solve_kernel(tile, following, partial, taper, out, grams, mat, piv, fac):
    for q, res in gram_products([(2, following)], pick_taper(tile, taper)):
        grams[q * PACK : (q + 1) * PACK, :] = partial[q * PACK : (q + 1) * PACK, :] + res

    sub = lax.broadcasted_iota(jnp.int32, (8, LANES), 0)
    half = (lax.broadcasted_iota(jnp.int32, (8, LANES), 1) // 32) % 2
    half0 = half == 0
    low = lax.broadcasted_iota(jnp.int32, (48, LANES), 1) < 64

    def columns(js):
        t = jnp.concatenate([grams[pl.ds(j, 32, stride=PACK), :] for j in js], 0).T
        return t[0:48], t[48:96]

    for j in range(12):
        t0, t1 = columns(range(4 * j, 4 * j + 4))
        mat[2 * j] = jnp.where(low, t0, pltpu.roll(t1, 64, 1))
        mat[2 * j + 1] = jnp.where(low, pltpu.roll(t0, 64, 1), t1)
    t0, t1 = columns([48] * 4)
    drive = jnp.where(low, t0, t1)
    drive = [drive[8 * j : 8 * j + 8] for j in range(6)]

    def bcast(x, k):
        return jnp.broadcast_to(x[k : k + 1, :], (8, LANES))

    def both(x, h):
        return jnp.where(half == h, x, pltpu.roll(x, 32 if h == 0 else 96, 1))

    scale = []
    for panel in range(6):
        buf = panel % 2
        others = [j for j in range(6) if j != panel]
        rows = [
            [mat[4 * panel + n, 8 * j : 8 * j + 8, :] for j in range(6)] for n in range(4)
        ]
        d = [both(rows[r // 2][panel], r % 2) for r in range(8)]
        d = [jnp.where(sub == r, d[r] + (MEMBERS - 1.0), d[r]) for r in range(8)]
        invs, fds = [], []
        for k in range(8):
            inv = 1.0 / bcast(d[k], k)
            invs.append(inv)
            scale.append(jnp.sqrt((MEMBERS - 1.0) * inv[0:1, :]))
            here = sub == k
            row = jnp.where(here, 1.0, d[k])
            for r in range(k + 1, 8):
                d[r] = jnp.where(here, 0.0, d[r]) - (bcast(d[k], r) * inv) * row
            fd = bcast(drive[panel], k) * inv
            fds.append(fd)
            drive[panel] = jnp.where(here, 0.0, drive[panel]) - fd * row
            d[k] = jnp.where(sub <= k, row, 0.0)
            piv[buf, k, 8 * panel : 8 * panel + 8, :] = d[k]
        for n in range(4):
            mat[4 * panel + n, 8 * panel : 8 * panel + 8, :] = jnp.where(
                half0, d[2 * n], d[2 * n + 1]
            )
        eb = [[bcast(d[r], c) for c in range(r)] for r in range(8)]
        for j in others:
            x = [both(rows[r // 2][j], r % 2) for r in range(8)]
            y = []
            for r in range(8):
                t = x[r]
                for c in range(r):
                    t = t + eb[r][c] * x[c]
                y.append(t)
                piv[buf, r, 8 * j : 8 * j + 8, :] = t
                if j > panel:
                    fac[buf, r, 8 * j : 8 * j + 8, :] = t * invs[r]
                drive[j] = drive[j] - fds[r] * t
            if j < panel:
                for n in range(4):
                    mat[4 * panel + n, 8 * j : 8 * j + 8, :] = jnp.where(
                        half0, y[2 * n], y[2 * n + 1]
                    )
        for block in range(panel + 1, 6):
            js = list(range(panel + 1)) + list(range(block, 6))
            acc = [
                {
                    j: jnp.zeros((8, LANES), F32)
                    if j == panel
                    else mat[4 * block + n, 8 * j : 8 * j + 8, :]
                    for j in js
                }
                for n in range(4)
            ]
            for k in range(8):
                pr = {j: piv[buf, k, 8 * j : 8 * j + 8, :] for j in js}
                for n in range(4):
                    i = 8 * block + 2 * n
                    fa = jnp.broadcast_to(fac[buf, k, i : i + 1, :], (8, LANES))
                    fb = jnp.broadcast_to(fac[buf, k, i + 1 : i + 2, :], (8, LANES))
                    fp = jnp.where(half0, fa, fb)
                    for j in js:
                        acc[n][j] = acc[n][j] - fp * pr[j]
            for n in range(4):
                for j in js:
                    mat[4 * block + n, 8 * j : 8 * j + 8, :] = acc[n][j]

    mean = [-x for x in drive]
    mean_total = mean[0] + mean[1] + mean[2] + mean[3] + mean[4] + mean[5]
    for j in range(6):
        out[MEAN_ROW + 8 * j : MEAN_ROW + 8 * j + 8, :] = mean[j]
    for t in range(24):
        panel = t // 4
        base = first_row(t)
        sc = jnp.where(half0, scale[2 * t], scale[2 * t + 1])
        total = mean_total
        for j in range(panel + 1):
            x = sc * mat[t, 8 * j : 8 * j + 8, :]
            out[base + 8 * j : base + 8 * j + 8, :] = x
            total = total + x
        total = jnp.sum(total, axis=0, keepdims=True)
        out[FIX_ROW + t : FIX_ROW + t + 1, :] = (1.0 - total) * (1.0 / MEMBERS)


def transform_kernel(w_ref, x_ref, expand, out, wide, xs, base):
    hi, low = split2(w_ref[...])
    wide[...] = nn(jnp.concatenate([hi, low], 1), expand[...])
    for i in range(MEMBERS):
        for l in range(8):
            xs[i, l] = x_ref[i, l].astype(F32)
    top = lax.broadcasted_iota(jnp.int32, (8, LANES), 0) < 4

    def weights(r, halves):
        line = wide[pl.ds(r, 1), :]
        res = []
        for h in range(halves):
            a = jnp.broadcast_to(line[:, h * 256 : h * 256 + 128], (8, LANES))
            b = jnp.broadcast_to(line[:, h * 256 + 128 : h * 256 + 256], (8, LANES))
            res.append(jnp.where(top, a, b))
        return res

    def common(i, acc):
        acc = list(acc)
        for u in range(16):
            w = weights(MEAN_ROW + i * 16 + u, 1)[0]
            for l in range(8):
                x = xs[i * 16 + u, l]
                acc[l] = acc[l] + x * w
                acc[8 + l] = acc[8 + l] + x
        return tuple(acc)

    zeros = tuple(jnp.zeros((8, LANES), F32) for _ in range(16))
    acc = lax.fori_loop(0, 3, common, zeros)
    for l in range(8):
        base[l] = acc[l]
        base[8 + l] = acc[8 + l]

    for panel, step in enumerate((8, 16, 24, 16, 20, 24)):
        count = 8 * (panel + 1)

        def pair(n, c, panel=panel, step=step, count=count):
            t = 4 * panel + n
            row = first_row(4 * panel) + n * count
            fix = weights(FIX_ROW + t, 2)

            def some(i, acc):
                acc = list(acc)
                for u in range(step):
                    w = weights(row + i * step + u, 2)
                    for l in range(8):
                        x = xs[i * step + u, l]
                        acc[l] = acc[l] + x * w[0]
                        acc[8 + l] = acc[8 + l] + x * w[1]
                return tuple(acc)

            acc = tuple(base[l] + base[8 + l] * fix[h] for h in range(2) for l in range(8))
            acc = lax.fori_loop(0, count // step, some, acc)
            for h in range(2):
                for l in range(8):
                    out[2 * t + h, l] = acc[8 * h + l].astype(BF16)
            return c

        lax.fori_loop(0, 4, pair, 0)


def send_kernel(x_ref, out, lower):
    for d in range(DOMS):
        out[d, 0] = x_ref[0, 0:UPPER, :, d * LANES : (d + 1) * LANES]
    lower[...] = x_ref[:, UPPER : 2 * UPPER]


def finish_kernel(b_ref, partial, out, work, sems):
    del partial
    copies = []
    for m in range(3):
        for d in range(DOMS):
            work[m, :, :, d * LANES : (d + 1) * LANES] = b_ref[d, m]
        copy = pltpu.make_async_copy(work.at[m], out.at[m, 0:UPPER], sems.at[m])
        copy.start()
        copies.append(copy)
    for copy in copies:
        copy.wait()


VM = pl.BlockSpec(memory_space=pltpu.VMEM)
SM = pl.BlockSpec(memory_space=pltpu.SMEM)
ANY = pl.BlockSpec(memory_space=pl.ANY)
FULL = pltpu.CompilerParams(vmem_limit_bytes=62000000)
LIMIT = pltpu.CompilerParams(vmem_limit_bytes=48 * 2**20)


def body(prior, reading, error, cell, tally):
    me = lax.axis_index("member").astype(jnp.int32).reshape(1)
    tile = lax.axis_index("tile").astype(jnp.int32).reshape(1)
    const = lambda a, t: jnp.asarray(a, t)
    whole = lambda *shape: pl.BlockSpec(shape, lambda g: (0,) * len(shape))
    packed, own = pl.pallas_call(
        pack_kernel,
        grid=(1,),
        in_specs=[
            SM,
            SM,
            whole(3, 2, 8, 2048),
            whole(1, SLOTS),
            whole(1, SLOTS),
            whole(1, SLOTS),
            whole(64, 48),
            whole(ROWS, 80),
        ],
        out_specs=[VM, VM],
        out_shape=[
            jax.ShapeDtypeStruct((DOMS, ROWS, LANES), BF16),
            jax.ShapeDtypeStruct((16, LANES), F32),
        ],
        scratch_shapes=[pltpu.VMEM((DOMS, 80, LANES), F32)],
        compiler_params=FULL,
        name="pack",
    )(
        me,
        tally.reshape(1),
        prior,
        reading.reshape(1, SLOTS),
        error.reshape(1, SLOTS),
        cell.reshape(1, SLOTS),
        const(row_spread(), BF16),
        const(row_compact(), BF16),
    )
    fields, partial = pl.pallas_call(
        send_kernel,
        grid=(3,),
        in_specs=[pl.BlockSpec((1, 2 * UPPER, 8, 2048), lambda g: (g, 0, 0, 0))],
        out_specs=[
            pl.BlockSpec((DOMS, 1, UPPER, 8, LANES), lambda g: (0, g, 0, 0, 0)),
            pl.BlockSpec((1, UPPER, 8, 2048), lambda g: (g, 1, 0, 0)),
        ],
        out_shape=[
            jax.ShapeDtypeStruct((DOMS, 3, UPPER, 8, LANES), BF16),
            jax.ShapeDtypeStruct(prior.shape, BF16),
        ],
        compiler_params=FULL,
        name="send",
    )(prior)
    packed = lax.all_to_all(packed, "member", 0, 0, tiled=True)
    fields = lax.all_to_all(
        fields.reshape(MEMBERS, UPPER, 8, LANES), "member", 0, 0, tiled=True
    )
    sampled = pl.pallas_call(
        sample_kernel,
        in_specs=[VM, VM, VM],
        out_specs=VM,
        out_shape=jax.ShapeDtypeStruct((9, PACK, LANES), F32),
        compiler_params=LIMIT,
        name="sample",
    )(packed, own, const(row_sample(), BF16))
    tiles = lax.axis_size("tile")
    pair = lax.ppermute(sampled, "tile", [(i, i ^ 1) for i in range(tiles)])
    following = lax.ppermute(
        sampled, "tile", [(i, (i + 1 if i % 2 else i - 1) % tiles) for i in range(tiles)]
    )
    table = const(taper_table(), F32)
    partial_gram = pl.pallas_call(
        near_kernel,
        in_specs=[SM, VM, VM, VM],
        out_specs=VM,
        out_shape=jax.ShapeDtypeStruct((BLOCKS_Y * PACK, LANES), F32),
        compiler_params=LIMIT,
        cost_estimate=pl.CostEstimate(flops=10**9, bytes_accessed=3 * 10**6, transcendentals=0),
        name="near_gram",
    )(tile, sampled, pair, table)
    weights = pl.pallas_call(
        solve_kernel,
        in_specs=[SM, VM, VM, VM],
        out_specs=VM,
        out_shape=jax.ShapeDtypeStruct((WEIGHT_ROWS, LANES), F32),
        scratch_shapes=[
            pltpu.VMEM((BLOCKS_Y * PACK + 64, LANES), F32),
            pltpu.VMEM((24, 48, LANES), F32),
            pltpu.VMEM((2, 8, 48, LANES), F32),
            pltpu.VMEM((2, 8, 48, LANES), F32),
        ],
        compiler_params=LIMIT,
        name="solve",
    )(tile, following, partial_gram, table)
    result = pl.pallas_call(
        transform_kernel,
        in_specs=[VM, VM, VM],
        out_specs=VM,
        out_shape=jax.ShapeDtypeStruct((MEMBERS, UPPER, 8, LANES), BF16),
        scratch_shapes=[
            pltpu.VMEM((WEIGHT_ROWS, 512), F32),
            pltpu.VMEM((MEMBERS, UPPER, 8, LANES), F32),
            pltpu.VMEM((16, 8, LANES), F32),
        ],
        compiler_params=LIMIT,
        name="transform",
    )(weights, fields, const(expand_rows(), BF16))
    result = lax.all_to_all(result, "member", 0, 0, tiled=True)
    return pl.pallas_call(
        finish_kernel,
        in_specs=[VM, ANY],
        out_specs=ANY,
        out_shape=jax.ShapeDtypeStruct(prior.shape, BF16),
        scratch_shapes=[
            pltpu.VMEM((3, UPPER, 8, 2048), BF16),
            pltpu.SemaphoreType.DMA((3,)),
        ],
        input_output_aliases={1: 0},
        compiler_params=LIMIT,
        name="finish",
    )(result.reshape(DOMS, 3, UPPER, 8, LANES), partial)


def solution(mesh):
    return jax.shard_map(
        body,
        mesh=mesh,
        in_specs=(
            P("member", None, "tile", None),
            P("tile", "member", None),
            P("tile", "member", None),
            P("tile", "member", None),
            P("tile", "member"),
        ),
        out_specs=P("member", None, "tile", None),
        check_vma=False,
    )
```

```python
import functools
import math

import jax
import jax.numpy as jnp
import numpy as np
from jax import lax
from jax.experimental import pallas as pl
from jax.experimental.pallas import tpu as pltpu
from jax.sharding import PartitionSpec as P

MEMBERS = 48
UPPER = 8
LANES = 128
SLOTS = 256
RADIUS = 8
BLOCK = 4
CHUNK = 16
GROUPS = LANES // CHUNK
BLOCKS_Y = LANES // BLOCK
ROWS = 64
PACK = 56
DOMS = 16
F32 = jnp.float32
BF16 = jnp.bfloat16


def split3(x):
    hi = x.astype(BF16)
    rest = x - hi.astype(F32)
    mid = rest.astype(BF16)
    low = (rest - mid.astype(F32)).astype(BF16)
    return hi, mid, low


def split2(x):
    hi = x.astype(BF16)
    return hi, (x - hi.astype(F32)).astype(BF16)


def nt(a, b):
    return lax.dot_general(a, b, (((1,), (1,)), ((), ())), preferred_element_type=F32)


def nn(a, b):
    return lax.dot_general(a, b, (((1,), (0,)), ((), ())), preferred_element_type=F32)


def row_spread():
    m = np.zeros((64, 48), np.float32)
    for x in range(8):
        for r in range(6):
            m[x * 8 + r, r * 8 + x] = 1.0
    return m


def row_compact():
    m = np.zeros((ROWS, 80), np.float32)
    for v in range(9):
        for r in range(6):
            m[v * 6 + r, v * 8 + r] = 1.0
    for r in range(6):
        m[54 + r, 72 + r] = 1.0
    return m


def row_sample():
    m = np.zeros((9 * PACK, DOMS * ROWS), np.float32)
    for v in range(9):
        for i in range(MEMBERS):
            for layer in range(2):
                m[v * PACK + i, (i // 3) * ROWS + v * 6 + (i % 3) * 2 + layer] = 0.5
    for s in range(DOMS):
        for r in range(3):
            m[8 * PACK + 48, s * ROWS + 54 + r] = 1.0
            m[8 * PACK + 49, s * ROWS + 57 + r] = 1.0
    return m


OFFSETS = (10, 14, 2, 6)
MEAN_ROW = 672
FIX_ROW = 720
WEIGHT_ROWS = 744


def first_row(t):
    panel = t // 4
    return 16 * panel * (panel + 1) + (t % 4) * 8 * (panel + 1)


def taper_rows():
    lane = np.arange(LANES)
    x, y = lane // CHUNK, lane % CHUNK
    t = np.zeros((24, LANES), np.float32)
    for k, o in enumerate(OFFSETS):
        gap_y = np.where(y >= o, y - o, y - o + CHUNK) - 6 - 1.5
        for seg in range(3):
            for p in range(2):
                gap_x = (seg - 1) * 8 + x - (4 * p + 1.5)
                s = gap_x * gap_x + gap_y * gap_y
                t[(k * 3 + seg) * 2 + p] = np.where(s < RADIUS * RADIUS, (1 - s / 64.0) ** 2, 0.0)
    return t


def taper_table():
    base = taper_rows().reshape(4, 3, 2, LANES)
    table = np.zeros((4, 4, 3, 2, LANES), np.float32)
    for odd in range(2):
        for edge in range(2):
            t = table[2 * odd + edge]
            t[:, 0] = base[:, 0 if odd else 2]
            t[:, 1] = base[:, 1]
            t[:, 2] = 0.0 if edge else base[:, 2 if odd else 0]
    return table.reshape(96, LANES)


def expand_rows():
    m = np.zeros((128, 512), np.float32)
    for h in range(2):
        for p in range(2):
            for y in range(128):
                m[p * 64 + h * 32 + y // 4, h * 256 + p * 128 + y] = 1.0
    return np.concatenate([m, m], 0)


def pack_kernel(where, tally, x_ref, reading, error, cell, spread, compact, out, own, work, chunk, sems):
    me = where[0]
    live = lax.broadcasted_iota(jnp.int32, (1, SLOTS), 1) < tally[0]
    prec = jnp.where(live, 1.0 / error[...], 0.0)
    vals = jnp.where(live, prec * reading[...], 0.0)
    c = cell[...]
    x, y = c // LANES, c % LANES
    group = y // CHUNK
    lane = x * CHUNK + y % CHUNK
    hit = lax.broadcasted_iota(jnp.int32, (8, SLOTS), 0) == group
    spot = (lax.broadcasted_iota(jnp.int32, (LANES, SLOTS), 0) == lane).astype(F32).astype(BF16)
    pv = jnp.concatenate([jnp.where(hit, prec, 0.0), jnp.where(hit, vals, 0.0)], 0)
    a, b, d = split3(pv)
    pv = nt(a, spot) + nt(b, spot) + nt(d, spot)
    own[...] = pv
    sub = lax.broadcasted_iota(jnp.int32, (8, LANES), 0)
    col = lax.broadcasted_iota(jnp.int32, (8, LANES), 1)
    high = (col % CHUNK) >= 8

    def edge(g):
        res = jnp.zeros((8, LANES), F32)
        for n in range(2):
            parts = split3(jnp.broadcast_to(pv[n * 8 + g : n * 8 + g + 1, :], (8, LANES)))
            for k in range(3):
                res = jnp.where(sub == n * 3 + k, parts[k].astype(F32), res)
        return res

    last = jnp.where(high, edge(7), 0.0)
    first = jnp.where(high, 0.0, edge(0))

    flat = x_ref[...].reshape(48, 16 * LANES)
    rows = nn(spread[...], flat)
    for d in range(DOMS):
        v = [rows[8 * k : 8 * k + 8, d * LANES : (d + 1) * LANES] for k in range(8)]
        for step in (4, 2, 1):
            width = step * CHUNK
            low = ((col // width) % 2) == 0
            new = list(v)
            for k in range(8):
                if not k & step:
                    a, b = v[k], v[k + step]
                    new[k] = jnp.where(low, a, pltpu.roll(b, width, 1))
                    new[k + step] = jnp.where(low, pltpu.roll(a, LANES - width, 1), b)
            v = new
        for k in range(8):
            work[d, 8 * k : 8 * k + 8, :] = v[k]
    for d in range(DOMS):
        left = work[(d - 1) % DOMS, 56:64, :]
        right = work[(d + 1) % DOMS, 0:8, :]
        work[d, 64:72, :] = jnp.where(high, left, right)
        work[d, 72:80, :] = jnp.where(
            me == d - 1, last, jnp.where(me == d + 1, first, jnp.zeros_like(first))
        )
    copies = []
    for d in range(DOMS):
        chunk[d] = nn(compact[...], work[d].astype(BF16)).astype(BF16)
        copy = pltpu.make_async_copy(chunk.at[d], out.at[d], sems.at[d])
        copy.start()
        copies.append(copy)
    for copy in copies:
        copy.wait()


def sample_kernel(r_ref, own, choose, out):
    pv = own[...]
    res = nn(choose[...], r_ref[...].reshape(DOMS * ROWS, LANES))
    for v in range(9):
        s = res[v * PACK : v * PACK + MEMBERS]
        mean = jnp.sum(s, axis=0, keepdims=True) * (1.0 / MEMBERS)
        if v < 8:
            prec, vals = pv[v : v + 1], pv[8 + v : 9 + v]
        else:
            prec, vals = res[v * PACK + 48 : v * PACK + 49], res[v * PACK + 49 : v * PACK + 50]
        out[v, 0:48, :] = s - mean
        sub = lax.broadcasted_iota(jnp.int32, (8, LANES), 0)
        out[v, 48:56, :] = jnp.where(
            sub == 0, prec, jnp.where(sub == 1, vals - prec * mean, 0.0)
        )


def gram_products(segs, taper):
    lane = lax.broadcasted_iota(jnp.int32, (1, LANES), 1) % CHUNK
    first = lax.broadcasted_iota(jnp.int32, (16, LANES), 0) == 0
    for g in range(GROUPS):
        for k, o in enumerate(OFFSETS):
            v0 = g - 1 if k < 2 else g
            v1 = v0 + 1
            v0, v1 = (8 if v in (-1, 8) else v for v in (v0, v1))
            mask = lane >= o
            shi, slo, whi, wlo = [], [], [], []
            for s, ref in segs:
                w = jnp.where(mask, ref[v0], ref[v1])
                a = w[0:48]
                prec, drv = w[48:49], w[49:50]
                row = (k * 3 + s) * 2
                stream = jnp.concatenate([a * prec, jnp.where(first, drv, 0.0)], 0)
                h, l = split2(stream)
                shi.append(h)
                slo.append(l)
                h, l = split2(
                    jnp.concatenate([a * taper[row : row + 1], a * taper[row + 1 : row + 2]], 0)
                )
                whi.append(h)
                wlo.append(l)
            stream = jnp.concatenate(
                [jnp.concatenate(shi + shi, 1), jnp.concatenate(slo + slo, 1)], 0
            )
            res = nt(stream, jnp.concatenate(whi + wlo, 1))
            res = res[0:56] + res[64:120]
            res = jnp.concatenate([res, jnp.zeros((56, LANES - 2 * MEMBERS), F32)], 1)
            yield g * 4 + k, res


def pick_taper(tile, taper):
    place = tile[0]
    edge = jnp.logical_or(place == 0, place == 15).astype(jnp.int32)
    variant = 2 * (place % 2) + edge
    return taper[pl.ds(pl.multiple_of(variant * 24, 8), 24), :]


def near_kernel(tile, own, pair, taper, out):
    for q, res in gram_products([(0, pair), (1, own)], pick_taper(tile, taper)):
        out[q * PACK : (q + 1) * PACK, :] = res


def solve_kernel(tile, following, partial, taper, out, grams, mat, piv, fac):
    for q, res in gram_products([(2, following)], pick_taper(tile, taper)):
        grams[q * PACK : (q + 1) * PACK, :] = partial[q * PACK : (q + 1) * PACK, :] + res

    sub = lax.broadcasted_iota(jnp.int32, (8, LANES), 0)
    half = (lax.broadcasted_iota(jnp.int32, (8, LANES), 1) // 32) % 2
    half0 = half == 0
    low = lax.broadcasted_iota(jnp.int32, (48, LANES), 1) < 64

    def columns(js):
        t = jnp.concatenate([grams[pl.ds(j, 32, stride=PACK), :] for j in js], 0).T
        return t[0:48], t[48:96]

    for j in range(12):
        t0, t1 = columns(range(4 * j, 4 * j + 4))
        mat[2 * j] = jnp.where(low, t0, pltpu.roll(t1, 64, 1))
        mat[2 * j + 1] = jnp.where(low, pltpu.roll(t0, 64, 1), t1)
    t0, t1 = columns([48] * 4)
    drive = jnp.where(low, t0, t1)
    drive = [drive[8 * j : 8 * j + 8] for j in range(6)]

    def bcast(x, k):
        return jnp.broadcast_to(x[k : k + 1, :], (8, LANES))

    def both(x, h):
        return jnp.where(half == h, x, pltpu.roll(x, 32 if h == 0 else 96, 1))

    scale = []
    for panel in range(6):
        buf = panel % 2
        others = [j for j in range(6) if j != panel]
        rows = [
            [mat[4 * panel + n, 8 * j : 8 * j + 8, :] for j in range(6)] for n in range(4)
        ]
        d = [both(rows[r // 2][panel], r % 2) for r in range(8)]
        d = [jnp.where(sub == r, d[r] + (MEMBERS - 1.0), d[r]) for r in range(8)]
        invs, fds = [], []
        for k in range(8):
            inv = 1.0 / bcast(d[k], k)
            invs.append(inv)
            scale.append(jnp.sqrt((MEMBERS - 1.0) * inv[0:1, :]))
            here = sub == k
            row = jnp.where(here, 1.0, d[k])
            for r in range(k + 1, 8):
                d[r] = jnp.where(here, 0.0, d[r]) - (bcast(d[k], r) * inv) * row
            fd = bcast(drive[panel], k) * inv
            fds.append(fd)
            drive[panel] = jnp.where(here, 0.0, drive[panel]) - fd * row
            d[k] = jnp.where(sub <= k, row, 0.0)
            piv[buf, k, 8 * panel : 8 * panel + 8, :] = d[k]
        for n in range(4):
            mat[4 * panel + n, 8 * panel : 8 * panel + 8, :] = jnp.where(
                half0, d[2 * n], d[2 * n + 1]
            )
        eb = [[bcast(d[r], c) for c in range(r)] for r in range(8)]
        for j in others:
            x = [both(rows[r // 2][j], r % 2) for r in range(8)]
            y = []
            for r in range(8):
                t = x[r]
                for c in range(r):
                    t = t + eb[r][c] * x[c]
                y.append(t)
                piv[buf, r, 8 * j : 8 * j + 8, :] = t
                if j > panel:
                    fac[buf, r, 8 * j : 8 * j + 8, :] = t * invs[r]
                drive[j] = drive[j] - fds[r] * t
            if j < panel:
                for n in range(4):
                    mat[4 * panel + n, 8 * j : 8 * j + 8, :] = jnp.where(
                        half0, y[2 * n], y[2 * n + 1]
                    )
        for block in range(panel + 1, 6):
            js = list(range(panel + 1)) + list(range(block, 6))
            acc = [
                {
                    j: jnp.zeros((8, LANES), F32)
                    if j == panel
                    else mat[4 * block + n, 8 * j : 8 * j + 8, :]
                    for j in js
                }
                for n in range(4)
            ]
            for k in range(8):
                pr = {j: piv[buf, k, 8 * j : 8 * j + 8, :] for j in js}
                for n in range(4):
                    i = 8 * block + 2 * n
                    fa = jnp.broadcast_to(fac[buf, k, i : i + 1, :], (8, LANES))
                    fb = jnp.broadcast_to(fac[buf, k, i + 1 : i + 2, :], (8, LANES))
                    fp = jnp.where(half0, fa, fb)
                    for j in js:
                        acc[n][j] = acc[n][j] - fp * pr[j]
            for n in range(4):
                for j in js:
                    mat[4 * block + n, 8 * j : 8 * j + 8, :] = acc[n][j]

    mean = [-x for x in drive]
    mean_total = mean[0] + mean[1] + mean[2] + mean[3] + mean[4] + mean[5]
    for j in range(6):
        out[MEAN_ROW + 8 * j : MEAN_ROW + 8 * j + 8, :] = mean[j]
    for t in range(24):
        panel = t // 4
        base = first_row(t)
        sc = jnp.where(half0, scale[2 * t], scale[2 * t + 1])
        total = mean_total
        for j in range(panel + 1):
            x = sc * mat[t, 8 * j : 8 * j + 8, :]
            out[base + 8 * j : base + 8 * j + 8, :] = x
            total = total + x
        total = jnp.sum(total, axis=0, keepdims=True)
        out[FIX_ROW + t : FIX_ROW + t + 1, :] = (1.0 - total) * (1.0 / MEMBERS)


def transform_kernel(w_ref, x_ref, expand, out, wide, xs, base):
    hi, low = split2(w_ref[...])
    wide[...] = nn(jnp.concatenate([hi, low], 1), expand[...])
    for i in range(MEMBERS):
        for l in range(8):
            xs[i, l] = x_ref[i, l].astype(F32)
    top = lax.broadcasted_iota(jnp.int32, (8, LANES), 0) < 4

    def weights(r, halves):
        line = wide[pl.ds(r, 1), :]
        res = []
        for h in range(halves):
            a = jnp.broadcast_to(line[:, h * 256 : h * 256 + 128], (8, LANES))
            b = jnp.broadcast_to(line[:, h * 256 + 128 : h * 256 + 256], (8, LANES))
            res.append(jnp.where(top, a, b))
        return res

    def common(i, acc):
        acc = list(acc)
        for u in range(16):
            w = weights(MEAN_ROW + i * 16 + u, 1)[0]
            for l in range(8):
                x = xs[i * 16 + u, l]
                acc[l] = acc[l] + x * w
                acc[8 + l] = acc[8 + l] + x
        return tuple(acc)

    zeros = tuple(jnp.zeros((8, LANES), F32) for _ in range(16))
    acc = lax.fori_loop(0, 3, common, zeros)
    for l in range(8):
        base[l] = acc[l]
        base[8 + l] = acc[8 + l]

    for panel, step in enumerate((8, 16, 24, 16, 20, 24)):
        count = 8 * (panel + 1)

        def pair(n, c, panel=panel, step=step, count=count):
            t = 4 * panel + n
            row = first_row(4 * panel) + n * count
            fix = weights(FIX_ROW + t, 2)

            def some(i, acc):
                acc = list(acc)
                for u in range(step):
                    w = weights(row + i * step + u, 2)
                    for l in range(8):
                        x = xs[i * step + u, l]
                        acc[l] = acc[l] + x * w[0]
                        acc[8 + l] = acc[8 + l] + x * w[1]
                return tuple(acc)

            acc = tuple(base[l] + base[8 + l] * fix[h] for h in range(2) for l in range(8))
            acc = lax.fori_loop(0, count // step, some, acc)
            for h in range(2):
                for l in range(8):
                    out[2 * t + h, l] = acc[8 * h + l].astype(BF16)
            return c

        lax.fori_loop(0, 4, pair, 0, unroll=2)


def send_kernel(x_ref, out, lower):
    for d in range(DOMS):
        out[d, 0] = x_ref[0, 0:UPPER, :, d * LANES : (d + 1) * LANES]
    lower[...] = x_ref[:, UPPER : 2 * UPPER]


def finish_kernel(b_ref, partial, out, work, sems):
    del partial
    copies = []
    for m in range(3):
        for d in range(DOMS):
            work[m, :, :, d * LANES : (d + 1) * LANES] = b_ref[d, m]
        copy = pltpu.make_async_copy(work.at[m], out.at[m, 0:UPPER], sems.at[m])
        copy.start()
        copies.append(copy)
    for copy in copies:
        copy.wait()


VM = pl.BlockSpec(memory_space=pltpu.VMEM)
SM = pl.BlockSpec(memory_space=pltpu.SMEM)
ANY = pl.BlockSpec(memory_space=pl.ANY)
FULL = pltpu.CompilerParams(vmem_limit_bytes=62000000)
LIMIT = pltpu.CompilerParams(vmem_limit_bytes=48 * 2**20)


def body(prior, reading, error, cell, tally):
    me = lax.axis_index("member").astype(jnp.int32).reshape(1)
    tile = lax.axis_index("tile").astype(jnp.int32).reshape(1)
    const = lambda a, t: jnp.asarray(a, t)
    whole = lambda *shape: pl.BlockSpec(shape, lambda g: (0,) * len(shape))
    packed, own = pl.pallas_call(
        pack_kernel,
        grid=(1,),
        in_specs=[
            SM,
            SM,
            whole(3, 2, 8, 2048),
            whole(1, SLOTS),
            whole(1, SLOTS),
            whole(1, SLOTS),
            whole(64, 48),
            whole(ROWS, 80),
        ],
        out_specs=[ANY, VM],
        out_shape=[
            jax.ShapeDtypeStruct((DOMS, ROWS, LANES), BF16),
            jax.ShapeDtypeStruct((16, LANES), F32),
        ],
        scratch_shapes=[
            pltpu.VMEM((DOMS, 80, LANES), F32),
            pltpu.VMEM((DOMS, ROWS, LANES), BF16),
            pltpu.SemaphoreType.DMA((DOMS,)),
        ],
        compiler_params=FULL,
        name="pack",
    )(
        me,
        tally.reshape(1),
        prior,
        reading.reshape(1, SLOTS),
        error.reshape(1, SLOTS),
        cell.reshape(1, SLOTS),
        const(row_spread(), BF16),
        const(row_compact(), BF16),
    )
    fields, partial = pl.pallas_call(
        send_kernel,
        grid=(3,),
        in_specs=[pl.BlockSpec((1, 2 * UPPER, 8, 2048), lambda g: (g, 0, 0, 0))],
        out_specs=[
            pl.BlockSpec((DOMS, 1, UPPER, 8, LANES), lambda g: (0, g, 0, 0, 0)),
            pl.BlockSpec((1, UPPER, 8, 2048), lambda g: (g, 1, 0, 0)),
        ],
        out_shape=[
            jax.ShapeDtypeStruct((DOMS, 3, UPPER, 8, LANES), BF16),
            jax.ShapeDtypeStruct(prior.shape, BF16),
        ],
        compiler_params=FULL,
        name="send",
    )(prior)
    packed = lax.all_to_all(packed, "member", 0, 0, tiled=True)
    fields = lax.all_to_all(
        fields.reshape(MEMBERS, UPPER, 8, LANES), "member", 0, 0, tiled=True
    )
    sampled = pl.pallas_call(
        sample_kernel,
        in_specs=[VM, VM, VM],
        out_specs=VM,
        out_shape=jax.ShapeDtypeStruct((9, PACK, LANES), F32),
        compiler_params=LIMIT,
        name="sample",
    )(packed, own, const(row_sample(), BF16))
    tiles = lax.axis_size("tile")
    pair = lax.ppermute(sampled, "tile", [(i, i ^ 1) for i in range(tiles)])
    following = lax.ppermute(
        sampled, "tile", [(i, (i + 1 if i % 2 else i - 1) % tiles) for i in range(tiles)]
    )
    table = const(taper_table(), F32)
    partial_gram = pl.pallas_call(
        near_kernel,
        in_specs=[SM, VM, VM, VM],
        out_specs=VM,
        out_shape=jax.ShapeDtypeStruct((BLOCKS_Y * PACK, LANES), F32),
        compiler_params=LIMIT,
        cost_estimate=pl.CostEstimate(flops=10**9, bytes_accessed=3 * 10**6, transcendentals=0),
        name="near_gram",
    )(tile, sampled, pair, table)
    weights = pl.pallas_call(
        solve_kernel,
        in_specs=[SM, VM, VM, VM],
        out_specs=VM,
        out_shape=jax.ShapeDtypeStruct((WEIGHT_ROWS, LANES), F32),
        scratch_shapes=[
            pltpu.VMEM((BLOCKS_Y * PACK + 64, LANES), F32),
            pltpu.VMEM((24, 48, LANES), F32),
            pltpu.VMEM((2, 8, 48, LANES), F32),
            pltpu.VMEM((2, 8, 48, LANES), F32),
        ],
        compiler_params=LIMIT,
        name="solve",
    )(tile, following, partial_gram, table)
    result = pl.pallas_call(
        transform_kernel,
        in_specs=[VM, VM, VM],
        out_specs=VM,
        out_shape=jax.ShapeDtypeStruct((MEMBERS, UPPER, 8, LANES), BF16),
        scratch_shapes=[
            pltpu.VMEM((WEIGHT_ROWS, 512), F32),
            pltpu.VMEM((MEMBERS, UPPER, 8, LANES), F32),
            pltpu.VMEM((16, 8, LANES), F32),
        ],
        compiler_params=LIMIT,
        name="transform",
    )(weights, fields, const(expand_rows(), BF16))
    result = lax.all_to_all(result, "member", 0, 0, tiled=True)
    return pl.pallas_call(
        finish_kernel,
        in_specs=[VM, ANY],
        out_specs=ANY,
        out_shape=jax.ShapeDtypeStruct(prior.shape, BF16),
        scratch_shapes=[
            pltpu.VMEM((3, UPPER, 8, 2048), BF16),
            pltpu.SemaphoreType.DMA((3,)),
        ],
        input_output_aliases={1: 0},
        compiler_params=LIMIT,
        name="finish",
    )(result.reshape(DOMS, 3, UPPER, 8, LANES), partial)


def solution(mesh):
    return jax.shard_map(
        body,
        mesh=mesh,
        in_specs=(
            P("member", None, "tile", None),
            P("tile", "member", None),
            P("tile", "member", None),
            P("tile", "member", None),
            P("tile", "member"),
        ),
        out_specs=P("member", None, "tile", None),
        check_vma=False,
    )
```

```python
import functools
import math

import jax
import jax.numpy as jnp
import numpy as np
from jax import lax
from jax.experimental import pallas as pl
from jax.experimental.pallas import tpu as pltpu
from jax.sharding import PartitionSpec as P

MEMBERS = 48
UPPER = 8
LANES = 128
SLOTS = 256
RADIUS = 8
BLOCK = 4
CHUNK = 16
GROUPS = LANES // CHUNK
BLOCKS_Y = LANES // BLOCK
ROWS = 64
PACK = 56
DOMS = 16
F32 = jnp.float32
BF16 = jnp.bfloat16


def split3(x):
    hi = x.astype(BF16)
    rest = x - hi.astype(F32)
    mid = rest.astype(BF16)
    low = (rest - mid.astype(F32)).astype(BF16)
    return hi, mid, low


def split2(x):
    hi = x.astype(BF16)
    return hi, (x - hi.astype(F32)).astype(BF16)


def nt(a, b):
    return lax.dot_general(a, b, (((1,), (1,)), ((), ())), preferred_element_type=F32)


def nn(a, b):
    return lax.dot_general(a, b, (((1,), (0,)), ((), ())), preferred_element_type=F32)


def row_spread():
    m = np.zeros((64, 48), np.float32)
    for x in range(8):
        for r in range(6):
            m[x * 8 + r, r * 8 + x] = 1.0
    return m


def row_compact():
    m = np.zeros((ROWS, 80), np.float32)
    for v in range(9):
        for r in range(6):
            m[v * 6 + r, v * 8 + r] = 1.0
    for r in range(6):
        m[54 + r, 72 + r] = 1.0
    return m


def row_sample():
    m = np.zeros((9 * PACK, DOMS * ROWS), np.float32)
    for v in range(9):
        for i in range(MEMBERS):
            for layer in range(2):
                m[v * PACK + i, (i // 3) * ROWS + v * 6 + (i % 3) * 2 + layer] = 0.5
    for s in range(DOMS):
        for r in range(3):
            m[8 * PACK + 48, s * ROWS + 54 + r] = 1.0
            m[8 * PACK + 49, s * ROWS + 57 + r] = 1.0
    return m


OFFSETS = (10, 14, 2, 6)
MEAN_ROW = 672
FIX_ROW = 720
WEIGHT_ROWS = 744


def first_row(t):
    panel = t // 4
    return 16 * panel * (panel + 1) + (t % 4) * 8 * (panel + 1)


def taper_rows():
    lane = np.arange(LANES)
    x, y = lane // CHUNK, lane % CHUNK
    t = np.zeros((24, LANES), np.float32)
    for k, o in enumerate(OFFSETS):
        gap_y = np.where(y >= o, y - o, y - o + CHUNK) - 6 - 1.5
        for seg in range(3):
            for p in range(2):
                gap_x = (seg - 1) * 8 + x - (4 * p + 1.5)
                s = gap_x * gap_x + gap_y * gap_y
                t[(k * 3 + seg) * 2 + p] = np.where(s < RADIUS * RADIUS, (1 - s / 64.0) ** 2, 0.0)
    return t


def taper_table():
    base = taper_rows().reshape(4, 3, 2, LANES)
    table = np.zeros((4, 4, 3, 2, LANES), np.float32)
    for odd in range(2):
        for edge in range(2):
            t = table[2 * odd + edge]
            t[:, 0] = base[:, 0 if odd else 2]
            t[:, 1] = base[:, 1]
            t[:, 2] = 0.0 if edge else base[:, 2 if odd else 0]
    return table.reshape(96, LANES)


def expand_rows():
    m = np.zeros((128, 512), np.float32)
    for h in range(2):
        for p in range(2):
            for y in range(128):
                m[p * 64 + h * 32 + y // 4, h * 256 + p * 128 + y] = 1.0
    return np.concatenate([m, m], 0)


def pack_kernel(where, tally, x_ref, reading, error, cell, spread, compact, out, own, work):
    me = where[0]
    live = lax.broadcasted_iota(jnp.int32, (1, SLOTS), 1) < tally[0]
    prec = jnp.where(live, 1.0 / error[...], 0.0)
    vals = jnp.where(live, prec * reading[...], 0.0)
    c = cell[...]
    x, y = c // LANES, c % LANES
    group = y // CHUNK
    lane = x * CHUNK + y % CHUNK
    hit = lax.broadcasted_iota(jnp.int32, (8, SLOTS), 0) == group
    spot = (lax.broadcasted_iota(jnp.int32, (LANES, SLOTS), 0) == lane).astype(F32).astype(BF16)
    pv = jnp.concatenate([jnp.where(hit, prec, 0.0), jnp.where(hit, vals, 0.0)], 0)
    a, b, d = split3(pv)
    pv = nt(a, spot) + nt(b, spot) + nt(d, spot)
    own[...] = pv
    sub = lax.broadcasted_iota(jnp.int32, (8, LANES), 0)
    col = lax.broadcasted_iota(jnp.int32, (8, LANES), 1)
    high = (col % CHUNK) >= 8

    def edge(g):
        res = jnp.zeros((8, LANES), F32)
        for n in range(2):
            parts = split3(jnp.broadcast_to(pv[n * 8 + g : n * 8 + g + 1, :], (8, LANES)))
            for k in range(3):
                res = jnp.where(sub == n * 3 + k, parts[k].astype(F32), res)
        return res

    last = jnp.where(high, edge(7), 0.0)
    first = jnp.where(high, 0.0, edge(0))

    flat = x_ref[...].reshape(48, 16 * LANES)
    rows = nn(spread[...], flat)
    for d in range(DOMS):
        v = [rows[8 * k : 8 * k + 8, d * LANES : (d + 1) * LANES] for k in range(8)]
        for step in (4, 2, 1):
            width = step * CHUNK
            low = ((col // width) % 2) == 0
            new = list(v)
            for k in range(8):
                if not k & step:
                    a, b = v[k], v[k + step]
                    new[k] = jnp.where(low, a, pltpu.roll(b, width, 1))
                    new[k + step] = jnp.where(low, pltpu.roll(a, LANES - width, 1), b)
            v = new
        for k in range(8):
            work[d, 8 * k : 8 * k + 8, :] = v[k]
    for d in range(DOMS):
        left = work[(d - 1) % DOMS, 56:64, :]
        right = work[(d + 1) % DOMS, 0:8, :]
        work[d, 64:72, :] = jnp.where(high, left, right)
        work[d, 72:80, :] = jnp.where(
            me == d - 1, last, jnp.where(me == d + 1, first, jnp.zeros_like(first))
        )
    for d in range(DOMS):
        out[d] = nn(compact[...], work[d].astype(BF16)).astype(BF16)


def sample_kernel(r_ref, own, choose, out):
    pv = own[...]
    res = nn(choose[...], r_ref[...].reshape(DOMS * ROWS, LANES))
    for v in range(9):
        s = res[v * PACK : v * PACK + MEMBERS]
        mean = jnp.sum(s, axis=0, keepdims=True) * (1.0 / MEMBERS)
        if v < 8:
            prec, vals = pv[v : v + 1], pv[8 + v : 9 + v]
        else:
            prec, vals = res[v * PACK + 48 : v * PACK + 49], res[v * PACK + 49 : v * PACK + 50]
        out[v, 0:48, :] = s - mean
        sub = lax.broadcasted_iota(jnp.int32, (8, LANES), 0)
        out[v, 48:56, :] = jnp.where(
            sub == 0, prec, jnp.where(sub == 1, vals - prec * mean, 0.0)
        )


def gram_products(segs, taper):
    lane = lax.broadcasted_iota(jnp.int32, (1, LANES), 1) % CHUNK
    first = lax.broadcasted_iota(jnp.int32, (16, LANES), 0) == 0
    for g in range(GROUPS):
        for k, o in enumerate(OFFSETS):
            v0 = g - 1 if k < 2 else g
            v1 = v0 + 1
            v0, v1 = (8 if v in (-1, 8) else v for v in (v0, v1))
            mask = lane >= o
            shi, slo, whi, wlo = [], [], [], []
            for s, ref in segs:
                w = jnp.where(mask, ref[v0], ref[v1])
                a = w[0:48]
                prec, drv = w[48:49], w[49:50]
                row = (k * 3 + s) * 2
                stream = jnp.concatenate([a * prec, jnp.where(first, drv, 0.0)], 0)
                h, l = split2(stream)
                shi.append(h)
                slo.append(l)
                h, l = split2(
                    jnp.concatenate([a * taper[row : row + 1], a * taper[row + 1 : row + 2]], 0)
                )
                whi.append(h)
                wlo.append(l)
            stream = jnp.concatenate(
                [jnp.concatenate(shi + shi, 1), jnp.concatenate(slo + slo, 1)], 0
            )
            res = nt(stream, jnp.concatenate(whi + wlo, 1))
            res = res[0:56] + res[64:120]
            res = jnp.concatenate([res, jnp.zeros((56, LANES - 2 * MEMBERS), F32)], 1)
            yield g * 4 + k, res


def pick_taper(tile, taper):
    place = tile[0]
    edge = jnp.logical_or(place == 0, place == 15).astype(jnp.int32)
    variant = 2 * (place % 2) + edge
    return taper[pl.ds(pl.multiple_of(variant * 24, 8), 24), :]


def near_kernel(tile, own, pair, taper, out):
    for q, res in gram_products([(0, pair), (1, own)], pick_taper(tile, taper)):
        out[q * PACK : (q + 1) * PACK, :] = res


def solve_kernel(tile, following, partial, taper, out, grams, mat, piv, fac):
    for q, res in gram_products([(2, following)], pick_taper(tile, taper)):
        grams[q * PACK : (q + 1) * PACK, :] = partial[q * PACK : (q + 1) * PACK, :] + res

    sub = lax.broadcasted_iota(jnp.int32, (8, LANES), 0)
    half = (lax.broadcasted_iota(jnp.int32, (8, LANES), 1) // 32) % 2
    half0 = half == 0
    low = lax.broadcasted_iota(jnp.int32, (48, LANES), 1) < 64

    def columns(js):
        t = jnp.concatenate([grams[pl.ds(j, 32, stride=PACK), :] for j in js], 0).T
        return t[0:48], t[48:96]

    for j in range(12):
        t0, t1 = columns(range(4 * j, 4 * j + 4))
        mat[2 * j] = jnp.where(low, t0, pltpu.roll(t1, 64, 1))
        mat[2 * j + 1] = jnp.where(low, pltpu.roll(t0, 64, 1), t1)
    t0, t1 = columns([48] * 4)
    drive = jnp.where(low, t0, t1)
    drive = [drive[8 * j : 8 * j + 8] for j in range(6)]

    def bcast(x, k):
        return jnp.broadcast_to(x[k : k + 1, :], (8, LANES))

    def both(x, h):
        return jnp.where(half == h, x, pltpu.roll(x, 32 if h == 0 else 96, 1))

    scale = []
    for panel in range(6):
        buf = panel % 2
        others = [j for j in range(6) if j != panel]
        rows = [
            [mat[4 * panel + n, 8 * j : 8 * j + 8, :] for j in range(6)] for n in range(4)
        ]
        d = [both(rows[r // 2][panel], r % 2) for r in range(8)]
        d = [jnp.where(sub == r, d[r] + (MEMBERS - 1.0), d[r]) for r in range(8)]
        invs, fds = [], []
        for k in range(8):
            inv = 1.0 / bcast(d[k], k)
            invs.append(inv)
            scale.append(jnp.sqrt((MEMBERS - 1.0) * inv[0:1, :]))
            here = sub == k
            row = jnp.where(here, 1.0, d[k])
            for r in range(k + 1, 8):
                d[r] = jnp.where(here, 0.0, d[r]) - (bcast(d[k], r) * inv) * row
            fd = bcast(drive[panel], k) * inv
            fds.append(fd)
            drive[panel] = jnp.where(here, 0.0, drive[panel]) - fd * row
            d[k] = jnp.where(sub <= k, row, 0.0)
            piv[buf, k, 8 * panel : 8 * panel + 8, :] = d[k]
        for n in range(4):
            mat[4 * panel + n, 8 * panel : 8 * panel + 8, :] = jnp.where(
                half0, d[2 * n], d[2 * n + 1]
            )
        eb = [[bcast(d[r], c) for c in range(r)] for r in range(8)]
        for j in others:
            x = [both(rows[r // 2][j], r % 2) for r in range(8)]
            y = []
            for r in range(8):
                t = x[r]
                for c in range(r):
                    t = t + eb[r][c] * x[c]
                y.append(t)
                piv[buf, r, 8 * j : 8 * j + 8, :] = t
                if j > panel:
                    fac[buf, r, 8 * j : 8 * j + 8, :] = t * invs[r]
                drive[j] = drive[j] - fds[r] * t
            if j < panel:
                for n in range(4):
                    mat[4 * panel + n, 8 * j : 8 * j + 8, :] = jnp.where(
                        half0, y[2 * n], y[2 * n + 1]
                    )
        for block in range(panel + 1, 6):
            js = list(range(panel + 1)) + list(range(block, 6))
            acc = [
                {
                    j: jnp.zeros((8, LANES), F32)
                    if j == panel
                    else mat[4 * block + n, 8 * j : 8 * j + 8, :]
                    for j in js
                }
                for n in range(4)
            ]
            for k in range(8):
                pr = {j: piv[buf, k, 8 * j : 8 * j + 8, :] for j in js}
                for n in range(4):
                    i = 8 * block + 2 * n
                    fa = jnp.broadcast_to(fac[buf, k, i : i + 1, :], (8, LANES))
                    fb = jnp.broadcast_to(fac[buf, k, i + 1 : i + 2, :], (8, LANES))
                    fp = jnp.where(half0, fa, fb)
                    for j in js:
                        acc[n][j] = acc[n][j] - fp * pr[j]
            for n in range(4):
                for j in js:
                    mat[4 * block + n, 8 * j : 8 * j + 8, :] = acc[n][j]

    mean = [-x for x in drive]
    mean_total = mean[0] + mean[1] + mean[2] + mean[3] + mean[4] + mean[5]
    for j in range(6):
        out[MEAN_ROW + 8 * j : MEAN_ROW + 8 * j + 8, :] = mean[j]
    for t in range(24):
        panel = t // 4
        base = first_row(t)
        sc = jnp.where(half0, scale[2 * t], scale[2 * t + 1])
        total = mean_total
        for j in range(panel + 1):
            x = sc * mat[t, 8 * j : 8 * j + 8, :]
            out[base + 8 * j : base + 8 * j + 8, :] = x
            total = total + x
        total = jnp.sum(total, axis=0, keepdims=True)
        out[FIX_ROW + t : FIX_ROW + t + 1, :] = (1.0 - total) * (1.0 / MEMBERS)


def transform_kernel(w_ref, x_ref, expand, out, wide, xs, base):
    hi, low = split2(w_ref[...])
    wide[...] = nn(jnp.concatenate([hi, low], 1), expand[...])
    for i in range(MEMBERS):
        for l in range(8):
            xs[i, l] = x_ref[i, l].astype(F32)
    top = lax.broadcasted_iota(jnp.int32, (8, LANES), 0) < 4

    def weights(r, halves):
        line = wide[pl.ds(r, 1), :]
        res = []
        for h in range(halves):
            a = jnp.broadcast_to(line[:, h * 256 : h * 256 + 128], (8, LANES))
            b = jnp.broadcast_to(line[:, h * 256 + 128 : h * 256 + 256], (8, LANES))
            res.append(jnp.where(top, a, b))
        return res

    def common(i, acc):
        acc = list(acc)
        for u in range(16):
            w = weights(MEAN_ROW + i * 16 + u, 1)[0]
            for l in range(8):
                x = xs[i * 16 + u, l]
                acc[l] = acc[l] + x * w
                acc[8 + l] = acc[8 + l] + x
        return tuple(acc)

    zeros = tuple(jnp.zeros((8, LANES), F32) for _ in range(16))
    acc = lax.fori_loop(0, 3, common, zeros)
    for l in range(8):
        base[l] = acc[l]
        base[8 + l] = acc[8 + l]

    for panel, step in enumerate((8, 16, 24, 16, 20, 24)):
        count = 8 * (panel + 1)

        def pair(n, c, panel=panel, step=step, count=count):
            t = 4 * panel + n
            row = first_row(4 * panel) + n * count
            fix = weights(FIX_ROW + t, 2)

            def some(i, acc):
                acc = list(acc)
                for u in range(step):
                    w = weights(row + i * step + u, 2)
                    for l in range(8):
                        x = xs[i * step + u, l]
                        acc[l] = acc[l] + x * w[0]
                        acc[8 + l] = acc[8 + l] + x * w[1]
                return tuple(acc)

            acc = tuple(base[l] + base[8 + l] * fix[h] for h in range(2) for l in range(8))
            acc = lax.fori_loop(0, count // step, some, acc)
            for h in range(2):
                for l in range(8):
                    out[2 * t + h, l] = acc[8 * h + l].astype(BF16)
            return c

        lax.fori_loop(0, 4, pair, 0, unroll=2)


def send_kernel(x_ref, out, lower):
    for d in range(DOMS):
        out[d, 0] = x_ref[0, 0:UPPER, :, d * LANES : (d + 1) * LANES]
    lower[...] = x_ref[:, UPPER : 2 * UPPER]


def finish_kernel(b_ref, partial, out, work, sems):
    del partial
    copies = []
    for m in range(3):
        for d in range(DOMS):
            work[m, :, :, d * LANES : (d + 1) * LANES] = b_ref[d, m]
        copy = pltpu.make_async_copy(work.at[m], out.at[m, 0:UPPER], sems.at[m])
        copy.start()
        copies.append(copy)
    for copy in copies:
        copy.wait()


VM = pl.BlockSpec(memory_space=pltpu.VMEM)
SM = pl.BlockSpec(memory_space=pltpu.SMEM)
ANY = pl.BlockSpec(memory_space=pl.ANY)
FULL = pltpu.CompilerParams(vmem_limit_bytes=62000000)
LIMIT = pltpu.CompilerParams(vmem_limit_bytes=48 * 2**20)


def body(prior, reading, error, cell, tally):
    me = lax.axis_index("member").astype(jnp.int32).reshape(1)
    tile = lax.axis_index("tile").astype(jnp.int32).reshape(1)
    const = lambda a, t: jnp.asarray(a, t)
    whole = lambda *shape: pl.BlockSpec(shape, lambda g: (0,) * len(shape))
    packed, own = pl.pallas_call(
        pack_kernel,
        grid=(1,),
        in_specs=[
            SM,
            SM,
            whole(3, 2, 8, 2048),
            whole(1, SLOTS),
            whole(1, SLOTS),
            whole(1, SLOTS),
            whole(64, 48),
            whole(ROWS, 80),
        ],
        out_specs=[VM, VM],
        out_shape=[
            jax.ShapeDtypeStruct((DOMS, ROWS, LANES), BF16),
            jax.ShapeDtypeStruct((16, LANES), F32),
        ],
        scratch_shapes=[pltpu.VMEM((DOMS, 80, LANES), F32)],
        compiler_params=FULL,
        name="pack",
    )(
        me,
        tally.reshape(1),
        prior,
        reading.reshape(1, SLOTS),
        error.reshape(1, SLOTS),
        cell.reshape(1, SLOTS),
        const(row_spread(), BF16),
        const(row_compact(), BF16),
    )
    fields, partial = pl.pallas_call(
        send_kernel,
        grid=(3,),
        in_specs=[pl.BlockSpec((1, 2 * UPPER, 8, 2048), lambda g: (g, 0, 0, 0))],
        out_specs=[
            pl.BlockSpec((DOMS, 1, UPPER, 8, LANES), lambda g: (0, g, 0, 0, 0)),
            pl.BlockSpec((1, UPPER, 8, 2048), lambda g: (g, 1, 0, 0)),
        ],
        out_shape=[
            jax.ShapeDtypeStruct((DOMS, 3, UPPER, 8, LANES), BF16),
            jax.ShapeDtypeStruct(prior.shape, BF16),
        ],
        compiler_params=FULL,
        name="send",
    )(prior)
    packed = lax.all_to_all(packed, "member", 0, 0, tiled=True)
    fields = lax.all_to_all(
        fields.reshape(MEMBERS, UPPER, 8, LANES), "member", 0, 0, tiled=True
    )
    sampled = pl.pallas_call(
        sample_kernel,
        in_specs=[VM, VM, VM],
        out_specs=VM,
        out_shape=jax.ShapeDtypeStruct((9, PACK, LANES), F32),
        compiler_params=LIMIT,
        name="sample",
    )(packed, own, const(row_sample(), BF16))
    tiles = lax.axis_size("tile")
    pair = lax.ppermute(sampled, "tile", [(i, i ^ 1) for i in range(tiles)])
    following = lax.ppermute(
        sampled, "tile", [(i, (i + 1 if i % 2 else i - 1) % tiles) for i in range(tiles)]
    )
    table = const(taper_table(), F32)
    partial_gram = pl.pallas_call(
        near_kernel,
        in_specs=[SM, VM, VM, VM],
        out_specs=VM,
        out_shape=jax.ShapeDtypeStruct((BLOCKS_Y * PACK, LANES), F32),
        compiler_params=LIMIT,
        cost_estimate=pl.CostEstimate(flops=10**9, bytes_accessed=3 * 10**6, transcendentals=0),
        name="near_gram",
    )(tile, sampled, pair, table)
    weights = pl.pallas_call(
        solve_kernel,
        in_specs=[SM, VM, VM, VM],
        out_specs=VM,
        out_shape=jax.ShapeDtypeStruct((WEIGHT_ROWS, LANES), F32),
        scratch_shapes=[
            pltpu.VMEM((BLOCKS_Y * PACK + 64, LANES), F32),
            pltpu.VMEM((24, 48, LANES), F32),
            pltpu.VMEM((2, 8, 48, LANES), F32),
            pltpu.VMEM((2, 8, 48, LANES), F32),
        ],
        compiler_params=LIMIT,
        name="solve",
    )(tile, following, partial_gram, table)
    result = pl.pallas_call(
        transform_kernel,
        in_specs=[VM, VM, VM],
        out_specs=VM,
        out_shape=jax.ShapeDtypeStruct((MEMBERS, UPPER, 8, LANES), BF16),
        scratch_shapes=[
            pltpu.VMEM((WEIGHT_ROWS, 512), F32),
            pltpu.VMEM((MEMBERS, UPPER, 8, LANES), F32),
            pltpu.VMEM((16, 8, LANES), F32),
        ],
        compiler_params=LIMIT,
        name="transform",
    )(weights, fields, const(expand_rows(), BF16))
    result = lax.all_to_all(result, "member", 0, 0, tiled=True)
    return pl.pallas_call(
        finish_kernel,
        in_specs=[VM, ANY],
        out_specs=ANY,
        out_shape=jax.ShapeDtypeStruct(prior.shape, BF16),
        scratch_shapes=[
            pltpu.VMEM((3, UPPER, 8, 2048), BF16),
            pltpu.SemaphoreType.DMA((3,)),
        ],
        input_output_aliases={1: 0},
        compiler_params=LIMIT,
        name="finish",
    )(result.reshape(DOMS, 3, UPPER, 8, LANES), partial)


def solution(mesh):
    return jax.shard_map(
        body,
        mesh=mesh,
        in_specs=(
            P("member", None, "tile", None),
            P("tile", "member", None),
            P("tile", "member", None),
            P("tile", "member", None),
            P("tile", "member"),
        ),
        out_specs=P("member", None, "tile", None),
        check_vma=False,
    )
```
